32 devices in a mesh: rep: 2 (over y), gx: 8 (over z, x), gy: 2 (over core).
Axes of the slice: x: 2, y: 2, z: 4, core: 2. Of those that a mesh axis runs over, the one named last changes fastest.
Arguments:
- hidden_in: bfloat16 [2, 32, 16384], P(None, ('rep', 'gy'), 'gx'), parts along dimension 1, may hold values from -180 to 180
- norm_gain: bfloat16 [16384], P('gx'), may hold values from 0.099609375 to 1.8984375
- query_weight: bfloat16 [16384, 8192], P('gx', 'gy'), may hold values from -0.046875 to 0.046875
- key_weight: bfloat16 [16384, 512], P('gx', 'gy'), may hold values from -0.046875 to 0.046875
- value_weight: bfloat16 [16384, 512], P('gx', 'gy'), may hold values from -0.046875 to 0.046875
- out_weight: bfloat16 [8192, 16384], P('gy', 'gx'), may hold values from -0.0625 to 0.0625
- cache_keys: bfloat16 [32, 384, 512], P(('rep', 'gx', 'gy')), parts along dimension 0, may hold values from -400 to 400
- cache_values: bfloat16 [32, 384, 512], P(('rep', 'gx', 'gy')), parts along dimension 0, may hold values from -12 to 12
- lengths: int32 [32], P(('rep', 'gx', 'gy')), parts along dimension 0, may hold values from 48 to 384, as said below
- positions: int32 [32], P(('rep', 'gx', 'gy')), parts along dimension 0, may hold values from 48 to 4479, as said below
Outputs:
- attention_out: bfloat16 [2, 32, 16384], P(None, ('rep', 'gy'), 'gx'), parts along dimension 1
- new_keys: bfloat16 [2, 32, 512], P(None, ('rep', 'gx', 'gy')), parts along dimension 1
- new_values: bfloat16 [2, 32, 512], P(None, ('rep', 'gx', 'gy')), parts along dimension 1
The draws below stay inside these ranges and needn't reach their ends.
There are 2 independent parts, one for each index of `rep`. The reference program is written for one: setup_inputs(seed, part) draws one part's arguments, and reference() takes and returns one part's arrays. A program takes and returns all parts, laid end to end along the dimension named above; an argument that names none is the same for every part. Nothing has to cross between parts.
Inputs may be any that keep to these rules, and one draw needn't show every extreme that they name: Sequence b's cached tokens fill its slots 0 to lengths[b] - 1; in every draw some sequence fills all 384 slots. positions[b] is never below the sequence's cached length; step t's token stands at positions[b] + t.
All inputs are finite; a program needn't handle non-finite values.
Results may differ from the reference program's by a relative error of at most 0.012.
Values may be sent and summed in bfloat16 or wider, within the bound.
No kernel may reach another device: no remote copies, remote signals or barrier semaphores. Data moves between devices by JAX's collectives and lax.ppermute only.
A program may use at most 128 MiB of HBM per device.

```python
import math
import jax
import jax.numpy as jnp
from jax import lax

D = 16384
HQ = 64
KVH = 4
HD = 128
CAP = 384
STEPS = 2
SEQS = 16


def sequence_lengths(key):
    length_key, spot_key = jax.random.split(jax.random.fold_in(key, 5))
    drawn = jax.random.randint(length_key, (SEQS,), CAP // 8, CAP + 1)
    spot = jax.random.randint(spot_key, (), 0, SEQS)
    return jnp.where(jnp.arange(SEQS) == spot, CAP, drawn).astype(jnp.int32)


def draw_lengths(key, part):
    return sequence_lengths(key)


def draw_positions(key, part):
    offset_key = jax.random.fold_in(key, 7)
    offsets = jax.random.randint(offset_key, (SEQS,), 0, 4096)
    return (sequence_lengths(key) + offsets).astype(jnp.int32)


def draw_hidden_in(key, part):
    key = jax.random.fold_in(key, 11)
    base_key, row_key, place_key, size_key, sign_key = jax.random.split(key, 5)
    ramp = jnp.arange(D).astype(jnp.float32) / (D - 1)
    base = jnp.clip(jax.random.normal(base_key, (STEPS, SEQS, D), jnp.float32), -6.0, 6.0)
    column = 0.05 * (1.0 + 2.0 * ramp)
    places = jax.random.randint(place_key, (STEPS, SEQS, 4), 0, D)
    sizes = jax.random.uniform(size_key, (STEPS, SEQS, 4), jnp.float32, 12.0, 17.5)
    signs = (2 * jax.random.randint(sign_key, (STEPS, SEQS, 4), 0, 2) - 1).astype(jnp.float32)
    feature = jnp.arange(D)[None, None, :]
    strong = jnp.zeros((STEPS, SEQS, D), jnp.float32)
    for slot in range(4):
        strong = jnp.where(feature == places[:, :, slot:slot + 1], (signs * sizes)[:, :, slot:slot + 1], strong)
    rows = jnp.exp(math.log(10.0) * jax.random.uniform(row_key, (STEPS, SEQS, 1), jnp.float32))
    return ((base * column + strong) * rows).astype(jnp.bfloat16)


def draw_cache_keys(key, part):
    key = jax.random.fold_in(key, 13)
    base_key = jax.random.fold_in(key, 0)
    base = jnp.clip(jax.random.normal(base_key, (SEQS, CAP, KVH * HD), jnp.float32), -4.0, 4.0)
    return base.astype(jnp.bfloat16)


def block_scale(key, shape, cuts, least, high):
    level, own = 1.0, jax.random.fold_in(key, 6)
    for axis_at, parts in cuts:
        steps = jnp.exp(jax.random.uniform(jax.random.fold_in(own, axis_at), (parts,), jnp.float32, least / len(cuts), high / len(cuts)))
        level = level * jnp.repeat(steps, shape[axis_at] // parts).reshape([-1 if axis == axis_at else 1 for axis in range(len(shape))])
    return level


def scatter_about(rng, extent, scale, bound, pieces=(), held_as=jnp.bfloat16):
    gain = block_scale(rng, extent, pieces, -0.22, 0.18) if pieces else 1.0
    array = jax.random.normal(rng, extent, jnp.float32) * scale * gain
    return jnp.minimum(jnp.maximum(array, -bound), bound).astype(held_as)


def setup_inputs(seed: int = 0, part: int = 0) -> dict:
    key_list = jax.random.split(jax.random.key(seed), 11)
    part_keys = jax.random.split(jax.random.fold_in(key_list[10], part), 11)
    return {
        "hidden_in": draw_hidden_in(jax.random.fold_in(jax.random.fold_in(key_list[10], part), 71), part),
        "norm_gain": jnp.clip(1.0 + 0.18 * jax.random.normal(key_list[1], (D,), jnp.float32), 0.099609375, 1.8984375).astype(jnp.bfloat16),
        "query_weight": scatter_about(key_list[2], (D, HQ * HD), D ** -0.5, 0.046875, ((0, 8), (1, 2))),
        "key_weight": scatter_about(key_list[3], (D, KVH * HD), D ** -0.5, 0.046875, ((0, 8), (1, 2))),
        "value_weight": scatter_about(key_list[4], (D, KVH * HD), D ** -0.5, 0.046875, ((0, 8), (1, 2))),
        "out_weight": scatter_about(key_list[5], (HQ * HD, D), (HQ * HD) ** -0.5, 0.0625, ((0, 2), (1, 8))),
        "cache_keys": draw_cache_keys(jax.random.fold_in(jax.random.fold_in(key_list[10], part), 71), part),
        "cache_values": scatter_about(part_keys[7], (SEQS, CAP, KVH * HD), 3.0, 12.0, ((0, 16),)),
        "lengths": draw_lengths(jax.random.fold_in(jax.random.fold_in(key_list[10], part), 71), part),
        "positions": draw_positions(jax.random.fold_in(jax.random.fold_in(key_list[10], part), 71), part),
    }


epsilon = 1e-05
rope_theta = 500000.0

def rope_frequencies(head_size):
    index = jnp.arange(head_size // 2).astype(jnp.float32)
    frequency = jnp.exp(-math.log(rope_theta) * 2.0 * index / head_size)
    wavelength = 2.0 * math.pi / frequency
    smooth = (8192.0 / wavelength - 1.0) / 3.0
    blended = (1.0 - smooth) * frequency / 8.0 + smooth * frequency
    adjusted = jnp.where(wavelength > 8192.0, frequency / 8.0, blended)
    return jnp.where(wavelength < 2048.0, frequency, adjusted)

def rotate(values, places):
    frequency = rope_frequencies(values.shape[-1])
    angle = places.astype(jnp.float32)[..., None] * frequency
    cosine = jnp.cos(angle)[..., None, :]
    sine = jnp.sin(angle)[..., None, :]
    half = values.shape[-1] // 2
    lower = values[..., :half]
    upper = values[..., half:]
    return jnp.concatenate([lower * cosine - upper * sine, upper * cosine + lower * sine], axis=-1)

def attend_sequence(queries, cached_keys, cached_values, fresh_keys, fresh_values, length, start_step):
    query_count, heads, head_size = queries.shape
    kv_heads = cached_keys.shape[1] // head_size
    group = heads // kv_heads
    grouped = queries.astype(jnp.float32).reshape(query_count, kv_heads, group, head_size)
    stored_keys = cached_keys.astype(jnp.float32).reshape(-1, kv_heads, head_size)
    stored_values = cached_values.astype(jnp.float32).reshape(-1, kv_heads, head_size)
    recent_keys = fresh_keys.astype(jnp.float32).reshape(-1, kv_heads, head_size)
    recent_values = fresh_values.astype(jnp.float32).reshape(-1, kv_heads, head_size)
    factor = 1.0 / math.sqrt(head_size)
    cache_scores = jnp.einsum('skgd,ckd->skgc', grouped, stored_keys) * factor
    live = jnp.arange(stored_keys.shape[0]) < length
    cache_scores = jnp.where(live[None, None, None, :], cache_scores, -jnp.inf)
    fresh_scores = jnp.einsum('skgd,tkd->skgt', grouped, recent_keys) * factor
    seen = jnp.arange(recent_keys.shape[0])[None, :] <= (start_step + jnp.arange(query_count))[:, None]
    fresh_scores = jnp.where(seen[:, None, None, :], fresh_scores, -jnp.inf)
    top = jnp.maximum(lax.optimization_barrier(jnp.max(cache_scores, axis=-1)), lax.optimization_barrier(jnp.max(fresh_scores, axis=-1)))
    cache_exp = jnp.exp(cache_scores - top[..., None])
    fresh_exp = jnp.exp(fresh_scores - top[..., None])
    total = lax.optimization_barrier(jnp.sum(cache_exp, axis=-1)) + lax.optimization_barrier(jnp.sum(fresh_exp, axis=-1))
    cache_weight = (cache_exp / total[..., None]).astype(jnp.bfloat16)
    fresh_weight = (fresh_exp / total[..., None]).astype(jnp.bfloat16)
    mixed = jnp.einsum('skgc,ckd->skgd', cache_weight.astype(jnp.float32), stored_values)
    mixed = mixed + jnp.einsum('skgt,tkd->skgd', fresh_weight.astype(jnp.float32), recent_values)
    return mixed.reshape(query_count, heads * head_size).astype(jnp.bfloat16)

def reference(hidden_in, norm_gain, query_weight, key_weight, value_weight, out_weight, cache_keys, cache_values, lengths, positions):
    step_total, seq_total, width = hidden_in.shape
    activations = hidden_in.astype(jnp.float32)
    inverse_rms = lax.rsqrt(lax.optimization_barrier(jnp.mean(activations * activations, axis=-1)) + epsilon)
    scaled = (activations * norm_gain.astype(jnp.float32)).astype(jnp.bfloat16).reshape(step_total * seq_total, width)
    row_scale = inverse_rms.reshape(step_total * seq_total, 1)
    queries = jnp.dot(scaled, query_weight, preferred_element_type=jnp.float32) * row_scale
    keys_all = jnp.dot(scaled, key_weight, preferred_element_type=jnp.float32) * row_scale
    values_all = jnp.dot(scaled, value_weight, preferred_element_type=jnp.float32) * row_scale
    places = positions[None, :] + jnp.arange(step_total).astype(jnp.int32)[:, None]
    queries = rotate(queries.reshape(step_total, seq_total, HQ, HD), places).astype(jnp.bfloat16)
    new_keys = rotate(keys_all.reshape(step_total, seq_total, KVH, HD), places).astype(jnp.bfloat16).reshape(step_total, seq_total, KVH * HD)
    new_values = values_all.astype(jnp.bfloat16).reshape(step_total, seq_total, KVH * HD)

    def one_sequence(item):
        return attend_sequence(item[0], item[1], item[2], item[3], item[4], item[5], 0)
    context = lax.map(one_sequence, (jnp.transpose(queries, (1, 0, 2, 3)), cache_keys, cache_values, jnp.transpose(new_keys, (1, 0, 2)), jnp.transpose(new_values, (1, 0, 2)), lengths))
    context = jnp.transpose(context, (1, 0, 2)).reshape(step_total * seq_total, HQ * HD)
    attention_out = jnp.dot(context, out_weight, preferred_element_type=jnp.float32).astype(jnp.bfloat16)
    return (attention_out.reshape(step_total, seq_total, width), new_keys, new_values)
```

```python
import functools
import math

import jax
import jax.numpy as jnp
from jax import lax
from jax.experimental import pallas as pl
from jax.experimental.pallas import tpu as pltpu
from jax.sharding import PartitionSpec as P

HD = 128
epsilon = 1e-05
rope_theta = 500000.0
MIB = 1024 * 1024


def rope_frequencies(head_size):
    index = jnp.arange(head_size // 2).astype(jnp.float32)
    frequency = jnp.exp(-math.log(rope_theta) * 2.0 * index / head_size)
    wavelength = 2.0 * math.pi / frequency
    smooth = (8192.0 / wavelength - 1.0) / 3.0
    blended = (1.0 - smooth) * frequency / 8.0 + smooth * frequency
    adjusted = jnp.where(wavelength > 8192.0, frequency / 8.0, blended)
    return jnp.where(wavelength < 2048.0, frequency, adjusted)


def rope_table(position, steps):
    frequency = rope_frequencies(HD)
    places = position + jnp.arange(steps, dtype=jnp.int32)
    angle = places.astype(jnp.float32)[:, None] * frequency
    cosine, sine = jnp.cos(angle), jnp.sin(angle)
    return jnp.concatenate(
        [cosine, cosine, -sine, sine], axis=-1
    ).reshape(2 * steps, HD)


def project_kernel(steps, pitch, chunk, x_ref, gain_ref, wq_ref, wk_ref, wv_ref, out_ref,
                   wq_buf, wk_buf, wv_buf, rows_buf, sems):
    q_cols = wq_ref.shape[1]
    kv_cols = wk_ref.shape[1]
    chunks = q_cols // chunk
    copies = []
    for c in range(chunks):
        copies.append(pltpu.make_async_copy(
            wq_ref.at[:, c * chunk:(c + 1) * chunk], wq_buf.at[c], sems.at[c]))
    copies.append(pltpu.make_async_copy(wk_ref, wk_buf, sems.at[chunks]))
    copies.append(pltpu.make_async_copy(wv_ref, wv_buf, sems.at[chunks + 1]))
    for copy in copies:
        copy.start()

    total_rows = x_ref.shape[0]
    half_seqs = total_rows // (2 * steps)
    stride = steps * pitch

    def spread(head, block):
        for g in range(2):
            for t in range(steps):
                first = (g * steps + t) * half_seqs
                start = (g * half_seqs * steps + t) * pitch + head
                rows_buf[pl.ds(start, half_seqs, stride=stride), :] = block[first:first + half_seqs, :]

    x = x_ref[...].astype(jnp.float32)
    scaled = (x * gain_ref[...].astype(jnp.float32)).astype(jnp.bfloat16)
    squares = jnp.sum(x * x, axis=-1, keepdims=True)
    high = squares.astype(jnp.bfloat16).astype(jnp.float32)
    low = squares - high
    heads = (q_cols + 2 * kv_cols) // HD
    spread(heads, jnp.broadcast_to(high, (total_rows, HD)))
    spread(heads + 1, jnp.broadcast_to(low, (total_rows, HD)))
    for spare in range(heads + 2, pitch):
        spread(spare, jnp.zeros((total_rows, HD), jnp.float32))

    def multiply(weights, first_head):
        product = jnp.dot(scaled, weights, preferred_element_type=jnp.float32)
        for i in range(product.shape[1] // HD):
            spread(first_head + i, product[:, i * HD:(i + 1) * HD])

    for c in range(chunks):
        copies[c].wait()
        multiply(wq_buf[c], c * chunk // HD)
    copies[chunks].wait()
    multiply(wk_buf[...], q_cols // HD)
    copies[chunks + 1].wait()
    multiply(wv_buf[...], (q_cols + kv_cols) // HD)
    out_ref[...] = rows_buf[...].reshape(out_ref.shape).astype(jnp.bfloat16)


def project(x, gain, wq, wk, wv, steps, pitch):
    total_rows, depth = x.shape
    q_cols, kv_cols = wq.shape[1], wk.shape[1]
    seqs = total_rows // steps
    chunk = 512
    vmem = pl.BlockSpec(memory_space=pltpu.VMEM)
    hbm = pl.BlockSpec(memory_space=pl.ANY)
    return pl.pallas_call(
        functools.partial(project_kernel, steps, pitch, chunk),
        out_shape=jax.ShapeDtypeStruct((seqs, steps * pitch, HD), jnp.bfloat16),
        in_specs=[vmem, vmem, hbm, hbm, hbm],
        out_specs=vmem,
        scratch_shapes=[
            pltpu.VMEM((q_cols // chunk, depth, chunk), jnp.bfloat16),
            pltpu.VMEM((depth, kv_cols), jnp.bfloat16),
            pltpu.VMEM((depth, kv_cols), jnp.bfloat16),
            pltpu.VMEM((seqs * steps * pitch, HD), jnp.float32),
            pltpu.SemaphoreType.DMA((q_cols // chunk + 2,)),
        ],
        compiler_params=pltpu.CompilerParams(vmem_limit_bytes=32 * MIB),
        cost_estimate=pl.CostEstimate(
            flops=2 * total_rows * depth * (q_cols + 2 * kv_cols),
            bytes_accessed=2 * depth * (q_cols + 2 * kv_cols), transcendentals=0),
        name="project",
    )(x, gain, wq, wk, wv)


def attend_kernel(steps, pitch, width, length_ref, parts_ref, table_ref, keys_ref, values_ref,
                  context_ref, new_keys_ref, new_values_ref):
    devices = parts_ref.shape[0]
    kv_heads = keys_ref.shape[1] // HD
    half_kv = kv_heads // 2
    half_heads = context_ref.shape[1] // steps
    group = half_heads // half_kv
    slots = keys_ref.shape[0]
    factor = 1.0 / math.sqrt(HD)
    live = lax.broadcasted_iota(jnp.int32, (steps * group, slots), 1) < length_ref[0]
    row_step = lax.broadcasted_iota(jnp.int32, (steps * group, 1), 0) // group
    fresh_keys = [[None] * kv_heads for _ in range(steps)]
    fresh_values = [[None] * kv_heads for _ in range(steps)]
    queries = [[None] * kv_heads for _ in range(steps)]
    for g in range(2):
        total = parts_ref[g].astype(jnp.float32)
        for i in range(1, devices // 2):
            total = total + parts_ref[2 * i + g].astype(jnp.float32)
        for t in range(steps):
            rows = total[t * pitch:(t + 1) * pitch]
            first_k = half_heads
            first_v = first_k + half_kv
            first_s = first_v + half_kv
            squares = rows[first_s:first_s + 1] + rows[first_s + 1:first_s + 2]
            rows = rows * lax.rsqrt(squares / width + epsilon)
            cosine = table_ref[2 * t:2 * t + 1, :]
            sine = table_ref[2 * t + 1:2 * t + 2, :]
            turned = rows * cosine + pltpu.roll(rows, HD // 2, 1) * sine
            turned = turned.astype(jnp.bfloat16)
            plain = rows.astype(jnp.bfloat16)
            for k in range(half_kv):
                head = g * half_kv + k
                queries[t][head] = turned[k * group:(k + 1) * group]
                fresh_keys[t][head] = turned[first_k + k:first_k + k + 1].astype(jnp.float32)
                fresh_values[t][head] = plain[first_v + k:first_v + k + 1].astype(jnp.float32)
    new_keys_ref[...] = jnp.concatenate(
        [jnp.concatenate(row, axis=1) for row in fresh_keys], axis=0).astype(jnp.bfloat16)
    new_values_ref[...] = jnp.concatenate(
        [jnp.concatenate(row, axis=1) for row in fresh_values], axis=0).astype(jnp.bfloat16)
    for head in range(kv_heads):
        columns = slice(head * HD, (head + 1) * HD)
        query = jnp.concatenate([queries[t][head] for t in range(steps)], axis=0)
        scores = lax.dot_general(
            query, keys_ref[:, columns], (((1,), (1,)), ((), ())),
            preferred_element_type=jnp.float32) * factor
        scores = jnp.where(live, scores, -jnp.inf)
        top = jnp.max(scores, axis=-1, keepdims=True)
        wide = query.astype(jnp.float32)
        fresh = []
        for s in range(steps):
            score = jnp.sum(wide * fresh_keys[s][head], axis=-1, keepdims=True) * factor
            score = jnp.where(row_step >= s, score, -jnp.inf)
            fresh.append(score)
            top = jnp.maximum(top, score)
        scores = jnp.exp(scores - top)
        total = jnp.sum(scores, axis=-1, keepdims=True)
        fresh = [jnp.exp(score - top) for score in fresh]
        for score in fresh:
            total = total + score
        weight = (scores / total).astype(jnp.bfloat16)
        mixed = jnp.dot(weight, values_ref[:, columns], preferred_element_type=jnp.float32)
        for s in range(steps):
            weight = (fresh[s] / total).astype(jnp.bfloat16).astype(jnp.float32)
            mixed = mixed + weight * fresh_values[s][head]
        mixed = mixed.astype(jnp.bfloat16)
        g, k = head // half_kv, head % half_kv
        for t in range(steps):
            piece = mixed[t * group:(t + 1) * group]
            first = t * half_heads + k * group
            for i in range(devices // 2):
                context_ref[2 * i + g, first:first + group, :] = piece


def attend(length, parts, table, keys, values, steps, pitch, width, half_heads):
    devices = parts.shape[0]
    vmem = pl.BlockSpec(memory_space=pltpu.VMEM)
    smem = pl.BlockSpec(memory_space=pltpu.SMEM)
    kv_cols = keys.shape[1]
    return pl.pallas_call(
        functools.partial(attend_kernel, steps, pitch, width),
        out_shape=(
            jax.ShapeDtypeStruct((devices, steps * half_heads, HD), jnp.bfloat16),
            jax.ShapeDtypeStruct((steps, kv_cols), jnp.bfloat16),
            jax.ShapeDtypeStruct((steps, kv_cols), jnp.bfloat16),
        ),
        in_specs=[smem, vmem, vmem, vmem, vmem],
        out_specs=(vmem, vmem, vmem),
        compiler_params=pltpu.CompilerParams(vmem_limit_bytes=16 * MIB),
        name="attend",
    )(length, parts, table, keys, values)


def output_kernel(steps, chunk, side_ref, context_ref, weight_ref, mine_ref, other_ref,
                  weight_buf, wide_buf, rows_buf, sems):
    devices, per_device, _ = context_ref.shape
    heads = per_device // steps
    half_seqs = devices // 2
    columns = weight_ref.shape[1]
    chunks = columns // chunk
    copies = [pltpu.make_async_copy(
        weight_ref.at[:, c * chunk:(c + 1) * chunk], weight_buf.at[c], sems.at[c])
        for c in range(chunks)]
    for copy in copies:
        copy.start()
    wide_buf[...] = context_ref[...].astype(jnp.float32).reshape(wide_buf.shape)
    for h in range(heads):
        pieces = []
        for g in range(2):
            for t in range(steps):
                start = (g * half_seqs * steps + t) * heads + h
                pieces.append(wide_buf[pl.ds(start, half_seqs, stride=per_device), :])
        rows_buf[:, h * HD:(h + 1) * HD] = jnp.concatenate(pieces, axis=0).astype(jnp.bfloat16)
    rows = rows_buf[...]
    side = side_ref[0]
    half = rows.shape[0] // 2
    for c in range(chunks):
        copies[c].wait()
        product = jnp.dot(rows, weight_buf[c], preferred_element_type=jnp.float32)
        lower, upper = product[:half], product[half:]
        span = slice(c * chunk, (c + 1) * chunk)
        mine_ref[:, span] = jnp.where(side == 0, lower, upper)
        other_ref[:, span] = jnp.where(side == 0, upper, lower).astype(jnp.bfloat16)


def output(side, context, weight, steps):
    devices, per_device, _ = context.shape
    depth, columns = weight.shape
    chunk = min(columns, 256)
    half = devices * steps // 2
    vmem = pl.BlockSpec(memory_space=pltpu.VMEM)
    smem = pl.BlockSpec(memory_space=pltpu.SMEM)
    hbm = pl.BlockSpec(memory_space=pl.ANY)
    return pl.pallas_call(
        functools.partial(output_kernel, steps, chunk),
        out_shape=(
            jax.ShapeDtypeStruct((half, columns), jnp.float32),
            jax.ShapeDtypeStruct((half, columns), jnp.bfloat16),
        ),
        in_specs=[smem, vmem, hbm],
        out_specs=(vmem, vmem),
        scratch_shapes=[
            pltpu.VMEM((columns // chunk, depth, chunk), jnp.bfloat16),
            pltpu.VMEM((devices * per_device, HD), jnp.float32),
            pltpu.VMEM((devices * steps, depth), jnp.bfloat16),
            pltpu.SemaphoreType.DMA((columns // chunk,)),
        ],
        compiler_params=pltpu.CompilerParams(vmem_limit_bytes=32 * MIB),
        cost_estimate=pl.CostEstimate(
            flops=2 * devices * steps * depth * columns,
            bytes_accessed=2 * depth * columns, transcendentals=0),
        name="output",
    )(side, context, weight)


def body(hidden_in, norm_gain, query_weight, key_weight, value_weight, out_weight,
         cache_keys, cache_values, lengths, positions):
    steps, half_seqs, depth = hidden_in.shape
    gx_count = lax.axis_size("gx")
    half_heads = query_weight.shape[1] // HD
    heads_here = half_heads + 2 * key_weight.shape[1] // HD
    pitch = -(-(heads_here + 2) // 8) * 8
    x = lax.all_gather(hidden_in.reshape(steps * half_seqs, depth), "gy", axis=0, tiled=True)
    parts = project(x, norm_gain[None, :], query_weight, key_weight, value_weight, steps, pitch)
    parts = lax.all_to_all(parts, ("gx", "gy"), split_axis=0, concat_axis=0, tiled=True)
    table = rope_table(positions[0], steps)
    context, new_keys, new_values = attend(
        lengths, parts, table, cache_keys[0], cache_values[0],
        steps, pitch, depth * gx_count, half_heads)
    context = lax.all_to_all(context, ("gx", "gy"), split_axis=0, concat_axis=0, tiled=True)
    side = lax.axis_index("gy").astype(jnp.int32).reshape(1)
    mine, other = output(side, context, out_weight, steps)
    other = lax.ppermute(other, "gy", [(0, 1), (1, 0)])
    result = (mine + other.astype(jnp.float32)).astype(jnp.bfloat16)
    return (
        result.reshape(steps, half_seqs, -1),
        new_keys[:, None, :],
        new_values[:, None, :],
    )


def solution(mesh):
    in_specs = (
        P(None, ("rep", "gy"), "gx"),
        P("gx"),
        P("gx", "gy"),
        P("gx", "gy"),
        P("gx", "gy"),
        P("gy", "gx"),
        P(("rep", "gx", "gy"), None, None),
        P(("rep", "gx", "gy"), None, None),
        P(("rep", "gx", "gy")),
        P(("rep", "gx", "gy")),
    )
    out_specs = (
        P(None, ("rep", "gy"), "gx"),
        P(None, ("rep", "gx", "gy"), None),
        P(None, ("rep", "gx", "gy"), None),
    )
    return jax.shard_map(body, mesh=mesh, in_specs=in_specs, out_specs=out_specs, check_vma=False)
```

```python
import functools
import math

import jax
import jax.numpy as jnp
from jax import lax
from jax.experimental import pallas as pl
from jax.experimental.pallas import tpu as pltpu
from jax.sharding import PartitionSpec as P

HD = 128
epsilon = 1e-05
rope_theta = 500000.0
MIB = 1024 * 1024


def rope_frequencies(head_size):
    index = jnp.arange(head_size // 2).astype(jnp.float32)
    frequency = jnp.exp(-math.log(rope_theta) * 2.0 * index / head_size)
    wavelength = 2.0 * math.pi / frequency
    smooth = (8192.0 / wavelength - 1.0) / 3.0
    blended = (1.0 - smooth) * frequency / 8.0 + smooth * frequency
    adjusted = jnp.where(wavelength > 8192.0, frequency / 8.0, blended)
    return jnp.where(wavelength < 2048.0, frequency, adjusted)


def rope_table(position, steps):
    frequency = rope_frequencies(HD)
    places = position + jnp.arange(steps, dtype=jnp.int32)
    angle = places.astype(jnp.float32)[:, None] * frequency
    cosine, sine = jnp.cos(angle), jnp.sin(angle)
    return jnp.concatenate(
        [cosine, cosine, -sine, sine], axis=-1
    ).reshape(2 * steps, HD)


def project_kernel(steps, pitch, chunk, place_ref, mine_ref, other_ref, gain_ref, wq_ref, wk_ref, wv_ref,
                   *rest):
    out_refs, (wq_buf, wk_buf, wv_buf, rows_buf, sems) = rest[:-5], rest[-5:]
    q_cols = wq_ref.shape[1]
    kv_cols = wk_ref.shape[1]
    chunks = q_cols // chunk
    copies = [pltpu.make_async_copy(wk_ref, wk_buf, sems.at[chunks]),
              pltpu.make_async_copy(wv_ref, wv_buf, sems.at[chunks + 1])]
    for c in range(chunks):
        copies.append(pltpu.make_async_copy(
            wq_ref.at[:, c * chunk:(c + 1) * chunk], wq_buf.at[c], sems.at[c]))
    for copy in copies:
        copy.start()

    device = place_ref[0]
    half_rows = mine_ref.shape[0]
    total_rows = 2 * half_rows
    half_seqs = half_rows // steps
    stride = steps * pitch

    def spread(head, block):
        for g in range(2):
            for t in range(steps):
                first = (g * steps + t) * half_seqs
                start = (g * half_seqs * steps + t) * pitch + head
                rows_buf[pl.ds(start, half_seqs, stride=stride), :] = block[first:first + half_seqs, :]

    low_side = device % 2 == 0
    mine = mine_ref[...].astype(jnp.float32)
    other = other_ref[...].astype(jnp.float32)
    x = jnp.concatenate(
        [jnp.where(low_side, mine, other), jnp.where(low_side, other, mine)], axis=0)
    gain = gain_ref[...].astype(jnp.float32)
    gain = jnp.concatenate([gain[i:i + 1] for i in range(gain.shape[0])], axis=1)
    scaled = (x * gain).astype(jnp.bfloat16)
    squares = jnp.sum(x * x, axis=-1, keepdims=True)
    high = squares.astype(jnp.bfloat16).astype(jnp.float32)
    low = squares - high
    heads = (q_cols + 2 * kv_cols) // HD
    spread(heads, jnp.broadcast_to(high, (total_rows, HD)))
    spread(heads + 1, jnp.broadcast_to(low, (total_rows, HD)))
    for spare in range(heads + 2, pitch):
        spread(spare, jnp.zeros((total_rows, HD), jnp.float32))

    def multiply(weights, first_head):
        product = jnp.dot(scaled, weights, preferred_element_type=jnp.float32)
        for i in range(product.shape[1] // HD):
            spread(first_head + i, product[:, i * HD:(i + 1) * HD])

    copies[0].wait()
    multiply(wk_buf[...], q_cols // HD)
    copies[1].wait()
    multiply(wv_buf[...], (q_cols + kv_cols) // HD)
    for c in range(chunks):
        copies[2 + c].wait()
        multiply(wq_buf[c], c * chunk // HD)
    if len(out_refs) == 1:
        out_refs[0][...] = rows_buf[...].reshape(out_refs[0].shape).astype(jnp.bfloat16)
    else:
        for k, out_ref in enumerate(out_refs):
            start = pl.multiple_of((device ^ k) * stride, 8)
            out_ref[...] = rows_buf[pl.ds(start, stride), :].astype(jnp.bfloat16)


def project(place, mine, other, gain, wq, wk, wv, steps, pitch, direct):
    half_rows, depth = mine.shape
    q_cols, kv_cols = wq.shape[1], wk.shape[1]
    seqs = 2 * half_rows // steps
    chunk = 512
    vmem = pl.BlockSpec(memory_space=pltpu.VMEM)
    smem = pl.BlockSpec(memory_space=pltpu.SMEM)
    hbm = pl.BlockSpec(memory_space=pltpu.HBM)
    if direct:
        out_shape = (jax.ShapeDtypeStruct((steps * pitch, HD), jnp.bfloat16),) * seqs
    else:
        out_shape = (jax.ShapeDtypeStruct((seqs, steps * pitch, HD), jnp.bfloat16),)
    return pl.pallas_call(
        functools.partial(project_kernel, steps, pitch, chunk),
        out_shape=out_shape,
        in_specs=[smem, vmem, vmem, vmem, hbm, hbm, hbm],
        out_specs=(vmem,) * len(out_shape),
        scratch_shapes=[
            pltpu.VMEM((q_cols // chunk, depth, chunk), jnp.bfloat16),
            pltpu.VMEM((depth, kv_cols), jnp.bfloat16),
            pltpu.VMEM((depth, kv_cols), jnp.bfloat16),
            pltpu.VMEM((seqs * steps * pitch, HD), jnp.float32),
            pltpu.SemaphoreType.DMA((q_cols // chunk + 2,)),
        ],
        compiler_params=pltpu.CompilerParams(vmem_limit_bytes=44 * MIB),
        cost_estimate=pl.CostEstimate(
            flops=4 * half_rows * depth * (q_cols + 2 * kv_cols),
            bytes_accessed=2 * depth * (q_cols + 2 * kv_cols), transcendentals=0),
        name="project",
    )(place, mine, other, gain, wq, wk, wv)


def attend_kernel(steps, pitch, width, direct, place_ref, length_ref, table_ref, keys_ref, values_ref, *rest):
    part_refs, (same_ref, cross_ref, new_keys_ref, new_values_ref) = rest[:-4], rest[-4:]
    kv_heads = keys_ref.shape[1] // HD
    half_kv = kv_heads // 2
    half_heads = same_ref.shape[0] // steps
    low_side = place_ref[0] % 2 == 0
    if direct:
        same, cross = [
            functools.reduce(jnp.add, [ref[...].astype(jnp.float32) for ref in part_refs[i::2]])
            for i in range(2)]
    else:
        parts_ref = part_refs[0]
        even, odd = [
            functools.reduce(jnp.add, [
                parts_ref[i].astype(jnp.float32) for i in range(g, parts_ref.shape[0], 2)])
            for g in range(2)]
        same, cross = jnp.where(low_side, even, odd), jnp.where(low_side, odd, even)
    halves = [jnp.where(low_side, same, cross), jnp.where(low_side, cross, same)]
    group = half_heads // half_kv
    slots = keys_ref.shape[0]
    factor = 1.0 / math.sqrt(HD)
    live = lax.broadcasted_iota(jnp.int32, (steps * group, slots), 1) < length_ref[0]
    row_step = lax.broadcasted_iota(jnp.int32, (steps * group, 1), 0) // group
    fresh_keys = [[None] * kv_heads for _ in range(steps)]
    fresh_values = [[None] * kv_heads for _ in range(steps)]
    queries = [[None] * kv_heads for _ in range(steps)]
    for g in range(2):
        for t in range(steps):
            rows = halves[g][t * pitch:(t + 1) * pitch]
            first_k = half_heads
            first_v = first_k + half_kv
            first_s = first_v + half_kv
            squares = rows[first_s:first_s + 1] + rows[first_s + 1:first_s + 2]
            rows = rows * lax.rsqrt(squares / width + epsilon)
            cosine = table_ref[2 * t:2 * t + 1, :]
            sine = table_ref[2 * t + 1:2 * t + 2, :]
            turned = rows * cosine + pltpu.roll(rows, HD // 2, 1) * sine
            turned = turned.astype(jnp.bfloat16)
            plain = rows.astype(jnp.bfloat16)
            for k in range(half_kv):
                head = g * half_kv + k
                queries[t][head] = turned[k * group:(k + 1) * group]
                fresh_keys[t][head] = turned[first_k + k:first_k + k + 1].astype(jnp.float32)
                fresh_values[t][head] = plain[first_v + k:first_v + k + 1].astype(jnp.float32)
    new_keys_ref[...] = jnp.concatenate(
        [jnp.concatenate(row, axis=1) for row in fresh_keys], axis=0).astype(jnp.bfloat16)
    new_values_ref[...] = jnp.concatenate(
        [jnp.concatenate(row, axis=1) for row in fresh_values], axis=0).astype(jnp.bfloat16)
    contexts = [[], []]
    for head in range(kv_heads):
        columns = slice(head * HD, (head + 1) * HD)
        query = jnp.concatenate([queries[t][head] for t in range(steps)], axis=0)
        scores = lax.dot_general(
            query, keys_ref[:, columns], (((1,), (1,)), ((), ())),
            preferred_element_type=jnp.float32) * factor
        scores = jnp.where(live, scores, -jnp.inf)
        top = jnp.max(scores, axis=-1, keepdims=True)
        wide = query.astype(jnp.float32)
        fresh = []
        for s in range(steps):
            score = jnp.sum(wide * fresh_keys[s][head], axis=-1, keepdims=True) * factor
            score = jnp.where(row_step >= s, score, -jnp.inf)
            fresh.append(score)
            top = jnp.maximum(top, score)
        scores = jnp.exp(scores - top)
        total = jnp.sum(scores, axis=-1, keepdims=True)
        fresh = [jnp.exp(score - top) for score in fresh]
        for score in fresh:
            total = total + score
        weight = (scores / total).astype(jnp.bfloat16)
        mixed = jnp.dot(weight, values_ref[:, columns], preferred_element_type=jnp.float32)
        for s in range(steps):
            weight = (fresh[s] / total).astype(jnp.bfloat16).astype(jnp.float32)
            mixed = mixed + weight * fresh_values[s][head]
        contexts[head // half_kv].append(mixed)
    rows = [
        jnp.concatenate([half[k][t * group:(t + 1) * group] for t in range(steps) for k in range(half_kv)], axis=0)
        for half in contexts]
    same_ref[...] = jnp.where(low_side, rows[0], rows[1]).astype(jnp.bfloat16)
    cross_ref[...] = jnp.where(low_side, rows[1], rows[0]).astype(jnp.bfloat16)


def attend(place, length, parts, table, keys, values, steps, pitch, width, half_heads, direct):
    vmem = pl.BlockSpec(memory_space=pltpu.VMEM)
    smem = pl.BlockSpec(memory_space=pltpu.SMEM)
    kv_cols = keys.shape[1]
    half = jax.ShapeDtypeStruct((steps * half_heads, HD), jnp.bfloat16)
    fresh = jax.ShapeDtypeStruct((steps, kv_cols), jnp.bfloat16)
    return pl.pallas_call(
        functools.partial(attend_kernel, steps, pitch, width, direct),
        out_shape=(half, half, fresh, fresh),
        in_specs=[smem, smem, vmem, vmem, vmem] + [vmem] * len(parts),
        out_specs=(vmem,) * 4,
        compiler_params=pltpu.CompilerParams(vmem_limit_bytes=16 * MIB),
        name="attend",
    )(place, length, table, keys, values, *parts)


def output_kernel(steps, chunk, place_ref, weight_ref, *rest):
    context_refs, (mine_ref, other_ref, wide_buf, rows_buf) = rest[:-4], rest[-4:]
    device = place_ref[0]
    heads = weight_ref.shape[0] // HD
    per_device = steps * heads
    devices = wide_buf.shape[0] // per_device
    half_seqs = devices // 2
    columns = weight_ref.shape[1]
    if len(context_refs) == 1:
        wide_buf[...] = context_refs[0][...].astype(jnp.float32).reshape(wide_buf.shape)
    else:
        for k, ref in enumerate(context_refs):
            start = pl.multiple_of((device ^ k) * per_device, 8)
            wide_buf[pl.ds(start, per_device), :] = ref[...].astype(jnp.float32)
    for h in range(heads):
        pieces = []
        for g in range(2):
            for t in range(steps):
                start = (g * half_seqs * steps + t) * heads + h
                pieces.append(wide_buf[pl.ds(start, half_seqs, stride=per_device), :])
        rows_buf[:, h * HD:(h + 1) * HD] = jnp.concatenate(pieces, axis=0).astype(jnp.bfloat16)
    rows = rows_buf[...]
    low_side = device % 2 == 0
    half = rows.shape[0] // 2
    for c in range(columns // chunk):
        span = slice(c * chunk, (c + 1) * chunk)
        product = jnp.dot(rows, weight_ref[:, span], preferred_element_type=jnp.float32)
        lower, upper = product[:half], product[half:]
        mine_ref[:, span] = jnp.where(low_side, lower, upper)
        other_ref[:, span] = jnp.where(low_side, upper, lower).astype(jnp.bfloat16)


def output(place, contexts, weight, devices, steps):
    depth, columns = weight.shape
    chunk = min(columns, 512)
    half = devices * steps // 2
    vmem = pl.BlockSpec(memory_space=pltpu.VMEM)
    smem = pl.BlockSpec(memory_space=pltpu.SMEM)
    return pl.pallas_call(
        functools.partial(output_kernel, steps, chunk),
        out_shape=(
            jax.ShapeDtypeStruct((half, columns), jnp.float32),
            jax.ShapeDtypeStruct((half, columns), jnp.bfloat16),
        ),
        in_specs=[smem, vmem] + [vmem] * len(contexts),
        out_specs=(vmem, vmem),
        scratch_shapes=[
            pltpu.VMEM((devices * steps * depth // HD, HD), jnp.float32),
            pltpu.VMEM((devices * steps, depth), jnp.bfloat16),
        ],
        compiler_params=pltpu.CompilerParams(vmem_limit_bytes=24 * MIB),
        cost_estimate=pl.CostEstimate(
            flops=2 * devices * steps * depth * columns,
            bytes_accessed=2 * depth * columns, transcendentals=0),
        name="output",
    )(place, weight, *contexts)


def body(hidden_in, norm_gain, query_weight, key_weight, value_weight, out_weight,
         cache_keys, cache_values, lengths, positions):
    steps, half_seqs, depth = hidden_in.shape
    both = ("gx", "gy")
    devices = lax.axis_size(both)
    direct = devices <= 16 and devices & (devices - 1) == 0
    half_heads = query_weight.shape[1] // HD
    heads_here = half_heads + 2 * key_weight.shape[1] // HD
    pitch = -(-(heads_here + 2) // 8) * 8
    place = lax.axis_index(both).astype(jnp.int32).reshape(1)
    swap = [(0, 1), (1, 0)]

    def partner(array, k):
        if k == 0:
            return array
        return lax.ppermute(array, both, [(i, i ^ k) for i in range(devices)])

    def to_all(array):
        return lax.all_to_all(array, both, split_axis=0, concat_axis=0, tiled=True)

    mine = hidden_in.reshape(steps * half_seqs, depth)
    other = lax.ppermute(mine, "gy", swap)
    parts = project(place, mine, other, norm_gain.reshape(-1, HD), query_weight, key_weight,
                    value_weight, steps, pitch, direct)

    if direct:
        parts = [partner(part, k) for k, part in enumerate(parts)]
    else:
        parts = [to_all(parts[0])]
    table = rope_table(positions[0], steps)
    same, cross, new_keys, new_values = attend(
        place, lengths, parts, table, cache_keys[0], cache_values[0],
        steps, pitch, depth * lax.axis_size("gx"), half_heads, direct)
    if direct:
        contexts = [partner(cross if k % 2 else same, k) for k in range(devices)]
    else:
        pair = jnp.where(place[0] % 2 == 0, jnp.stack([same, cross]), jnp.stack([cross, same]))
        contexts = [to_all(jnp.tile(pair, (devices // 2, 1, 1)))]
    mine, other = output(place, contexts, out_weight, devices, steps)
    other = lax.ppermute(other, "gy", swap)
    result = (mine + other.astype(jnp.float32)).astype(jnp.bfloat16)
    return (
        result.reshape(steps, half_seqs, -1),
        new_keys[:, None, :],
        new_values[:, None, :],
    )


def solution(mesh):
    in_specs = (
        P(None, ("rep", "gy"), "gx"),
        P("gx"),
        P("gx", "gy"),
        P("gx", "gy"),
        P("gx", "gy"),
        P("gy", "gx"),
        P(("rep", "gx", "gy"), None, None),
        P(("rep", "gx", "gy"), None, None),
        P(("rep", "gx", "gy")),
        P(("rep", "gx", "gy")),
    )
    out_specs = (
        P(None, ("rep", "gy"), "gx"),
        P(None, ("rep", "gx", "gy"), None),
        P(None, ("rep", "gx", "gy"), None),
    )
    return jax.shard_map(body, mesh=mesh, in_specs=in_specs, out_specs=out_specs, check_vma=False)
```

```python
import functools
import math

import jax
import jax.numpy as jnp
from jax import lax
from jax.experimental import pallas as pl
from jax.experimental.pallas import tpu as pltpu
from jax.sharding import PartitionSpec as P

HD = 128
epsilon = 1e-05
rope_theta = 500000.0
MIB = 1024 * 1024


def rope_frequencies(head_size):
    index = jnp.arange(head_size // 2).astype(jnp.float32)
    frequency = jnp.exp(-math.log(rope_theta) * 2.0 * index / head_size)
    wavelength = 2.0 * math.pi / frequency
    smooth = (8192.0 / wavelength - 1.0) / 3.0
    blended = (1.0 - smooth) * frequency / 8.0 + smooth * frequency
    adjusted = jnp.where(wavelength > 8192.0, frequency / 8.0, blended)
    return jnp.where(wavelength < 2048.0, frequency, adjusted)


def rope_table(position, steps):
    frequency = rope_frequencies(HD)
    places = position + jnp.arange(steps, dtype=jnp.int32)
    angle = places.astype(jnp.float32)[:, None] * frequency
    cosine, sine = jnp.cos(angle), jnp.sin(angle)
    return jnp.concatenate(
        [cosine, cosine, -sine, sine], axis=-1
    ).reshape(2 * steps, HD)


def in_hbm(array):
    return pltpu.with_memory_space_constraint(array, pltpu.HBM)


def project_kernel(steps, pitch, chunk, place_ref, mine_ref, other_ref, gain_ref, wq_ref, wk_ref, wv_ref,
                   *rest):
    out_refs, (mine_buf, gain_buf, wq_buf, wk_buf, wv_buf, rows_buf, sems) = rest[:-7], rest[-7:]
    q_cols = wq_ref.shape[1]
    kv_cols = wk_ref.shape[1]
    chunks = q_cols // chunk
    copies = [pltpu.make_async_copy(mine_ref, mine_buf, sems.at[chunks]),
              pltpu.make_async_copy(gain_ref, gain_buf, sems.at[chunks + 1]),
              pltpu.make_async_copy(wk_ref, wk_buf, sems.at[chunks + 2]),
              pltpu.make_async_copy(wv_ref, wv_buf, sems.at[chunks + 3])]
    for c in range(chunks):
        copies.append(pltpu.make_async_copy(
            wq_ref.at[:, c * chunk:(c + 1) * chunk], wq_buf.at[c], sems.at[c]))
    for copy in copies:
        copy.start()

    device = place_ref[0]
    half_rows = mine_ref.shape[0]
    total_rows = 2 * half_rows
    half_seqs = half_rows // steps
    stride = steps * pitch

    def spread(head, block):
        for g in range(2):
            for t in range(steps):
                first = (g * steps + t) * half_seqs
                start = (g * half_seqs * steps + t) * pitch + head
                rows_buf[pl.ds(start, half_seqs, stride=stride), :] = block[first:first + half_seqs, :]

    low_side = device % 2 == 0
    copies[0].wait()
    copies[1].wait()
    mine = mine_buf[...].astype(jnp.float32)
    other = other_ref[...].astype(jnp.float32)
    x = jnp.concatenate(
        [jnp.where(low_side, mine, other), jnp.where(low_side, other, mine)], axis=0)
    gain = gain_buf[...].astype(jnp.float32)
    gain = jnp.concatenate([gain[i:i + 1] for i in range(gain.shape[0])], axis=1)
    scaled = (x * gain).astype(jnp.bfloat16)
    squares = jnp.sum(x * x, axis=-1, keepdims=True)
    high = squares.astype(jnp.bfloat16).astype(jnp.float32)
    low = squares - high
    heads = (q_cols + 2 * kv_cols) // HD
    spread(heads, jnp.broadcast_to(high, (total_rows, HD)))
    spread(heads + 1, jnp.broadcast_to(low, (total_rows, HD)))
    for spare in range(heads + 2, pitch):
        spread(spare, jnp.zeros((total_rows, HD), jnp.float32))

    def multiply(weights, first_head):
        product = jnp.dot(scaled, weights, preferred_element_type=jnp.float32)
        for i in range(product.shape[1] // HD):
            spread(first_head + i, product[:, i * HD:(i + 1) * HD])

    copies[2].wait()
    multiply(wk_buf[...], q_cols // HD)
    copies[3].wait()
    multiply(wv_buf[...], (q_cols + kv_cols) // HD)
    for c in range(chunks):
        copies[4 + c].wait()
        multiply(wq_buf[c], c * chunk // HD)
    if len(out_refs) == 1:
        out_refs[0][...] = rows_buf[...].reshape(out_refs[0].shape).astype(jnp.bfloat16)
    else:
        for k, out_ref in enumerate(out_refs):
            start = pl.multiple_of((device ^ k) * stride, 8)
            out_ref[...] = rows_buf[pl.ds(start, stride), :].astype(jnp.bfloat16)


def project(place, mine, other, gain, wq, wk, wv, steps, pitch, direct):
    half_rows, depth = mine.shape
    q_cols, kv_cols = wq.shape[1], wk.shape[1]
    seqs = 2 * half_rows // steps
    chunk = 512
    vmem = pl.BlockSpec(memory_space=pltpu.VMEM)
    smem = pl.BlockSpec(memory_space=pltpu.SMEM)
    hbm = pl.BlockSpec(memory_space=pltpu.HBM)
    if direct:
        out_shape = (jax.ShapeDtypeStruct((steps * pitch, HD), jnp.bfloat16),) * seqs
    else:
        out_shape = (jax.ShapeDtypeStruct((seqs, steps * pitch, HD), jnp.bfloat16),)
    return pl.pallas_call(
        functools.partial(project_kernel, steps, pitch, chunk),
        out_shape=out_shape,
        in_specs=[smem, hbm, vmem, hbm, hbm, hbm, hbm],
        out_specs=(vmem,) * len(out_shape),
        scratch_shapes=[
            pltpu.VMEM(mine.shape, jnp.bfloat16),
            pltpu.VMEM(gain.shape, jnp.bfloat16),
            pltpu.VMEM((q_cols // chunk, depth, chunk), jnp.bfloat16),
            pltpu.VMEM((depth, kv_cols), jnp.bfloat16),
            pltpu.VMEM((depth, kv_cols), jnp.bfloat16),
            pltpu.VMEM((seqs * steps * pitch, HD), jnp.float32),
            pltpu.SemaphoreType.DMA((q_cols // chunk + 4,)),
        ],
        compiler_params=pltpu.CompilerParams(vmem_limit_bytes=26 * MIB),
        cost_estimate=pl.CostEstimate(
            flops=4 * half_rows * depth * (q_cols + 2 * kv_cols),
            bytes_accessed=2 * depth * (q_cols + 2 * kv_cols), transcendentals=0),
        name="project",
    )(place, in_hbm(mine), other, in_hbm(gain), in_hbm(wq), in_hbm(wk), in_hbm(wv))


def fetch_kernel(chunks, weight_ref, after_ref, held_ref, sems):
    rows = weight_ref.shape[0] // chunks
    copies = [pltpu.make_async_copy(
        weight_ref.at[c * rows:(c + 1) * rows], held_ref.at[c * rows:(c + 1) * rows], sems.at[c])
        for c in range(chunks)]
    for copy in copies:
        copy.start()
    for copy in copies:
        copy.wait()


def fetch(weight, after):
    chunks = 8
    return pl.pallas_call(
        functools.partial(fetch_kernel, chunks),
        out_shape=pltpu.VMEM(weight.shape, weight.dtype),
        in_specs=[pl.BlockSpec(memory_space=pltpu.HBM), pl.BlockSpec(memory_space=pl.ANY)],
        out_specs=pl.BlockSpec(memory_space=pltpu.VMEM),
        scratch_shapes=[pltpu.SemaphoreType.DMA((chunks,))],
        compiler_params=pltpu.CompilerParams(vmem_limit_bytes=8 * MIB),
        cost_estimate=pl.CostEstimate(
            flops=0, bytes_accessed=2 * weight.size, transcendentals=0),
        name="fetch",
    )(in_hbm(weight), after)


def attend_kernel(steps, pitch, width, direct, place_ref, length_ref, table_ref, keys_ref, values_ref, held_ref,
                  *rest):
    part_refs, (same_ref, cross_ref, new_keys_ref, new_values_ref) = rest[:-4], rest[-4:]
    kv_heads = keys_ref.shape[1] // HD
    half_kv = kv_heads // 2
    half_heads = same_ref.shape[0] // steps
    low_side = place_ref[0] % 2 == 0
    if direct:
        same, cross = [
            functools.reduce(jnp.add, [ref[...].astype(jnp.float32) for ref in part_refs[i::2]])
            for i in range(2)]
    else:
        parts_ref = part_refs[0]
        even, odd = [
            functools.reduce(jnp.add, [
                parts_ref[i].astype(jnp.float32) for i in range(g, parts_ref.shape[0], 2)])
            for g in range(2)]
        same, cross = jnp.where(low_side, even, odd), jnp.where(low_side, odd, even)
    halves = [jnp.where(low_side, same, cross), jnp.where(low_side, cross, same)]
    group = half_heads // half_kv
    slots = keys_ref.shape[0]
    factor = 1.0 / math.sqrt(HD)
    live = lax.broadcasted_iota(jnp.int32, (steps * group, slots), 1) < length_ref[0]
    row_step = lax.broadcasted_iota(jnp.int32, (steps * group, 1), 0) // group
    fresh_keys = [[None] * kv_heads for _ in range(steps)]
    fresh_values = [[None] * kv_heads for _ in range(steps)]
    queries = [[None] * kv_heads for _ in range(steps)]
    for g in range(2):
        for t in range(steps):
            rows = halves[g][t * pitch:(t + 1) * pitch]
            first_k = half_heads
            first_v = first_k + half_kv
            first_s = first_v + half_kv
            squares = rows[first_s:first_s + 1] + rows[first_s + 1:first_s + 2]
            rows = rows * lax.rsqrt(squares / width + epsilon)
            cosine = table_ref[2 * t:2 * t + 1, :]
            sine = table_ref[2 * t + 1:2 * t + 2, :]
            turned = rows * cosine + pltpu.roll(rows, HD // 2, 1) * sine
            turned = turned.astype(jnp.bfloat16)
            plain = rows.astype(jnp.bfloat16)
            for k in range(half_kv):
                head = g * half_kv + k
                queries[t][head] = turned[k * group:(k + 1) * group]
                fresh_keys[t][head] = turned[first_k + k:first_k + k + 1].astype(jnp.float32)
                fresh_values[t][head] = plain[first_v + k:first_v + k + 1].astype(jnp.float32)
    new_keys_ref[...] = jnp.concatenate(
        [jnp.concatenate(row, axis=1) for row in fresh_keys], axis=0).astype(jnp.bfloat16)
    new_values_ref[...] = jnp.concatenate(
        [jnp.concatenate(row, axis=1) for row in fresh_values], axis=0).astype(jnp.bfloat16)
    contexts = [[], []]
    for head in range(kv_heads):
        columns = slice(head * HD, (head + 1) * HD)
        query = jnp.concatenate([queries[t][head] for t in range(steps)], axis=0)
        scores = lax.dot_general(
            query, keys_ref[:, columns], (((1,), (1,)), ((), ())),
            preferred_element_type=jnp.float32) * factor
        scores = jnp.where(live, scores, -jnp.inf)
        top = jnp.max(scores, axis=-1, keepdims=True)
        wide = query.astype(jnp.float32)
        fresh = []
        for s in range(steps):
            score = jnp.sum(wide * fresh_keys[s][head], axis=-1, keepdims=True) * factor
            score = jnp.where(row_step >= s, score, -jnp.inf)
            fresh.append(score)
            top = jnp.maximum(top, score)
        scores = jnp.exp(scores - top)
        total = jnp.sum(scores, axis=-1, keepdims=True)
        fresh = [jnp.exp(score - top) for score in fresh]
        for score in fresh:
            total = total + score
        weight = (scores / total).astype(jnp.bfloat16)
        mixed = jnp.dot(weight, values_ref[:, columns], preferred_element_type=jnp.float32)
        for s in range(steps):
            weight = (fresh[s] / total).astype(jnp.bfloat16).astype(jnp.float32)
            mixed = mixed + weight * fresh_values[s][head]
        contexts[head // half_kv].append(mixed)
    rows = [
        jnp.concatenate([half[k][t * group:(t + 1) * group] for t in range(steps) for k in range(half_kv)], axis=0)
        for half in contexts]
    same_ref[...] = jnp.where(low_side, rows[0], rows[1]).astype(jnp.bfloat16)
    cross_ref[...] = jnp.where(low_side, rows[1], rows[0]).astype(jnp.bfloat16)


def attend(place, length, parts, table, keys, values, held, steps, pitch, width, half_heads, direct):
    vmem = pl.BlockSpec(memory_space=pltpu.VMEM)
    smem = pl.BlockSpec(memory_space=pltpu.SMEM)
    kv_cols = keys.shape[1]
    half = jax.ShapeDtypeStruct((steps * half_heads, HD), jnp.bfloat16)
    fresh = jax.ShapeDtypeStruct((steps, kv_cols), jnp.bfloat16)
    return pl.pallas_call(
        functools.partial(attend_kernel, steps, pitch, width, direct),
        out_shape=(half, half, fresh, fresh),
        in_specs=[smem, smem, vmem, vmem, vmem, pl.BlockSpec(memory_space=pl.ANY)] + [vmem] * len(parts),
        out_specs=(vmem,) * 4,
        compiler_params=pltpu.CompilerParams(vmem_limit_bytes=16 * MIB),
        name="attend",
    )(place, length, table, keys, values, held, *parts)


def output_kernel(steps, chunk, place_ref, weight_ref, *rest):
    context_refs, (mine_ref, other_ref, wide_buf, rows_buf) = rest[:-4], rest[-4:]
    device = place_ref[0]
    heads = weight_ref.shape[0] // HD
    per_device = steps * heads
    devices = wide_buf.shape[0] // per_device
    half_seqs = devices // 2
    columns = weight_ref.shape[1]
    if len(context_refs) == 1:
        wide_buf[...] = context_refs[0][...].astype(jnp.float32).reshape(wide_buf.shape)
    else:
        for k, ref in enumerate(context_refs):
            start = pl.multiple_of((device ^ k) * per_device, 8)
            wide_buf[pl.ds(start, per_device), :] = ref[...].astype(jnp.float32)
    for h in range(heads):
        pieces = []
        for g in range(2):
            for t in range(steps):
                start = (g * half_seqs * steps + t) * heads + h
                pieces.append(wide_buf[pl.ds(start, half_seqs, stride=per_device), :])
        rows_buf[:, h * HD:(h + 1) * HD] = jnp.concatenate(pieces, axis=0).astype(jnp.bfloat16)
    rows = rows_buf[...]
    low_side = device % 2 == 0
    half = rows.shape[0] // 2
    for c in range(columns // chunk):
        span = slice(c * chunk, (c + 1) * chunk)
        product = jnp.dot(rows, weight_ref[:, span], preferred_element_type=jnp.float32)
        lower, upper = product[:half], product[half:]
        mine_ref[:, span] = jnp.where(low_side, lower, upper)
        other_ref[:, span] = jnp.where(low_side, upper, lower).astype(jnp.bfloat16)


def output(place, contexts, weight, devices, steps):
    depth, columns = weight.shape
    chunk = min(columns, 512)
    half = devices * steps // 2
    vmem = pl.BlockSpec(memory_space=pltpu.VMEM)
    smem = pl.BlockSpec(memory_space=pltpu.SMEM)
    return pl.pallas_call(
        functools.partial(output_kernel, steps, chunk),
        out_shape=(
            jax.ShapeDtypeStruct((half, columns), jnp.float32),
            jax.ShapeDtypeStruct((half, columns), jnp.bfloat16),
        ),
        in_specs=[smem, vmem] + [vmem] * len(contexts),
        out_specs=(vmem, vmem),
        scratch_shapes=[
            pltpu.VMEM((devices * steps * depth // HD, HD), jnp.float32),
            pltpu.VMEM((devices * steps, depth), jnp.bfloat16),
        ],
        compiler_params=pltpu.CompilerParams(vmem_limit_bytes=24 * MIB),
        cost_estimate=pl.CostEstimate(
            flops=2 * devices * steps * depth * columns,
            bytes_accessed=2 * depth * columns, transcendentals=0),
        name="output",
    )(place, weight, *contexts)


def body(hidden_in, norm_gain, query_weight, key_weight, value_weight, out_weight,
         cache_keys, cache_values, lengths, positions):
    steps, half_seqs, depth = hidden_in.shape
    both = ("gx", "gy")
    devices = lax.axis_size(both)
    direct = False
    half_heads = query_weight.shape[1] // HD
    heads_here = half_heads + 2 * key_weight.shape[1] // HD
    pitch = -(-(heads_here + 2) // 8) * 8
    place = lax.axis_index(both).astype(jnp.int32).reshape(1)
    swap = [(0, 1), (1, 0)]

    def partner(array, k):
        if k == 0:
            return array
        return lax.ppermute(array, both, [(i, i ^ k) for i in range(devices)])

    def to_all(array):
        return lax.all_to_all(array, both, split_axis=0, concat_axis=0, tiled=True)

    mine = hidden_in.reshape(steps * half_seqs, depth)
    other = lax.ppermute(mine, "gy", swap)
    parts = project(place, mine, other, norm_gain.reshape(-1, HD), query_weight, key_weight,
                    value_weight, steps, pitch, direct)

    held_weight = fetch(out_weight, parts[0])
    if direct:
        parts = [partner(part, k) for k, part in enumerate(parts)]
    else:
        parts = [to_all(parts[0])]
    table = rope_table(positions[0], steps)
    same, cross, new_keys, new_values = attend(
        place, lengths, parts, table, cache_keys[0], cache_values[0], held_weight,
        steps, pitch, depth * lax.axis_size("gx"), half_heads, direct)
    if direct:
        contexts = [partner(cross if k % 2 else same, k) for k in range(devices)]
    else:
        pair = jnp.where(place[0] % 2 == 0, jnp.stack([same, cross]), jnp.stack([cross, same]))
        contexts = [to_all(jnp.tile(pair, (devices // 2, 1, 1)))]
    mine, other = output(place, contexts, held_weight, devices, steps)
    other = lax.ppermute(other, "gy", swap)
    result = (mine + other.astype(jnp.float32)).astype(jnp.bfloat16)
    return (
        result.reshape(steps, half_seqs, -1),
        new_keys[:, None, :],
        new_values[:, None, :],
    )


def solution(mesh):
    in_specs = (
        P(None, ("rep", "gy"), "gx"),
        P("gx"),
        P("gx", "gy"),
        P("gx", "gy"),
        P("gx", "gy"),
        P("gy", "gx"),
        P(("rep", "gx", "gy"), None, None),
        P(("rep", "gx", "gy"), None, None),
        P(("rep", "gx", "gy")),
        P(("rep", "gx", "gy")),
    )
    out_specs = (
        P(None, ("rep", "gy"), "gx"),
        P(None, ("rep", "gx", "gy"), None),
        P(None, ("rep", "gx", "gy"), None),
    )
    return jax.shard_map(body, mesh=mesh, in_specs=in_specs, out_specs=out_specs, check_vma=False)
```

```python
import functools
import math

import jax
import jax.numpy as jnp
from jax import lax
from jax.experimental import pallas as pl
from jax.experimental.pallas import tpu as pltpu
from jax.sharding import PartitionSpec as P

HD = 128
epsilon = 1e-05
rope_theta = 500000.0
MIB = 1024 * 1024


def rope_frequencies(head_size):
    index = jnp.arange(head_size // 2).astype(jnp.float32)
    frequency = jnp.exp(-math.log(rope_theta) * 2.0 * index / head_size)
    wavelength = 2.0 * math.pi / frequency
    smooth = (8192.0 / wavelength - 1.0) / 3.0
    blended = (1.0 - smooth) * frequency / 8.0 + smooth * frequency
    adjusted = jnp.where(wavelength > 8192.0, frequency / 8.0, blended)
    return jnp.where(wavelength < 2048.0, frequency, adjusted)


def rope_table(position, steps):
    frequency = rope_frequencies(HD)
    places = position + jnp.arange(steps, dtype=jnp.int32)
    angle = places.astype(jnp.float32)[:, None] * frequency
    cosine, sine = jnp.cos(angle), jnp.sin(angle)
    return jnp.concatenate(
        [cosine, cosine, -sine, sine], axis=-1
    ).reshape(2 * steps, HD)


def in_hbm(array):
    return pltpu.with_memory_space_constraint(array, pltpu.HBM)


def in_vmem(array):
    return pltpu.with_memory_space_constraint(array, pltpu.VMEM)


def project_kernel(steps, pitch, chunk, place_ref, mine_ref, other_ref, gain_ref, wq_ref, wk_ref, wv_ref,
                   *rest):
    out_refs, (mine_buf, gain_buf, wq_buf, wk_buf, wv_buf, rows_buf, sems) = rest[:-7], rest[-7:]
    q_cols = wq_ref.shape[1]
    kv_cols = wk_ref.shape[1]
    chunks = q_cols // chunk
    copies = [pltpu.make_async_copy(mine_ref, mine_buf, sems.at[chunks]),
              pltpu.make_async_copy(gain_ref, gain_buf, sems.at[chunks + 1]),
              pltpu.make_async_copy(wk_ref, wk_buf, sems.at[chunks + 2]),
              pltpu.make_async_copy(wv_ref, wv_buf, sems.at[chunks + 3])]
    for c in range(chunks):
        copies.append(pltpu.make_async_copy(
            wq_ref.at[:, c * chunk:(c + 1) * chunk], wq_buf.at[c], sems.at[c]))
    for copy in copies:
        copy.start()

    device = place_ref[0]
    half_rows = mine_ref.shape[0]
    total_rows = 2 * half_rows
    half_seqs = half_rows // steps
    stride = steps * pitch

    def spread(head, block):
        for g in range(2):
            for t in range(steps):
                first = (g * steps + t) * half_seqs
                start = (g * half_seqs * steps + t) * pitch + head
                rows_buf[pl.ds(start, half_seqs, stride=stride), :] = block[first:first + half_seqs, :]

    low_side = device % 2 == 0
    copies[0].wait()
    copies[1].wait()
    mine = mine_buf[...].astype(jnp.float32)
    other = other_ref[...].astype(jnp.float32)
    x = jnp.concatenate(
        [jnp.where(low_side, mine, other), jnp.where(low_side, other, mine)], axis=0)
    gain = gain_buf[...].astype(jnp.float32)
    gain = jnp.concatenate([gain[i:i + 1] for i in range(gain.shape[0])], axis=1)
    scaled = (x * gain).astype(jnp.bfloat16)
    squares = jnp.sum(x * x, axis=-1, keepdims=True)
    high = squares.astype(jnp.bfloat16).astype(jnp.float32)
    low = squares - high
    heads = (q_cols + 2 * kv_cols) // HD
    spread(heads, jnp.broadcast_to(high, (total_rows, HD)))
    spread(heads + 1, jnp.broadcast_to(low, (total_rows, HD)))
    for spare in range(heads + 2, pitch):
        spread(spare, jnp.zeros((total_rows, HD), jnp.float32))

    def multiply(weights, first_head):
        product = jnp.dot(scaled, weights, preferred_element_type=jnp.float32)
        for i in range(product.shape[1] // HD):
            spread(first_head + i, product[:, i * HD:(i + 1) * HD])

    copies[2].wait()
    multiply(wk_buf[...], q_cols // HD)
    copies[3].wait()
    multiply(wv_buf[...], (q_cols + kv_cols) // HD)
    for c in range(chunks):
        copies[4 + c].wait()
        multiply(wq_buf[c], c * chunk // HD)
    if len(out_refs) == 1:
        out_refs[0][...] = rows_buf[...].reshape(out_refs[0].shape).astype(jnp.bfloat16)
    else:
        for k, out_ref in enumerate(out_refs):
            start = pl.multiple_of((device ^ k) * stride, 8)
            out_ref[...] = rows_buf[pl.ds(start, stride), :].astype(jnp.bfloat16)


def project(place, mine, other, gain, wq, wk, wv, steps, pitch, direct):
    half_rows, depth = mine.shape
    q_cols, kv_cols = wq.shape[1], wk.shape[1]
    seqs = 2 * half_rows // steps
    chunk = 512
    vmem = pl.BlockSpec(memory_space=pltpu.VMEM)
    smem = pl.BlockSpec(memory_space=pltpu.SMEM)
    hbm = pl.BlockSpec(memory_space=pltpu.HBM)
    if direct:
        out_shape = (jax.ShapeDtypeStruct((steps * pitch, HD), jnp.bfloat16),) * seqs
    else:
        out_shape = (jax.ShapeDtypeStruct((seqs, steps * pitch, HD), jnp.bfloat16),)
    return pl.pallas_call(
        functools.partial(project_kernel, steps, pitch, chunk),
        out_shape=out_shape,
        in_specs=[smem, hbm, vmem, hbm, hbm, hbm, hbm],
        out_specs=(vmem,) * len(out_shape),
        scratch_shapes=[
            pltpu.VMEM(mine.shape, jnp.bfloat16),
            pltpu.VMEM(gain.shape, jnp.bfloat16),
            pltpu.VMEM((q_cols // chunk, depth, chunk), jnp.bfloat16),
            pltpu.VMEM((depth, kv_cols), jnp.bfloat16),
            pltpu.VMEM((depth, kv_cols), jnp.bfloat16),
            pltpu.VMEM((seqs * steps * pitch, HD), jnp.float32),
            pltpu.SemaphoreType.DMA((q_cols // chunk + 4,)),
        ],
        compiler_params=pltpu.CompilerParams(vmem_limit_bytes=26 * MIB),
        cost_estimate=pl.CostEstimate(
            flops=4 * half_rows * depth * (q_cols + 2 * kv_cols),
            bytes_accessed=2 * depth * (q_cols + 2 * kv_cols), transcendentals=0),
        name="project",
    )(place, in_hbm(mine), other, in_hbm(gain), in_hbm(wq), in_hbm(wk), in_hbm(wv))


def fetch_kernel(chunks, weight_ref, after_ref, held_ref, sems):
    rows = weight_ref.shape[0] // chunks
    copies = [pltpu.make_async_copy(
        weight_ref.at[c * rows:(c + 1) * rows], held_ref.at[c * rows:(c + 1) * rows], sems.at[c])
        for c in range(chunks)]
    for copy in copies:
        copy.start()
    for copy in copies:
        copy.wait()


def fetch(weight, after):
    chunks = 8
    return pl.pallas_call(
        functools.partial(fetch_kernel, chunks),
        out_shape=pltpu.VMEM(weight.shape, weight.dtype),
        in_specs=[pl.BlockSpec(memory_space=pltpu.HBM), pl.BlockSpec(memory_space=pl.ANY)],
        out_specs=pl.BlockSpec(memory_space=pltpu.VMEM),
        scratch_shapes=[pltpu.SemaphoreType.DMA((chunks,))],
        compiler_params=pltpu.CompilerParams(vmem_limit_bytes=8 * MIB),
        cost_estimate=pl.CostEstimate(
            flops=0, bytes_accessed=2 * weight.size, transcendentals=0),
        name="fetch",
    )(in_hbm(weight), after)


def attend_kernel(steps, pitch, width, direct, place_ref, length_ref, table_ref, keys_ref, values_ref, held_ref,
                  *rest):
    part_refs, (same_ref, cross_ref, new_keys_ref, new_values_ref) = rest[:-4], rest[-4:]
    kv_heads = keys_ref.shape[1] // HD
    half_kv = kv_heads // 2
    half_heads = same_ref.shape[0] // steps
    low_side = place_ref[0] % 2 == 0
    if direct:
        same, cross = [
            functools.reduce(jnp.add, [ref[...].astype(jnp.float32) for ref in part_refs[i::2]])
            for i in range(2)]
    else:
        parts_ref = part_refs[0]
        even, odd = [
            functools.reduce(jnp.add, [
                parts_ref[i].astype(jnp.float32) for i in range(g, parts_ref.shape[0], 2)])
            for g in range(2)]
        same, cross = jnp.where(low_side, even, odd), jnp.where(low_side, odd, even)
    halves = [jnp.where(low_side, same, cross), jnp.where(low_side, cross, same)]
    group = half_heads // half_kv
    slots = keys_ref.shape[0]
    factor = 1.0 / math.sqrt(HD)
    live = lax.broadcasted_iota(jnp.int32, (steps * group, slots), 1) < length_ref[0]
    row_step = lax.broadcasted_iota(jnp.int32, (steps * group, 1), 0) // group
    fresh_keys = [[None] * kv_heads for _ in range(steps)]
    fresh_values = [[None] * kv_heads for _ in range(steps)]
    queries = [[None] * kv_heads for _ in range(steps)]
    for g in range(2):
        for t in range(steps):
            rows = halves[g][t * pitch:(t + 1) * pitch]
            first_k = half_heads
            first_v = first_k + half_kv
            first_s = first_v + half_kv
            squares = rows[first_s:first_s + 1] + rows[first_s + 1:first_s + 2]
            rows = rows * lax.rsqrt(squares / width + epsilon)
            cosine = table_ref[2 * t:2 * t + 1, :]
            sine = table_ref[2 * t + 1:2 * t + 2, :]
            turned = rows * cosine + pltpu.roll(rows, HD // 2, 1) * sine
            turned = turned.astype(jnp.bfloat16)
            plain = rows.astype(jnp.bfloat16)
            for k in range(half_kv):
                head = g * half_kv + k
                queries[t][head] = turned[k * group:(k + 1) * group]
                fresh_keys[t][head] = turned[first_k + k:first_k + k + 1].astype(jnp.float32)
                fresh_values[t][head] = plain[first_v + k:first_v + k + 1].astype(jnp.float32)
    new_keys_ref[...] = jnp.concatenate(
        [jnp.concatenate(row, axis=1) for row in fresh_keys], axis=0).astype(jnp.bfloat16)
    new_values_ref[...] = jnp.concatenate(
        [jnp.concatenate(row, axis=1) for row in fresh_values], axis=0).astype(jnp.bfloat16)
    contexts = [[], []]
    for head in range(kv_heads):
        columns = slice(head * HD, (head + 1) * HD)
        query = jnp.concatenate([queries[t][head] for t in range(steps)], axis=0)
        scores = lax.dot_general(
            query, keys_ref[:, columns], (((1,), (1,)), ((), ())),
            preferred_element_type=jnp.float32) * factor
        scores = jnp.where(live, scores, -jnp.inf)
        top = jnp.max(scores, axis=-1, keepdims=True)
        wide = query.astype(jnp.float32)
        fresh = []
        for s in range(steps):
            score = jnp.sum(wide * fresh_keys[s][head], axis=-1, keepdims=True) * factor
            score = jnp.where(row_step >= s, score, -jnp.inf)
            fresh.append(score)
            top = jnp.maximum(top, score)
        scores = jnp.exp(scores - top)
        total = jnp.sum(scores, axis=-1, keepdims=True)
        fresh = [jnp.exp(score - top) for score in fresh]
        for score in fresh:
            total = total + score
        weight = (scores / total).astype(jnp.bfloat16)
        mixed = jnp.dot(weight, values_ref[:, columns], preferred_element_type=jnp.float32)
        for s in range(steps):
            weight = (fresh[s] / total).astype(jnp.bfloat16).astype(jnp.float32)
            mixed = mixed + weight * fresh_values[s][head]
        contexts[head // half_kv].append(mixed)
    rows = [
        jnp.concatenate([half[k][t * group:(t + 1) * group] for t in range(steps) for k in range(half_kv)], axis=0)
        for half in contexts]
    same_ref[...] = jnp.where(low_side, rows[0], rows[1]).astype(jnp.bfloat16)
    cross_ref[...] = jnp.where(low_side, rows[1], rows[0]).astype(jnp.bfloat16)


def attend(place, length, parts, table, keys, values, held, steps, pitch, width, half_heads, direct):
    vmem = pl.BlockSpec(memory_space=pltpu.VMEM)
    smem = pl.BlockSpec(memory_space=pltpu.SMEM)
    kv_cols = keys.shape[1]
    half = jax.ShapeDtypeStruct((steps * half_heads, HD), jnp.bfloat16)
    fresh = jax.ShapeDtypeStruct((steps, kv_cols), jnp.bfloat16)
    return pl.pallas_call(
        functools.partial(attend_kernel, steps, pitch, width, direct),
        out_shape=(half, half, fresh, fresh),
        in_specs=[smem, smem, vmem, vmem, vmem, pl.BlockSpec(memory_space=pl.ANY)] + [vmem] * len(parts),
        out_specs=(vmem,) * 4,
        compiler_params=pltpu.CompilerParams(vmem_limit_bytes=16 * MIB),
        name="attend",
    )(place, length, table, keys, values, in_vmem(held), *parts)


def output_kernel(steps, chunk, place_ref, weight_ref, *rest):
    context_refs, (mine_ref, other_ref, wide_buf, rows_buf) = rest[:-4], rest[-4:]
    device = place_ref[0]
    heads = weight_ref.shape[0] // HD
    per_device = steps * heads
    devices = wide_buf.shape[0] // per_device
    half_seqs = devices // 2
    columns = weight_ref.shape[1]
    if len(context_refs) == 1:
        wide_buf[...] = context_refs[0][...].astype(jnp.float32).reshape(wide_buf.shape)
    else:
        for k, ref in enumerate(context_refs):
            start = pl.multiple_of((device ^ k) * per_device, 8)
            wide_buf[pl.ds(start, per_device), :] = ref[...].astype(jnp.float32)
    for h in range(heads):
        pieces = []
        for g in range(2):
            for t in range(steps):
                start = (g * half_seqs * steps + t) * heads + h
                pieces.append(wide_buf[pl.ds(start, half_seqs, stride=per_device), :])
        rows_buf[:, h * HD:(h + 1) * HD] = jnp.concatenate(pieces, axis=0).astype(jnp.bfloat16)
    rows = rows_buf[...]
    low_side = device % 2 == 0
    half = rows.shape[0] // 2
    for c in range(columns // chunk):
        span = slice(c * chunk, (c + 1) * chunk)
        product = jnp.dot(rows, weight_ref[:, span], preferred_element_type=jnp.float32)
        lower, upper = product[:half], product[half:]
        mine_ref[:, span] = jnp.where(low_side, lower, upper)
        other_ref[:, span] = jnp.where(low_side, upper, lower).astype(jnp.bfloat16)


def output(place, contexts, weight, devices, steps):
    depth, columns = weight.shape
    chunk = min(columns, 512)
    half = devices * steps // 2
    vmem = pl.BlockSpec(memory_space=pltpu.VMEM)
    smem = pl.BlockSpec(memory_space=pltpu.SMEM)
    return pl.pallas_call(
        functools.partial(output_kernel, steps, chunk),
        out_shape=(
            jax.ShapeDtypeStruct((half, columns), jnp.float32),
            jax.ShapeDtypeStruct((half, columns), jnp.bfloat16),
        ),
        in_specs=[smem, vmem] + [vmem] * len(contexts),
        out_specs=(vmem, vmem),
        scratch_shapes=[
            pltpu.VMEM((devices * steps * depth // HD, HD), jnp.float32),
            pltpu.VMEM((devices * steps, depth), jnp.bfloat16),
        ],
        compiler_params=pltpu.CompilerParams(vmem_limit_bytes=24 * MIB),
        cost_estimate=pl.CostEstimate(
            flops=2 * devices * steps * depth * columns,
            bytes_accessed=2 * depth * columns, transcendentals=0),
        name="output",
    )(place, in_vmem(weight), *contexts)


def body(hidden_in, norm_gain, query_weight, key_weight, value_weight, out_weight,
         cache_keys, cache_values, lengths, positions):
    steps, half_seqs, depth = hidden_in.shape
    both = ("gx", "gy")
    devices = lax.axis_size(both)
    direct = False
    half_heads = query_weight.shape[1] // HD
    heads_here = half_heads + 2 * key_weight.shape[1] // HD
    pitch = -(-(heads_here + 2) // 8) * 8
    place = lax.axis_index(both).astype(jnp.int32).reshape(1)
    swap = [(0, 1), (1, 0)]

    def partner(array, k):
        if k == 0:
            return array
        return lax.ppermute(array, both, [(i, i ^ k) for i in range(devices)])

    def to_all(array):
        return lax.all_to_all(array, both, split_axis=0, concat_axis=0, tiled=True)

    mine = hidden_in.reshape(steps * half_seqs, depth)
    other = lax.ppermute(mine, "gy", swap)
    parts = project(place, mine, other, norm_gain.reshape(-1, HD), query_weight, key_weight,
                    value_weight, steps, pitch, direct)

    held_weight = fetch(out_weight, parts[0])
    if direct:
        parts = [partner(part, k) for k, part in enumerate(parts)]
    else:
        parts = [to_all(parts[0])]
    table = rope_table(positions[0], steps)
    same, cross, new_keys, new_values = attend(
        place, lengths, parts, table, cache_keys[0], cache_values[0], held_weight,
        steps, pitch, depth * lax.axis_size("gx"), half_heads, direct)
    if direct:
        contexts = [partner(cross if k % 2 else same, k) for k in range(devices)]
    else:
        pair = jnp.where(place[0] % 2 == 0, jnp.stack([same, cross]), jnp.stack([cross, same]))
        contexts = [to_all(jnp.tile(pair, (devices // 2, 1, 1)))]
    mine, other = output(place, contexts, held_weight, devices, steps)
    other = lax.ppermute(other, "gy", swap)
    result = (mine + other.astype(jnp.float32)).astype(jnp.bfloat16)
    return (
        result.reshape(steps, half_seqs, -1),
        new_keys[:, None, :],
        new_values[:, None, :],
    )


def solution(mesh):
    in_specs = (
        P(None, ("rep", "gy"), "gx"),
        P("gx"),
        P("gx", "gy"),
        P("gx", "gy"),
        P("gx", "gy"),
        P("gy", "gx"),
        P(("rep", "gx", "gy"), None, None),
        P(("rep", "gx", "gy"), None, None),
        P(("rep", "gx", "gy")),
        P(("rep", "gx", "gy")),
    )
    out_specs = (
        P(None, ("rep", "gy"), "gx"),
        P(None, ("rep", "gx", "gy"), None),
        P(None, ("rep", "gx", "gy"), None),
    )
    return jax.shard_map(body, mesh=mesh, in_specs=in_specs, out_specs=out_specs, check_vma=False)
```

```python
import functools
import math

import jax
import jax.numpy as jnp
from jax import lax
from jax.experimental import pallas as pl
from jax.experimental.pallas import tpu as pltpu
from jax.sharding import PartitionSpec as P

HD = 128
epsilon = 1e-05
rope_theta = 500000.0
MIB = 1024 * 1024


def rope_frequencies(head_size):
    index = jnp.arange(head_size // 2).astype(jnp.float32)
    frequency = jnp.exp(-math.log(rope_theta) * 2.0 * index / head_size)
    wavelength = 2.0 * math.pi / frequency
    smooth = (8192.0 / wavelength - 1.0) / 3.0
    blended = (1.0 - smooth) * frequency / 8.0 + smooth * frequency
    adjusted = jnp.where(wavelength > 8192.0, frequency / 8.0, blended)
    return jnp.where(wavelength < 2048.0, frequency, adjusted)


def rope_table(position, steps):
    frequency = rope_frequencies(HD)
    places = position + jnp.arange(steps, dtype=jnp.int32)
    angle = places.astype(jnp.float32)[:, None] * frequency
    cosine, sine = jnp.cos(angle), jnp.sin(angle)
    return jnp.concatenate(
        [cosine, cosine, -sine, sine], axis=-1
    ).reshape(2 * steps, HD)


def in_hbm(array):
    return pltpu.with_memory_space_constraint(array, pltpu.HBM)


def in_vmem(array):
    return pltpu.with_memory_space_constraint(array, pltpu.VMEM)


def slot_patterns(order):
    count = len(order)
    return [
        sum(((j >> (count - 1 - i)) & 1) << bit for i, bit in enumerate(order))
        for j in range(1 << count)]


def project_kernel(steps, group, orders, chunk, place_ref, mine_ref, other_ref, gain_ref, wq_ref, wk_ref, wv_ref,
                   table_ref, length_ref, *rest):
    out_refs, (mine_buf, gain_buf, wq_buf, wk_buf, wv_buf, rows_buf, sems) = rest[:-7], rest[-7:]
    q_cols = wq_ref.shape[1]
    kv_cols = wk_ref.shape[1]
    chunks = q_cols // chunk
    copies = [pltpu.make_async_copy(mine_ref, mine_buf, sems.at[chunks]),
              pltpu.make_async_copy(gain_ref, gain_buf, sems.at[chunks + 1]),
              pltpu.make_async_copy(wk_ref, wk_buf, sems.at[chunks + 2]),
              pltpu.make_async_copy(wv_ref, wv_buf, sems.at[chunks + 3])]
    for c in range(chunks):
        copies.append(pltpu.make_async_copy(
            wq_ref.at[:, c * chunk:(c + 1) * chunk], wq_buf.at[c], sems.at[c]))
    for copy in copies:
        copy.start()

    device = place_ref[0]
    half_rows = mine_ref.shape[0]
    total_rows = 2 * half_rows
    half_seqs = half_rows // steps
    pitch = group + 4
    stride = steps * pitch
    seqs = 2 * half_seqs

    def spread(color, row, block):
        for g in range(2):
            for t in range(steps):
                first = (g * steps + t) * half_seqs
                start = color * seqs * stride + (g * half_seqs * steps + t) * pitch + row
                rows_buf[pl.ds(start, half_seqs, stride=stride), :] = block[first:first + half_seqs, :]

    low_side = device % 2 == 0
    copies[0].wait()
    copies[1].wait()
    mine = mine_buf[...].astype(jnp.float32)
    other = other_ref[...].astype(jnp.float32)
    x = jnp.concatenate(
        [jnp.where(low_side, mine, other), jnp.where(low_side, other, mine)], axis=0)
    gain = gain_buf[...].astype(jnp.float32)
    gain = jnp.concatenate([gain[i:i + 1] for i in range(gain.shape[0])], axis=1)
    scaled = (x * gain).astype(jnp.bfloat16)
    squares = jnp.sum(x * x, axis=-1, keepdims=True)
    high = squares.astype(jnp.bfloat16).astype(jnp.float32)
    low = squares - high
    for color in range(len(orders)):
        spread(color, group + 2, jnp.broadcast_to(high, (total_rows, HD)))
        spread(color, group + 3, jnp.broadcast_to(low, (total_rows, HD)))

    def multiply(weights, place_of_head):
        product = jnp.dot(scaled, weights, preferred_element_type=jnp.float32)
        for i in range(product.shape[1] // HD):
            spread(*place_of_head(i), product[:, i * HD:(i + 1) * HD])

    copies[2].wait()
    multiply(wk_buf[...], lambda i: (i, group))
    copies[3].wait()
    multiply(wv_buf[...], lambda i: (i, group + 1))
    for c in range(chunks):
        copies[4 + c].wait()
        first = c * chunk // HD
        multiply(wq_buf[c], lambda i: ((first + i) // group, (first + i) % group))
    for color, order in enumerate(orders):
        keep_ref, send_ref = out_refs[2 * color:2 * color + 2]
        for j, pattern in enumerate(slot_patterns(order)):
            start = pl.multiple_of(color * seqs * stride + (device ^ pattern) * stride, 8)
            rows = rows_buf[pl.ds(start, stride), :]
            if j < seqs // 2:
                keep_ref[j] = rows
            else:
                send_ref[j - seqs // 2] = rows.astype(jnp.bfloat16)


def project(place, mine, other, gain, wq, wk, wv, table, length, steps, group, orders):
    half_rows, depth = mine.shape
    q_cols, kv_cols = wq.shape[1], wk.shape[1]
    seqs = 2 * half_rows // steps
    chunk = 512
    vmem = pl.BlockSpec(memory_space=pltpu.VMEM)
    smem = pl.BlockSpec(memory_space=pltpu.SMEM)
    hbm = pl.BlockSpec(memory_space=pltpu.HBM)
    block = (seqs // 2, steps * (group + 4), HD)
    out_shape = (
        jax.ShapeDtypeStruct(block, jnp.float32), jax.ShapeDtypeStruct(block, jnp.bfloat16)) * len(orders)
    return pl.pallas_call(
        functools.partial(project_kernel, steps, group, orders, chunk),
        out_shape=out_shape,
        in_specs=[smem, hbm, vmem, hbm, hbm, hbm, hbm, pl.BlockSpec(memory_space=pl.ANY), smem],
        out_specs=(vmem,) * len(out_shape),
        scratch_shapes=[
            pltpu.VMEM(mine.shape, jnp.bfloat16),
            pltpu.VMEM(gain.shape, jnp.bfloat16),
            pltpu.VMEM((q_cols // chunk, depth, chunk), jnp.bfloat16),
            pltpu.VMEM((depth, kv_cols), jnp.bfloat16),
            pltpu.VMEM((depth, kv_cols), jnp.bfloat16),
            pltpu.VMEM((len(orders) * seqs * steps * (group + 4), HD), jnp.float32),
            pltpu.SemaphoreType.DMA((q_cols // chunk + 4,)),
        ],
        compiler_params=pltpu.CompilerParams(vmem_limit_bytes=28 * MIB),
        cost_estimate=pl.CostEstimate(
            flops=4 * half_rows * depth * (q_cols + 2 * kv_cols),
            bytes_accessed=2 * depth * (q_cols + 2 * kv_cols), transcendentals=0),
        name="project",
    )(place, in_hbm(mine), other, in_hbm(gain), in_hbm(wq), in_hbm(wk), in_hbm(wv), table, length)


def combine_kernel(colors, last, *refs):
    ins, outs = refs[:2 * colors], refs[-2 * colors:]
    if last:
        outs = refs[-2:]
    for color in range(colors):
        total = ins[2 * color][...] + ins[2 * color + 1][...].astype(jnp.float32)
        half = total.shape[0] // 2
        if last:
            outs[0][color] = total[0]
            outs[1][color] = total[1].astype(jnp.bfloat16)
        else:
            outs[2 * color][...] = total[:half]
            outs[2 * color + 1][...] = total[half:].astype(jnp.bfloat16)


def combine(pairs, held):
    colors = len(pairs)
    shape = pairs[0][0].shape
    last = shape[0] == 2
    vmem = pl.BlockSpec(memory_space=pltpu.VMEM)
    block = ((colors,) if last else (shape[0] // 2,)) + shape[1:]
    out_shape = (
        jax.ShapeDtypeStruct(block, jnp.float32), jax.ShapeDtypeStruct(block, jnp.bfloat16))
    if not last:
        out_shape = out_shape * colors
    return pl.pallas_call(
        functools.partial(combine_kernel, colors, last),
        out_shape=out_shape,
        in_specs=[vmem] * (2 * colors) + [pl.BlockSpec(memory_space=pl.ANY)] * len(held),
        out_specs=(vmem,) * len(out_shape),
        compiler_params=pltpu.CompilerParams(vmem_limit_bytes=16 * MIB),
        name="combine",
    )(*[array for pair in pairs for array in pair], *[in_vmem(piece) for piece in held])


def fetch_kernel(first, parts, weight_ref, after_ref, held_ref, sems):
    rows = weight_ref.shape[0] // parts
    columns = held_ref.shape[1]
    copies = []
    for c in range(parts):
        span = slice(c * rows, (c + 1) * rows)
        copies.append(pltpu.make_async_copy(
            weight_ref.at[span, first:first + columns], held_ref.at[span], sems.at[c]))
    for copy in copies:
        copy.start()
    for copy in copies:
        copy.wait()


def fetch(weight, first, columns, after):
    parts = 4
    return pl.pallas_call(
        functools.partial(fetch_kernel, first, parts),
        out_shape=pltpu.VMEM((weight.shape[0], columns), weight.dtype),
        in_specs=[pl.BlockSpec(memory_space=pltpu.HBM), pl.BlockSpec(memory_space=pl.ANY)],
        out_specs=pl.BlockSpec(memory_space=pltpu.VMEM),
        scratch_shapes=[pltpu.SemaphoreType.DMA((parts,))],
        compiler_params=pltpu.CompilerParams(vmem_limit_bytes=8 * MIB),
        cost_estimate=pl.CostEstimate(
            flops=0, bytes_accessed=2 * weight.shape[0] * columns, transcendentals=0),
        name="fetch",
    )(in_hbm(weight), after)


def attend_kernel(steps, width, place_ref, length_ref, table_ref, keys_ref, values_ref, same_in_ref, cross_in_ref,
                  *rest):
    same_ref, cross_ref, new_keys_ref, new_values_ref = rest[-4:]
    kv_heads = keys_ref.shape[1] // HD
    half_kv = kv_heads // 2
    pitch = same_in_ref.shape[1] // steps
    group = pitch - 4
    slots = keys_ref.shape[0]
    factor = 1.0 / math.sqrt(HD)
    low_side = place_ref[0] % 2 == 0
    live = lax.broadcasted_iota(jnp.int32, (steps * group, slots), 1) < length_ref[0]
    row_step = lax.broadcasted_iota(jnp.int32, (steps * group, 1), 0) // group
    fresh_keys = [[None] * kv_heads for _ in range(steps)]
    fresh_values = [[None] * kv_heads for _ in range(steps)]
    queries = [None] * kv_heads
    for k in range(half_kv):
        same, cross = same_in_ref[k], cross_in_ref[k].astype(jnp.float32)
        halves = [jnp.where(low_side, same, cross), jnp.where(low_side, cross, same)]
        for g in range(2):
            head = g * half_kv + k
            query = []
            for t in range(steps):
                rows = halves[g][t * pitch:(t + 1) * pitch]
                squares = rows[group + 2:group + 3] + rows[group + 3:group + 4]
                rows = rows * lax.rsqrt(squares / width + epsilon)
                cosine = table_ref[2 * t:2 * t + 1, :]
                sine = table_ref[2 * t + 1:2 * t + 2, :]
                turned = rows * cosine + pltpu.roll(rows, HD // 2, 1) * sine
                query.append(turned[:group])
                fresh_keys[t][head] = turned[group:group + 1].astype(jnp.bfloat16).astype(jnp.float32)
                fresh_values[t][head] = rows[group + 1:group + 2].astype(jnp.bfloat16).astype(jnp.float32)
            queries[head] = jnp.concatenate(query, axis=0).astype(jnp.bfloat16)
    new_keys_ref[...] = jnp.concatenate(
        [jnp.concatenate(row, axis=1) for row in fresh_keys], axis=0).astype(jnp.bfloat16)
    new_values_ref[...] = jnp.concatenate(
        [jnp.concatenate(row, axis=1) for row in fresh_values], axis=0).astype(jnp.bfloat16)
    contexts = []
    for head in range(kv_heads):
        columns = slice(head * HD, (head + 1) * HD)
        query = queries[head]
        scores = lax.dot_general(
            query, keys_ref[:, columns], (((1,), (1,)), ((), ())),
            preferred_element_type=jnp.float32) * factor
        scores = jnp.where(live, scores, -jnp.inf)
        top = jnp.max(scores, axis=-1, keepdims=True)
        wide = query.astype(jnp.float32)
        fresh = []
        for s in range(steps):
            score = jnp.sum(wide * fresh_keys[s][head], axis=-1, keepdims=True) * factor
            score = jnp.where(row_step >= s, score, -jnp.inf)
            fresh.append(score)
            top = jnp.maximum(top, score)
        scores = jnp.exp(scores - top)
        total = jnp.sum(scores, axis=-1, keepdims=True)
        fresh = [jnp.exp(score - top) for score in fresh]
        for score in fresh:
            total = total + score
        weight = (scores / total).astype(jnp.bfloat16)
        mixed = jnp.dot(weight, values_ref[:, columns], preferred_element_type=jnp.float32)
        for s in range(steps):
            weight = (fresh[s] / total).astype(jnp.bfloat16).astype(jnp.float32)
            mixed = mixed + weight * fresh_values[s][head]
        contexts.append(mixed)
    for k in range(half_kv):
        lower, upper = contexts[k], contexts[half_kv + k]
        same_ref[k] = jnp.where(low_side, lower, upper).astype(jnp.bfloat16)
        cross_ref[k] = jnp.where(low_side, upper, lower).astype(jnp.bfloat16)


def attend(place, length, same, cross, table, keys, values, held, steps, width):
    vmem = pl.BlockSpec(memory_space=pltpu.VMEM)
    smem = pl.BlockSpec(memory_space=pltpu.SMEM)
    kv_cols = keys.shape[1]
    group = same.shape[1] // steps - 4
    half = jax.ShapeDtypeStruct((same.shape[0], steps * group, HD), jnp.bfloat16)
    fresh = jax.ShapeDtypeStruct((steps, kv_cols), jnp.bfloat16)
    return pl.pallas_call(
        functools.partial(attend_kernel, steps, width),
        out_shape=(half, half, fresh, fresh),
        in_specs=[smem, smem] + [vmem] * 5 + [pl.BlockSpec(memory_space=pl.ANY)] * len(held),
        out_specs=(vmem,) * 4,
        compiler_params=pltpu.CompilerParams(vmem_limit_bytes=16 * MIB),
        name="attend",
    )(place, length, table, keys, values, same, cross, *[in_vmem(piece) for piece in held])


def pack_kernel(same_ref, other_ref, *out_refs):
    for color, out_ref in enumerate(out_refs):
        out_ref[0] = same_ref[color]
        out_ref[1] = other_ref[color]


def join_kernel(*refs):
    colors = len(refs) // 3
    for color in range(colors):
        first, second, out_ref = refs[2 * color], refs[2 * color + 1], refs[2 * colors + color]
        count = first.shape[0]
        out_ref[:count] = first[...]
        out_ref[count:] = second[...]


def local_call(kernel, out_shape, *arrays):
    vmem = pl.BlockSpec(memory_space=pltpu.VMEM)
    return pl.pallas_call(
        kernel,
        out_shape=out_shape,
        in_specs=[vmem] * len(arrays),
        out_specs=(vmem,) * len(out_shape),
        compiler_params=pltpu.CompilerParams(vmem_limit_bytes=8 * MIB),
        name="join",
    )(*arrays)


def output_kernel(steps, devices, patterns, pieces, place_ref, *rest):
    weight_refs, rest = rest[:pieces], rest[pieces:]
    buffer_refs, (mine_ref, other_ref, wide_buf, rows_buf) = rest[:-4], rest[-4:]
    device = place_ref[0]
    half_seqs = devices // 2
    block = buffer_refs[0].shape[1]
    group = block // steps
    for color, slots in enumerate(patterns):
        base = color * devices * block
        held_ref, came_ref = buffer_refs[2 * color:2 * color + 2]
        for j, pattern in enumerate(slots):
            count = held_ref.shape[0]
            rows = held_ref[j] if j < count else came_ref[j - count]
            start = pl.multiple_of(base + (device ^ pattern) * block, 8)
            wide_buf[pl.ds(start, block), :] = rows.astype(jnp.float32)
        for h in range(group):
            lines = []
            for g in range(2):
                for t in range(steps):
                    start = base + g * half_seqs * block + t * group + h
                    lines.append(wide_buf[pl.ds(start, half_seqs, stride=block), :])
            head = color * group + h
            rows_buf[:, head * HD:(head + 1) * HD] = jnp.concatenate(lines, axis=0).astype(jnp.bfloat16)
    rows = rows_buf[...]
    low_side = device % 2 == 0
    half = rows.shape[0] // 2
    chunk = weight_refs[0].shape[1]
    for c, weight_ref in enumerate(weight_refs):
        span = slice(c * chunk, (c + 1) * chunk)
        product = jnp.dot(rows, weight_ref[...], preferred_element_type=jnp.float32)
        lower, upper = product[:half], product[half:]
        mine_ref[:, span] = jnp.where(low_side, lower, upper)
        other_ref[:, span] = jnp.where(low_side, upper, lower).astype(jnp.bfloat16)


def output(place, buffers, patterns, held, devices, steps):
    depth, chunk = held[0].shape
    columns = chunk * len(held)
    block = buffers[0].shape[1]
    half = devices * steps // 2
    vmem = pl.BlockSpec(memory_space=pltpu.VMEM)
    smem = pl.BlockSpec(memory_space=pltpu.SMEM)
    return pl.pallas_call(
        functools.partial(output_kernel, steps, devices, patterns, len(held)),
        out_shape=(
            jax.ShapeDtypeStruct((half, columns), jnp.float32),
            jax.ShapeDtypeStruct((half, columns), jnp.bfloat16),
        ),
        in_specs=[smem] + [vmem] * (len(held) + len(buffers)),
        out_specs=(vmem, vmem),
        scratch_shapes=[
            pltpu.VMEM((len(patterns) * devices * block, HD), jnp.float32),
            pltpu.VMEM((devices * steps, depth), jnp.bfloat16),
        ],
        compiler_params=pltpu.CompilerParams(vmem_limit_bytes=26 * MIB),
        cost_estimate=pl.CostEstimate(
            flops=2 * devices * steps * depth * columns,
            bytes_accessed=2 * depth * columns, transcendentals=0),
        name="output",
    )(place, *[in_vmem(piece) for piece in held], *buffers)


def body(hidden_in, norm_gain, query_weight, key_weight, value_weight, out_weight,
         cache_keys, cache_values, lengths, positions):
    steps, half_seqs, depth = hidden_in.shape
    both = ("gx", "gy")
    devices = lax.axis_size(both)
    bits = devices.bit_length() - 1
    colors = key_weight.shape[1] // HD
    group = query_weight.shape[1] // HD // colors
    place = lax.axis_index(both).astype(jnp.int32).reshape(1)
    table = rope_table(positions[0], steps)

    def partner(array, bit):
        return lax.ppermute(array, both, [(i, i ^ (1 << bit)) for i in range(devices)])

    far = list(range(1, bits))
    halving = [far[c % 2:] + far[:c % 2] + [0] for c in range(colors)]
    doubling = [far[::-1] if c % 2 == 0 else far[:1] + far[:0:-1] for c in range(colors)]

    chunk = min(out_weight.shape[1], 512)
    pieces = out_weight.shape[1] // chunk
    windows = bits
    held = []

    def fetch_in(window, after):
        now = []
        for i in range(pieces):
            if min(i, windows - 1) == window:
                now.append(fetch(out_weight, i * chunk, chunk, after))
        held.extend(now)
        return now

    mine = hidden_in.reshape(steps * half_seqs, depth)
    other = partner(mine, 0)
    parts = project(place, mine, other, norm_gain.reshape(-1, HD), query_weight, key_weight,
                    value_weight, table, lengths, steps, group, halving)
    for i in range(bits - 1):
        came = [partner(parts[2 * c + 1], halving[c][i]) for c in range(colors)]
        now = fetch_in(i, parts[1])
        parts = combine([(parts[2 * c], came[c]) for c in range(colors)], now)
    same, cross = parts
    now = fetch_in(bits - 1, cross)
    cross = partner(cross, 0)
    same, cross, new_keys, new_values = attend(
        place, lengths, same, cross, table, cache_keys[0], cache_values[0], now,
        steps, depth * lax.axis_size("gx"))
    came = partner(cross, 0)
    pair = jax.ShapeDtypeStruct((2,) + same.shape[1:], jnp.bfloat16)
    buffers = local_call(pack_kernel, (pair,) * colors, same, came)
    patterns = [[0, 1] for _ in range(colors)]
    for i in range(bits - 1):
        came = [partner(buffers[c], doubling[c][i]) for c in range(colors)]
        patterns = [slots + [p ^ (1 << doubling[c][i]) for p in slots] for c, slots in enumerate(patterns)]
        both_now = [array for c in range(colors) for array in (buffers[c], came[c])]
        if i < bits - 2:
            shape = buffers[0].shape
            wider = jax.ShapeDtypeStruct((2 * shape[0],) + shape[1:], jnp.bfloat16)
            buffers = local_call(join_kernel, (wider,) * colors, *both_now)
    mine, other = output(place, both_now, patterns, held, devices, steps)
    other = partner(other, 0)
    result = (mine + other.astype(jnp.float32)).astype(jnp.bfloat16)
    return (
        result.reshape(steps, half_seqs, -1),
        new_keys[:, None, :],
        new_values[:, None, :],
    )


def solution(mesh):
    in_specs = (
        P(None, ("rep", "gy"), "gx"),
        P("gx"),
        P("gx", "gy"),
        P("gx", "gy"),
        P("gx", "gy"),
        P("gy", "gx"),
        P(("rep", "gx", "gy"), None, None),
        P(("rep", "gx", "gy"), None, None),
        P(("rep", "gx", "gy")),
        P(("rep", "gx", "gy")),
    )
    out_specs = (
        P(None, ("rep", "gy"), "gx"),
        P(None, ("rep", "gx", "gy"), None),
        P(None, ("rep", "gx", "gy"), None),
    )
    return jax.shard_map(body, mesh=mesh, in_specs=in_specs, out_specs=out_specs, check_vma=False)
```

```python
import functools
import math

import jax
import jax.numpy as jnp
from jax import lax
from jax.experimental import pallas as pl
from jax.experimental.pallas import tpu as pltpu
from jax.sharding import PartitionSpec as P

HD = 128
epsilon = 1e-05
rope_theta = 500000.0
MIB = 1024 * 1024


def rope_frequencies(head_size):
    index = jnp.arange(head_size // 2).astype(jnp.float32)
    frequency = jnp.exp(-math.log(rope_theta) * 2.0 * index / head_size)
    wavelength = 2.0 * math.pi / frequency
    smooth = (8192.0 / wavelength - 1.0) / 3.0
    blended = (1.0 - smooth) * frequency / 8.0 + smooth * frequency
    adjusted = jnp.where(wavelength > 8192.0, frequency / 8.0, blended)
    return jnp.where(wavelength < 2048.0, frequency, adjusted)


def rope_table(position, steps):
    frequency = rope_frequencies(HD)
    places = position + jnp.arange(steps, dtype=jnp.int32)
    angle = places.astype(jnp.float32)[:, None] * frequency
    cosine, sine = jnp.cos(angle), jnp.sin(angle)
    return jnp.concatenate(
        [cosine, cosine, -sine, sine], axis=-1
    ).reshape(2 * steps, HD)


def in_hbm(array):
    return pltpu.with_memory_space_constraint(array, pltpu.HBM)


def in_vmem(array):
    return pltpu.with_memory_space_constraint(array, pltpu.VMEM)


def project_kernel(steps, group, colors, chunk, place_ref, mine_ref, other_ref, gain_ref, wq_ref, wk_ref, wv_ref,
                   table_ref, length_ref, *rest):
    out_refs, (mine_buf, gain_buf, wq_buf, wk_buf, wv_buf, rows_buf, sems) = rest[:-7], rest[-7:]
    q_cols = wq_ref.shape[1]
    kv_cols = wk_ref.shape[1]
    chunks = q_cols // chunk
    copies = [pltpu.make_async_copy(mine_ref, mine_buf, sems.at[chunks]),
              pltpu.make_async_copy(gain_ref, gain_buf, sems.at[chunks + 1]),
              pltpu.make_async_copy(wk_ref, wk_buf, sems.at[chunks + 2]),
              pltpu.make_async_copy(wv_ref, wv_buf, sems.at[chunks + 3])]
    for c in range(chunks):
        copies.append(pltpu.make_async_copy(
            wq_ref.at[:, c * chunk:(c + 1) * chunk], wq_buf.at[c], sems.at[c]))
    for copy in copies:
        copy.start()

    device = place_ref[0]
    half_rows = mine_ref.shape[0]
    total_rows = 2 * half_rows
    half_seqs = half_rows // steps
    pitch = group + 4
    stride = colors * steps * pitch

    def spread(color, row, block):
        for g in range(2):
            for t in range(steps):
                first = (g * steps + t) * half_seqs
                start = g * half_seqs * stride + (color * steps + t) * pitch + row
                rows_buf[pl.ds(start, half_seqs, stride=stride), :] = block[first:first + half_seqs, :]

    low_side = device % 2 == 0
    copies[0].wait()
    copies[1].wait()
    mine = mine_buf[...].astype(jnp.float32)
    other = other_ref[...].astype(jnp.float32)
    x = jnp.concatenate(
        [jnp.where(low_side, mine, other), jnp.where(low_side, other, mine)], axis=0)
    gain = gain_buf[...].astype(jnp.float32)
    gain = jnp.concatenate([gain[i:i + 1] for i in range(gain.shape[0])], axis=1)
    scaled = (x * gain).astype(jnp.bfloat16)
    squares = jnp.sum(x * x, axis=-1, keepdims=True)
    high = squares.astype(jnp.bfloat16).astype(jnp.float32)
    low = squares - high
    for color in range(colors):
        spread(color, group + 2, jnp.broadcast_to(high, (total_rows, HD)))
        spread(color, group + 3, jnp.broadcast_to(low, (total_rows, HD)))

    def multiply(weights, place_of_head):
        product = jnp.dot(scaled, weights, preferred_element_type=jnp.float32)
        for i in range(product.shape[1] // HD):
            spread(*place_of_head(i), product[:, i * HD:(i + 1) * HD])

    copies[2].wait()
    multiply(wk_buf[...], lambda i: (i, group))
    copies[3].wait()
    multiply(wv_buf[...], lambda i: (i, group + 1))
    for c in range(chunks):
        copies[4 + c].wait()
        first = c * chunk // HD
        multiply(wq_buf[c], lambda i: ((first + i) // group, (first + i) % group))
    keep_ref, send_ref = out_refs
    near = (device >> 1) % 2
    for slot in range(keep_ref.shape[0]):
        for ref, side in ((keep_ref, near), (send_ref, 1 - near)):
            seq = (slot // 2) * 4 + side * 2 + slot % 2
            start = pl.multiple_of(seq * stride, 8)
            ref[slot] = rows_buf[pl.ds(start, stride), :].astype(ref.dtype)


def project(place, mine, other, gain, wq, wk, wv, table, length, steps, group, colors):
    half_rows, depth = mine.shape
    q_cols, kv_cols = wq.shape[1], wk.shape[1]
    seqs = 2 * half_rows // steps
    chunk = 512
    vmem = pl.BlockSpec(memory_space=pltpu.VMEM)
    smem = pl.BlockSpec(memory_space=pltpu.SMEM)
    hbm = pl.BlockSpec(memory_space=pltpu.HBM)
    block = (seqs // 2, colors * steps * (group + 4), HD)
    out_shape = (jax.ShapeDtypeStruct(block, jnp.float32), jax.ShapeDtypeStruct(block, jnp.bfloat16))
    return pl.pallas_call(
        functools.partial(project_kernel, steps, group, colors, chunk),
        out_shape=out_shape,
        in_specs=[smem, hbm, vmem, hbm, hbm, hbm, hbm, pl.BlockSpec(memory_space=pl.ANY), smem],
        out_specs=(vmem,) * len(out_shape),
        scratch_shapes=[
            pltpu.VMEM(mine.shape, jnp.bfloat16),
            pltpu.VMEM(gain.shape, jnp.bfloat16),
            pltpu.VMEM((q_cols // chunk, depth, chunk), jnp.bfloat16),
            pltpu.VMEM((depth, kv_cols), jnp.bfloat16),
            pltpu.VMEM((depth, kv_cols), jnp.bfloat16),
            pltpu.VMEM((seqs * colors * steps * (group + 4), HD), jnp.float32),
            pltpu.SemaphoreType.DMA((q_cols // chunk + 4,)),
        ],
        compiler_params=pltpu.CompilerParams(vmem_limit_bytes=28 * MIB),
        cost_estimate=pl.CostEstimate(
            flops=4 * half_rows * depth * (q_cols + 2 * kv_cols),
            bytes_accessed=2 * depth * (q_cols + 2 * kv_cols), transcendentals=0),
        name="project",
    )(place, in_hbm(mine), other, in_hbm(gain), in_hbm(wq), in_hbm(wk), in_hbm(wv), table, length)


def combine_kernel(keep_ref, came_ref, out_ref):
    out_ref[...] = (keep_ref[...] + came_ref[...].astype(jnp.float32)).astype(jnp.bfloat16)


def fetch_kernel(first, parts, weight_ref, after_ref, held_ref, sems):
    rows = held_ref.shape[0] // parts
    copies = [
        pltpu.make_async_copy(
            weight_ref.at[first + c * rows:first + (c + 1) * rows],
            held_ref.at[c * rows:(c + 1) * rows], sems.at[c])
        for c in range(parts)]
    for copy in copies:
        copy.start()
    for copy in copies:
        copy.wait()


def fetch(weight, first, rows, after):
    parts = 4
    return pl.pallas_call(
        functools.partial(fetch_kernel, first, parts),
        out_shape=pltpu.VMEM((rows, weight.shape[1]), weight.dtype),
        in_specs=[pl.BlockSpec(memory_space=pltpu.HBM), pl.BlockSpec(memory_space=pl.ANY)],
        out_specs=pl.BlockSpec(memory_space=pltpu.VMEM),
        scratch_shapes=[pltpu.SemaphoreType.DMA((parts,))],
        compiler_params=pltpu.CompilerParams(vmem_limit_bytes=16 * MIB),
        cost_estimate=pl.CostEstimate(
            flops=0, bytes_accessed=2 * rows * weight.shape[1], transcendentals=0),
        name="fetch",
    )(in_hbm(weight), after)


def attend_kernel(steps, width, place_ref, length_ref, table_ref, keys_ref, values_ref, parts_ref,
                  same_ref, cross_ref, new_keys_ref, new_values_ref):
    kv_heads = keys_ref.shape[1] // HD
    half_kv = kv_heads // 2
    pitch = parts_ref.shape[1] // (half_kv * steps)
    group = pitch - 4
    halves = [
        functools.reduce(jnp.add, [
            parts_ref[i].astype(jnp.float32) for i in range(g, parts_ref.shape[0], 2)])
        for g in range(2)]
    slots = keys_ref.shape[0]
    factor = 1.0 / math.sqrt(HD)
    low_side = place_ref[0] % 2 == 0
    live = lax.broadcasted_iota(jnp.int32, (steps * group, slots), 1) < length_ref[0]
    row_step = lax.broadcasted_iota(jnp.int32, (steps * group, 1), 0) // group
    fresh_keys = [[None] * kv_heads for _ in range(steps)]
    fresh_values = [[None] * kv_heads for _ in range(steps)]
    queries = [None] * kv_heads
    for k in range(half_kv):
        for g in range(2):
            head = g * half_kv + k
            query = []
            for t in range(steps):
                rows = halves[g][(k * steps + t) * pitch:(k * steps + t + 1) * pitch]
                squares = rows[group + 2:group + 3] + rows[group + 3:group + 4]
                rows = rows * lax.rsqrt(squares / width + epsilon)
                cosine = table_ref[2 * t:2 * t + 1, :]
                sine = table_ref[2 * t + 1:2 * t + 2, :]
                turned = rows * cosine + pltpu.roll(rows, HD // 2, 1) * sine
                query.append(turned[:group])
                fresh_keys[t][head] = turned[group:group + 1].astype(jnp.bfloat16).astype(jnp.float32)
                fresh_values[t][head] = rows[group + 1:group + 2].astype(jnp.bfloat16).astype(jnp.float32)
            queries[head] = jnp.concatenate(query, axis=0).astype(jnp.bfloat16)
    new_keys_ref[...] = jnp.concatenate(
        [jnp.concatenate(row, axis=1) for row in fresh_keys], axis=0).astype(jnp.bfloat16)
    new_values_ref[...] = jnp.concatenate(
        [jnp.concatenate(row, axis=1) for row in fresh_values], axis=0).astype(jnp.bfloat16)
    contexts = []
    for head in range(kv_heads):
        columns = slice(head * HD, (head + 1) * HD)
        query = queries[head]
        scores = lax.dot_general(
            query, keys_ref[:, columns], (((1,), (1,)), ((), ())),
            preferred_element_type=jnp.float32) * factor
        scores = jnp.where(live, scores, -jnp.inf)
        top = jnp.max(scores, axis=-1, keepdims=True)
        wide = query.astype(jnp.float32)
        fresh = []
        for s in range(steps):
            score = jnp.sum(wide * fresh_keys[s][head], axis=-1, keepdims=True) * factor
            score = jnp.where(row_step >= s, score, -jnp.inf)
            fresh.append(score)
            top = jnp.maximum(top, score)
        scores = jnp.exp(scores - top)
        total = jnp.sum(scores, axis=-1, keepdims=True)
        fresh = [jnp.exp(score - top) for score in fresh]
        for score in fresh:
            total = total + score
        weight = (scores / total).astype(jnp.bfloat16)
        mixed = jnp.dot(weight, values_ref[:, columns], preferred_element_type=jnp.float32)
        for s in range(steps):
            weight = (fresh[s] / total).astype(jnp.bfloat16).astype(jnp.float32)
            mixed = mixed + weight * fresh_values[s][head]
        contexts.append(mixed)
    for k in range(half_kv):
        lower, upper = contexts[k], contexts[half_kv + k]
        span = slice(k * steps * group, (k + 1) * steps * group)
        same_ref[span, :] = jnp.where(low_side, lower, upper).astype(jnp.bfloat16)
        cross_ref[span, :] = jnp.where(low_side, upper, lower).astype(jnp.bfloat16)


def attend(place, length, parts, table, keys, values, steps, width, half_heads):
    vmem = pl.BlockSpec(memory_space=pltpu.VMEM)
    smem = pl.BlockSpec(memory_space=pltpu.SMEM)
    kv_cols = keys.shape[1]
    half = jax.ShapeDtypeStruct((steps * half_heads, HD), jnp.bfloat16)
    fresh = jax.ShapeDtypeStruct((steps, kv_cols), jnp.bfloat16)
    return pl.pallas_call(
        functools.partial(attend_kernel, steps, width),
        out_shape=(half, half, fresh, fresh),
        in_specs=[smem, smem] + [vmem] * 4,
        out_specs=(vmem,) * 4,
        compiler_params=pltpu.CompilerParams(vmem_limit_bytes=16 * MIB),
        name="attend",
    )(place, length, table, keys, values, parts)


def pack_kernel(same_ref, other_ref, out_ref):
    out_ref[0] = same_ref[...]
    out_ref[1] = other_ref[...]


def join_kernel(first_ref, second_ref, *rest):
    out_ref = rest[-1]
    count = first_ref.shape[0]
    out_ref[:count] = first_ref[...]
    out_ref[count:] = second_ref[...]


def local_call(kernel, shape, arrays, held=()):
    vmem = pl.BlockSpec(memory_space=pltpu.VMEM)
    return pl.pallas_call(
        kernel,
        out_shape=jax.ShapeDtypeStruct(shape, jnp.bfloat16),
        in_specs=[vmem] * len(arrays) + [pl.BlockSpec(memory_space=pl.ANY)] * len(held),
        out_specs=vmem,
        compiler_params=pltpu.CompilerParams(vmem_limit_bytes=16 * MIB),
        name="local",
    )(*arrays, *[in_vmem(piece) for piece in held])


def output_kernel(steps, colors, patterns, pieces, place_ref, *rest):
    weight_refs, (held_ref, came_ref, mine_ref, other_ref, wide_buf, rows_buf) = rest[:pieces], rest[pieces:]
    device = place_ref[0]
    devices = len(patterns)
    half_seqs = devices // 2
    count, block, _ = held_ref.shape
    group = block // (steps * colors)
    for j, pattern in enumerate(patterns):
        rows = held_ref[j] if j < count else came_ref[j - count]
        start = pl.multiple_of((device ^ pattern) * block, 8)
        wide_buf[pl.ds(start, block), :] = rows.astype(jnp.float32)
    for head in range(colors * group):
        color, h = head // group, head % group
        lines = []
        for g in range(2):
            for t in range(steps):
                start = g * half_seqs * block + (color * steps + t) * group + h
                lines.append(wide_buf[pl.ds(start, half_seqs, stride=block), :])
        rows_buf[:, head * HD:(head + 1) * HD] = jnp.concatenate(lines, axis=0).astype(jnp.bfloat16)
    low_side = device % 2 == 0
    half = rows_buf.shape[0] // 2
    columns = mine_ref.shape[1]
    chunk = min(columns, 512)
    for c in range(columns // chunk):
        span = slice(c * chunk, (c + 1) * chunk)
        product, first = None, 0
        for weight_ref in weight_refs:
            last = first + weight_ref.shape[0]
            part = jnp.dot(rows_buf[:, first:last], weight_ref[:, span], preferred_element_type=jnp.float32)
            product = part if product is None else product + part
            first = last
        lower, upper = product[:half], product[half:]
        mine_ref[:, span] = jnp.where(low_side, lower, upper)
        other_ref[:, span] = jnp.where(low_side, upper, lower).astype(jnp.bfloat16)


def output(place, held_context, came_context, patterns, held, steps, colors):
    columns = held[0].shape[1]
    depth = sum(piece.shape[0] for piece in held)
    devices = len(patterns)
    half = devices * steps // 2
    vmem = pl.BlockSpec(memory_space=pltpu.VMEM)
    smem = pl.BlockSpec(memory_space=pltpu.SMEM)
    return pl.pallas_call(
        functools.partial(output_kernel, steps, colors, patterns, len(held)),
        out_shape=(
            jax.ShapeDtypeStruct((half, columns), jnp.float32),
            jax.ShapeDtypeStruct((half, columns), jnp.bfloat16),
        ),
        in_specs=[smem] + [vmem] * (len(held) + 2),
        out_specs=(vmem, vmem),
        scratch_shapes=[
            pltpu.VMEM((devices * held_context.shape[1], HD), jnp.float32),
            pltpu.VMEM((devices * steps, depth), jnp.bfloat16),
        ],
        compiler_params=pltpu.CompilerParams(vmem_limit_bytes=26 * MIB),
        cost_estimate=pl.CostEstimate(
            flops=2 * devices * steps * depth * columns,
            bytes_accessed=2 * depth * columns, transcendentals=0),
        name="output",
    )(place, *[in_vmem(piece) for piece in held], held_context, came_context)


def body(hidden_in, norm_gain, query_weight, key_weight, value_weight, out_weight,
         cache_keys, cache_values, lengths, positions):
    steps, half_seqs, depth = hidden_in.shape
    everyone = ("far", "near", "gy")
    devices = lax.axis_size(everyone)
    bits = devices.bit_length() - 1
    colors = key_weight.shape[1] // HD
    half_heads = query_weight.shape[1] // HD
    group = half_heads // colors
    place = lax.axis_index(everyone).astype(jnp.int32).reshape(1)
    table = rope_table(positions[0], steps)

    def partner(array, bit):
        return lax.ppermute(array, everyone, [(i, i ^ (1 << bit)) for i in range(devices)])

    mine = hidden_in.reshape(steps * half_seqs, depth)
    other = partner(mine, 0)
    keep, send = project(place, mine, other, norm_gain.reshape(-1, HD), query_weight, key_weight,
                         value_weight, table, lengths, steps, group, colors)
    parts = local_call(combine_kernel, keep.shape, [keep, partner(send, 1)])
    parts = lax.all_to_all(parts, ("far", "gy"), split_axis=0, concat_axis=0, tiled=True)
    same, cross, new_keys, new_values = attend(
        place, lengths, parts, table, cache_keys[0], cache_values[0],
        steps, depth * devices // 2, half_heads)

    context = local_call(pack_kernel, (2,) + same.shape, [same, partner(cross, 0)])
    patterns = [0, 1]
    order = list(range(bits - 1, 0, -1))
    total = out_weight.shape[0]
    cuts = [total * i // 8 for i in (0, 2, 5, 8)]
    held = []
    for i, bit in enumerate(order):
        came = partner(context, bit)
        patterns = patterns + [p ^ (1 << bit) for p in patterns]
        now = []
        if i < len(cuts) - 1:
            now.append(fetch(out_weight, cuts[i], cuts[i + 1] - cuts[i], context))
            held += now
        if i < len(order) - 1:
            shape = (2 * context.shape[0],) + context.shape[1:]
            context = local_call(join_kernel, shape, [context, came], now)
    mine, other = output(place, context, came, patterns, held, steps, colors)
    other = partner(other, 0)
    result = (mine + other.astype(jnp.float32)).astype(jnp.bfloat16)
    return (
        result.reshape(steps, half_seqs, -1),
        new_keys[:, None, :],
        new_values[:, None, :],
    )


def solution(mesh):
    rep, gx, gy = mesh.devices.shape
    split = jax.sharding.Mesh(mesh.devices.reshape(rep, gx // 2, 2, gy), ("rep", "far", "near", "gy"))
    gx = ("far", "near")
    in_specs = (
        P(None, ("rep", "gy"), gx),
        P(gx),
        P(gx, "gy"),
        P(gx, "gy"),
        P(gx, "gy"),
        P("gy", gx),
        P(("rep", *gx, "gy"), None, None),
        P(("rep", *gx, "gy"), None, None),
        P(("rep", *gx, "gy")),
        P(("rep", *gx, "gy")),
    )
    out_specs = (
        P(None, ("rep", "gy"), gx),
        P(None, ("rep", *gx, "gy"), None),
        P(None, ("rep", *gx, "gy"), None),
    )
    return jax.shard_map(body, mesh=split, in_specs=in_specs, out_specs=out_specs, check_vma=False)
```

```python
import functools
import math

import jax
import jax.numpy as jnp
from jax import lax
from jax.experimental import pallas as pl
from jax.experimental.pallas import tpu as pltpu
from jax.sharding import PartitionSpec as P

HD = 128
epsilon = 1e-05
rope_theta = 500000.0
MIB = 1024 * 1024


def rope_frequencies(index, head_size):
    frequency = jnp.exp(-math.log(rope_theta) * 2.0 * index / head_size)
    wavelength = 2.0 * math.pi / frequency
    smooth = (8192.0 / wavelength - 1.0) / 3.0
    blended = (1.0 - smooth) * frequency / 8.0 + smooth * frequency
    adjusted = jnp.where(wavelength > 8192.0, frequency / 8.0, blended)
    return jnp.where(wavelength < 2048.0, frequency, adjusted)


def slot_patterns(order):
    count = len(order)
    return [
        sum(((j >> (count - 1 - i)) & 1) << bit for i, bit in enumerate(order))
        for j in range(1 << count)]


def in_hbm(array):
    return pltpu.with_memory_space_constraint(array, pltpu.HBM)


def in_vmem(array):
    return pltpu.with_memory_space_constraint(array, pltpu.VMEM)


def project_kernel(steps, group, colors, order, chunk, place_ref, mine_ref, other_ref, gain_ref, early_ref, wk_ref, wv_ref,
                   wq_ref, position_ref, length_ref, notes_ref, *rest):
    part_refs, rest = rest[:-7], rest[-7:]
    mine_buf, gain_buf, wq_buf, rows_buf, position_buf, length_buf, sems = rest
    early = early_ref.shape[1]
    q_cols = wq_ref.shape[1]
    chunks = (q_cols - early) // chunk
    copies = [pltpu.make_async_copy(mine_ref, mine_buf, sems.at[chunks]),
              pltpu.make_async_copy(gain_ref, gain_buf, sems.at[chunks + 1]),
              pltpu.make_async_copy(position_ref, position_buf, sems.at[chunks + 2]),
              pltpu.make_async_copy(length_ref, length_buf, sems.at[chunks + 3])]
    for c in range(chunks):
        copies.append(pltpu.make_async_copy(
            wq_ref.at[:, early + c * chunk:early + (c + 1) * chunk], wq_buf.at[c], sems.at[c]))
    for copy in copies:
        copy.start()

    device = place_ref[0]
    half_rows = mine_ref.shape[0]
    total_rows = 2 * half_rows
    half_seqs = half_rows // steps
    pitch = group + 4
    stride = colors * steps * pitch

    def spread(color, row, block):
        for g in range(2):
            for t in range(steps):
                first = (g * steps + t) * half_seqs
                start = g * half_seqs * stride + (color * steps + t) * pitch + row
                rows_buf[pl.ds(start, half_seqs, stride=stride), :] = block[first:first + half_seqs, :]

    low_side = device % 2 == 0
    copies[0].wait()
    copies[1].wait()
    mine = mine_buf[...].astype(jnp.float32)
    other = other_ref[...].astype(jnp.float32)
    x = jnp.concatenate(
        [jnp.where(low_side, mine, other), jnp.where(low_side, other, mine)], axis=0)
    gain = gain_buf[...].astype(jnp.float32)
    gain = jnp.concatenate([gain[i:i + 1] for i in range(gain.shape[0])], axis=1)
    scaled = (x * gain).astype(jnp.bfloat16)
    squares = jnp.sum(x * x, axis=-1, keepdims=True)
    high = squares.astype(jnp.bfloat16).astype(jnp.float32)
    low = squares - high
    for color in range(colors):
        spread(color, group + 2, jnp.broadcast_to(high, (total_rows, HD)))
        spread(color, group + 3, jnp.broadcast_to(low, (total_rows, HD)))

    def multiply(weights, place_of_head):
        product = jnp.dot(scaled, weights, preferred_element_type=jnp.float32)
        for i in range(product.shape[1] // HD):
            spread(*place_of_head(i), product[:, i * HD:(i + 1) * HD])

    multiply(wk_ref[...], lambda i: (i, group))
    multiply(wv_ref[...], lambda i: (i, group + 1))
    multiply(early_ref[...], lambda i: (i // group, i % group))

    copies[2].wait()
    copies[3].wait()
    lane = lax.broadcasted_iota(jnp.int32, (1, HD), 1)
    frequency = rope_frequencies((lane % (HD // 2)).astype(jnp.float32), HD)
    sign = jnp.where(lane < HD // 2, -1.0, 1.0)
    for t in range(steps):
        angle = (position_buf[...] + t).astype(jnp.float32) * frequency
        notes_ref[2 * t:2 * t + 1, :] = jnp.cos(angle)
        notes_ref[2 * t + 1:2 * t + 2, :] = jnp.sin(angle) * sign
    notes_ref[2 * steps:2 * steps + 1, :] = jnp.broadcast_to(length_buf[...].astype(jnp.float32), (1, HD))

    for c in range(chunks):
        copies[4 + c].wait()
        first = (early + c * chunk) // HD
        multiply(wq_buf[c], lambda i: ((first + i) // group, (first + i) % group))
    per_part = part_refs[0].shape[0]
    for slot, pattern in enumerate(slot_patterns(order)):
        ref = part_refs[slot // per_part]
        start = pl.multiple_of((device ^ pattern) * stride, 8)
        ref[slot % per_part] = rows_buf[pl.ds(start, stride), :].astype(ref.dtype)


def part_shapes(total, count, block):
    shape = (total // count,) + block
    return (jax.ShapeDtypeStruct(shape, jnp.float32),) + (jax.ShapeDtypeStruct(shape, jnp.bfloat16),) * (count - 1)


def project(place, mine, other, gain, early, wk, wv, wq, position, length, steps, group, colors, order, count):
    half_rows, depth = mine.shape
    q_cols, kv_cols = wq.shape[1], wk.shape[1]
    seqs = 2 * half_rows // steps
    chunk = 512
    chunks = (q_cols - early.shape[1]) // chunk
    vmem = pl.BlockSpec(memory_space=pltpu.VMEM)
    smem = pl.BlockSpec(memory_space=pltpu.SMEM)
    hbm = pl.BlockSpec(memory_space=pltpu.HBM)
    any_space = pl.BlockSpec(memory_space=pl.ANY)
    out_shape = (jax.ShapeDtypeStruct((2 * steps + 4, HD), jnp.float32),) + part_shapes(
        seqs, count, (colors * steps * (group + 4), HD))
    return pl.pallas_call(
        functools.partial(project_kernel, steps, group, colors, order, chunk),
        out_shape=out_shape,
        in_specs=[smem, hbm, vmem, hbm, vmem, vmem, vmem, hbm, any_space, any_space],
        out_specs=(vmem,) * len(out_shape),
        scratch_shapes=[
            pltpu.VMEM(mine.shape, jnp.bfloat16),
            pltpu.VMEM(gain.shape, jnp.bfloat16),
            pltpu.VMEM((chunks, depth, chunk), jnp.bfloat16),
            pltpu.VMEM((seqs * colors * steps * (group + 4), HD), jnp.float32),
            pltpu.VMEM((1, 1), jnp.int32),
            pltpu.VMEM((1, 1), jnp.int32),
            pltpu.SemaphoreType.DMA((chunks + 4,)),
        ],
        compiler_params=pltpu.CompilerParams(vmem_limit_bytes=28 * MIB),
        cost_estimate=pl.CostEstimate(
            flops=4 * half_rows * depth * (q_cols + 2 * kv_cols),
            bytes_accessed=2 * depth * (q_cols + 2 * kv_cols), transcendentals=0),
        name="project",
    )(place, in_hbm(mine), other, in_hbm(gain), in_vmem(early), in_vmem(wk), in_vmem(wv), in_hbm(wq),
      position, length)


def fetch_first_kernel(wq_ref, wk_ref, wv_ref, early_ref, wk_out, wv_out, sems):
    copies = [
        pltpu.make_async_copy(wk_ref, wk_out, sems.at[0]),
        pltpu.make_async_copy(wv_ref, wv_out, sems.at[1]),
        pltpu.make_async_copy(wq_ref.at[:, :early_ref.shape[1]], early_ref, sems.at[2])]
    for copy in copies:
        copy.start()
    for copy in copies:
        copy.wait()


def fetch_first(wq, wk, wv, early):
    hbm = pl.BlockSpec(memory_space=pltpu.HBM)
    vmem = pl.BlockSpec(memory_space=pltpu.VMEM)
    depth = wq.shape[0]
    return pl.pallas_call(
        fetch_first_kernel,
        out_shape=(
            pltpu.VMEM((depth, early), wq.dtype), pltpu.VMEM(wk.shape, wk.dtype), pltpu.VMEM(wv.shape, wv.dtype)),
        in_specs=[hbm] * 3,
        out_specs=(vmem,) * 3,
        scratch_shapes=[pltpu.SemaphoreType.DMA((3,))],
        compiler_params=pltpu.CompilerParams(vmem_limit_bytes=16 * MIB),
        cost_estimate=pl.CostEstimate(
            flops=0, bytes_accessed=2 * depth * (early + 2 * wk.shape[1]), transcendentals=0),
        name="fetch_first",
    )(in_hbm(wq), in_hbm(wk), in_hbm(wv))


def combine_kernel(arrived, parts, *refs):
    total = refs[0][...]
    for ref in refs[1:arrived + 1]:
        total = total + ref[...].astype(jnp.float32)
    count = total.shape[0] // parts
    for i, ref in enumerate(refs[-parts:]):
        ref[...] = total[i * count:(i + 1) * count].astype(ref.dtype)


def combine(keep, came, held, parts):
    vmem = pl.BlockSpec(memory_space=pltpu.VMEM)
    out_shape = part_shapes(keep.shape[0], parts, keep.shape[1:])
    return pl.pallas_call(
        functools.partial(combine_kernel, len(came), parts),
        out_shape=out_shape,
        in_specs=[vmem] * (1 + len(came)) + [pl.BlockSpec(memory_space=pl.ANY)] * len(held),
        out_specs=(vmem,) * parts,
        compiler_params=pltpu.CompilerParams(vmem_limit_bytes=24 * MIB),
        name="combine",
    )(keep, *came, *[in_vmem(piece) for piece in held])


def fetch_kernel(first, parts, weight_ref, after_ref, held_ref, sems):
    rows = held_ref.shape[0] // parts
    copies = [
        pltpu.make_async_copy(
            weight_ref.at[first + c * rows:first + (c + 1) * rows],
            held_ref.at[c * rows:(c + 1) * rows], sems.at[c])
        for c in range(parts)]
    for copy in copies:
        copy.start()
    for copy in copies:
        copy.wait()


def fetch(weight, first, rows, after):
    parts = 4
    return pl.pallas_call(
        functools.partial(fetch_kernel, first, parts),
        out_shape=pltpu.VMEM((rows, weight.shape[1]), weight.dtype),
        in_specs=[pl.BlockSpec(memory_space=pltpu.HBM), pl.BlockSpec(memory_space=pl.ANY)],
        out_specs=pl.BlockSpec(memory_space=pltpu.VMEM),
        scratch_shapes=[pltpu.SemaphoreType.DMA((parts,))],
        compiler_params=pltpu.CompilerParams(vmem_limit_bytes=16 * MIB),
        cost_estimate=pl.CostEstimate(
            flops=0, bytes_accessed=2 * rows * weight.shape[1], transcendentals=0),
        name="fetch",
    )(in_hbm(weight), after)


def attend_kernel(steps, width, place_ref, table_ref, keys_ref, values_ref, same_in_ref, cross_in_ref,
                  same_ref, cross_ref, new_keys_ref, new_values_ref):
    kv_heads = keys_ref.shape[1] // HD
    half_kv = kv_heads // 2
    pitch = same_in_ref.shape[1] // (half_kv * steps)
    group = pitch - 4
    slots = keys_ref.shape[0]
    factor = 1.0 / math.sqrt(HD)
    low_side = place_ref[0] % 2 == 0
    same, cross = same_in_ref[0], cross_in_ref[0].astype(jnp.float32)
    halves = [jnp.where(low_side, same, cross), jnp.where(low_side, cross, same)]
    live = lax.broadcasted_iota(jnp.int32, (steps * group, slots), 1) < (
        table_ref[2 * steps:2 * steps + 1, :1].astype(jnp.int32))
    row_step = lax.broadcasted_iota(jnp.int32, (steps * group, 1), 0) // group
    fresh_keys = [[None] * kv_heads for _ in range(steps)]
    fresh_values = [[None] * kv_heads for _ in range(steps)]
    queries = [None] * kv_heads
    for k in range(half_kv):
        for g in range(2):
            head = g * half_kv + k
            query = []
            for t in range(steps):
                rows = halves[g][(k * steps + t) * pitch:(k * steps + t + 1) * pitch]
                squares = rows[group + 2:group + 3] + rows[group + 3:group + 4]
                rows = rows * lax.rsqrt(squares / width + epsilon)
                cosine = table_ref[2 * t:2 * t + 1, :]
                sine = table_ref[2 * t + 1:2 * t + 2, :]
                turned = rows * cosine + pltpu.roll(rows, HD // 2, 1) * sine
                query.append(turned[:group])
                fresh_keys[t][head] = turned[group:group + 1].astype(jnp.bfloat16).astype(jnp.float32)
                fresh_values[t][head] = rows[group + 1:group + 2].astype(jnp.bfloat16).astype(jnp.float32)
            queries[head] = jnp.concatenate(query, axis=0).astype(jnp.bfloat16)
    new_keys_ref[...] = jnp.concatenate(
        [jnp.concatenate(row, axis=1) for row in fresh_keys], axis=0).astype(jnp.bfloat16)
    new_values_ref[...] = jnp.concatenate(
        [jnp.concatenate(row, axis=1) for row in fresh_values], axis=0).astype(jnp.bfloat16)
    contexts = []
    for head in range(kv_heads):
        columns = slice(head * HD, (head + 1) * HD)
        query = queries[head]
        scores = lax.dot_general(
            query, keys_ref[:, columns], (((1,), (1,)), ((), ())),
            preferred_element_type=jnp.float32) * factor
        scores = jnp.where(live, scores, -jnp.inf)
        top = jnp.max(scores, axis=-1, keepdims=True)
        wide = query.astype(jnp.float32)
        fresh = []
        for s in range(steps):
            score = jnp.sum(wide * fresh_keys[s][head], axis=-1, keepdims=True) * factor
            score = jnp.where(row_step >= s, score, -jnp.inf)
            fresh.append(score)
            top = jnp.maximum(top, score)
        scores = jnp.exp(scores - top)
        total = jnp.sum(scores, axis=-1, keepdims=True)
        fresh = [jnp.exp(score - top) for score in fresh]
        for score in fresh:
            total = total + score
        weight = (scores / total).astype(jnp.bfloat16)
        mixed = jnp.dot(weight, values_ref[:, columns], preferred_element_type=jnp.float32)
        for s in range(steps):
            weight = (fresh[s] / total).astype(jnp.bfloat16).astype(jnp.float32)
            mixed = mixed + weight * fresh_values[s][head]
        contexts.append(mixed)
    for k in range(half_kv):
        lower, upper = contexts[k], contexts[half_kv + k]
        span = slice(k * steps * group, (k + 1) * steps * group)
        same_ref[span, :] = jnp.where(low_side, lower, upper).astype(jnp.bfloat16)
        cross_ref[span, :] = jnp.where(low_side, upper, lower).astype(jnp.bfloat16)


def attend(place, same, cross, table, keys, values, steps, width, half_heads):
    vmem = pl.BlockSpec(memory_space=pltpu.VMEM)
    smem = pl.BlockSpec(memory_space=pltpu.SMEM)
    kv_cols = keys.shape[1]
    half = jax.ShapeDtypeStruct((steps * half_heads, HD), jnp.bfloat16)
    fresh = jax.ShapeDtypeStruct((steps, kv_cols), jnp.bfloat16)
    return pl.pallas_call(
        functools.partial(attend_kernel, steps, width),
        out_shape=(half, half, fresh, fresh),
        in_specs=[smem] + [vmem] * 5,
        out_specs=(vmem,) * 4,
        compiler_params=pltpu.CompilerParams(vmem_limit_bytes=16 * MIB),
        name="attend",
    )(place, table, keys, values, same, cross)


def pack_kernel(same_ref, other_ref, out_ref):
    out_ref[0] = same_ref[...]
    out_ref[1] = other_ref[...]


def join_kernel(arrived, *refs):
    out_ref = refs[-1]
    for i, ref in enumerate(refs[:arrived + 1]):
        count = ref.shape[0]
        out_ref[i * count:(i + 1) * count] = ref[...]


def local_call(kernel, shape, arrays, held=()):
    vmem = pl.BlockSpec(memory_space=pltpu.VMEM)
    return pl.pallas_call(
        kernel,
        out_shape=jax.ShapeDtypeStruct(shape, jnp.bfloat16),
        in_specs=[vmem] * len(arrays) + [pl.BlockSpec(memory_space=pl.ANY)] * len(held),
        out_specs=vmem,
        compiler_params=pltpu.CompilerParams(vmem_limit_bytes=16 * MIB),
        name="local",
    )(*arrays, *[in_vmem(piece) for piece in held])


def output_kernel(steps, colors, patterns, pieces, place_ref, *rest):
    weight_refs, context_refs = rest[:pieces], rest[pieces:-4]
    mine_ref, other_ref, wide_buf, rows_buf = rest[-4:]
    device = place_ref[0]
    devices = len(patterns)
    half_seqs = devices // 2
    count, block, _ = context_refs[0].shape
    group = block // (steps * colors)
    for j, pattern in enumerate(patterns):
        rows = context_refs[j // count][j % count]
        start = pl.multiple_of((device ^ pattern) * block, 8)
        wide_buf[pl.ds(start, block), :] = rows.astype(jnp.float32)
    for head in range(colors * group):
        color, h = head // group, head % group
        lines = []
        for g in range(2):
            for t in range(steps):
                start = g * half_seqs * block + (color * steps + t) * group + h
                lines.append(wide_buf[pl.ds(start, half_seqs, stride=block), :])
        rows_buf[:, head * HD:(head + 1) * HD] = jnp.concatenate(lines, axis=0).astype(jnp.bfloat16)
    low_side = device % 2 == 0
    half = rows_buf.shape[0] // 2
    columns = mine_ref.shape[1]
    chunk = min(columns, 512)
    for c in range(columns // chunk):
        span = slice(c * chunk, (c + 1) * chunk)
        product, first = None, 0
        for weight_ref in weight_refs:
            last = first + weight_ref.shape[0]
            part = jnp.dot(rows_buf[:, first:last], weight_ref[:, span], preferred_element_type=jnp.float32)
            product = part if product is None else product + part
            first = last
        lower, upper = product[:half], product[half:]
        mine_ref[:, span] = jnp.where(low_side, lower, upper)
        other_ref[:, span] = jnp.where(low_side, upper, lower).astype(jnp.bfloat16)


def output(place, contexts, patterns, held, steps, colors):
    columns = held[0].shape[1]
    depth = sum(piece.shape[0] for piece in held)
    devices = len(patterns)
    half = devices * steps // 2
    vmem = pl.BlockSpec(memory_space=pltpu.VMEM)
    smem = pl.BlockSpec(memory_space=pltpu.SMEM)
    return pl.pallas_call(
        functools.partial(output_kernel, steps, colors, patterns, len(held)),
        out_shape=(
            jax.ShapeDtypeStruct((half, columns), jnp.float32),
            jax.ShapeDtypeStruct((half, columns), jnp.bfloat16),
        ),
        in_specs=[smem] + [vmem] * (len(held) + len(contexts)),
        out_specs=(vmem, vmem),
        scratch_shapes=[
            pltpu.VMEM((devices * contexts[0].shape[1], HD), jnp.float32),
            pltpu.VMEM((devices * steps, depth), jnp.bfloat16),
        ],
        compiler_params=pltpu.CompilerParams(vmem_limit_bytes=26 * MIB),
        cost_estimate=pl.CostEstimate(
            flops=2 * devices * steps * depth * columns,
            bytes_accessed=2 * depth * columns, transcendentals=0),
        name="output",
    )(place, *[in_vmem(piece) for piece in held], *contexts)


def body(hidden_in, norm_gain, query_weight, key_weight, value_weight, out_weight,
         cache_keys, cache_values, lengths, positions):
    steps, half_seqs, depth = hidden_in.shape
    everyone = ("gx", "gy")
    devices = lax.axis_size(everyone)
    bits = devices.bit_length() - 1
    colors = key_weight.shape[1] // HD
    half_heads = query_weight.shape[1] // HD
    group = half_heads // colors
    place = lax.axis_index(everyone).astype(jnp.int32).reshape(1)

    def partner(array, pattern):
        return lax.ppermute(array, everyone, [(i, i ^ pattern) for i in range(devices)])

    near_first = [list(range(first, min(first + 2, bits))) for first in range(1, bits, 2)]
    stages = near_first + [[0]]
    order = [bit for stage in stages for bit in stage]
    total = out_weight.shape[0]
    cuts = [total * i // 4 for i in range(5)]
    held = []

    def fetch_next(after):
        i = len(held)
        if i == 4:
            return []
        held.append(fetch(out_weight, cuts[i], cuts[i + 1] - cuts[i], after))
        return held[-1:]

    mine = hidden_in.reshape(steps * half_seqs, depth)
    other = partner(mine, 1)
    early, wk, wv = fetch_first(query_weight, key_weight, value_weight, 512)
    notes, *parts = project(
        place, mine, other, norm_gain.reshape(-1, HD), early, wk, wv, query_weight, positions[:, None], lengths[:, None],
        steps, group, colors, order, 1 << len(stages[0]))
    for i, stage in enumerate(stages[:-1]):
        came = [partner(part, pattern) for part, pattern in zip(parts[1:], slot_patterns(stage)[1:])]
        now = fetch_next(parts[1]) if i < 2 else []
        parts = combine(parts[0], came, now, 1 << len(stages[i + 1]))
    same, cross, new_keys, new_values = attend(
        place, parts[0], partner(parts[1], 1), notes, cache_keys[0], cache_values[0],
        steps, depth * lax.axis_size("gx"), half_heads)

    context = local_call(pack_kernel, (2,) + same.shape, [same, partner(cross, 1)])
    patterns = [0, 1]
    for i, stage in enumerate(near_first[::-1]):
        moves = slot_patterns(stage)
        came = [partner(context, move) for move in moves[1:]]
        patterns = [p ^ move for move in moves for p in patterns]
        now = fetch_next(context)
        if i < len(near_first) - 1:
            shape = (len(moves) * context.shape[0],) + context.shape[1:]
            context = local_call(functools.partial(join_kernel, len(came)), shape, [context, *came], now)
    mine, other = output(place, [context, *came], patterns, held, steps, colors)
    other = partner(other, 1)
    result = (mine + other.astype(jnp.float32)).astype(jnp.bfloat16)
    return (
        result.reshape(steps, half_seqs, -1),
        new_keys[:, None, :],
        new_values[:, None, :],
    )


def solution(mesh):
    in_specs = (
        P(None, ("rep", "gy"), "gx"),
        P("gx"),
        P("gx", "gy"),
        P("gx", "gy"),
        P("gx", "gy"),
        P("gy", "gx"),
        P(("rep", "gx", "gy"), None, None),
        P(("rep", "gx", "gy"), None, None),
        P(("rep", "gx", "gy")),
        P(("rep", "gx", "gy")),
    )
    out_specs = (
        P(None, ("rep", "gy"), "gx"),
        P(None, ("rep", "gx", "gy"), None),
        P(None, ("rep", "gx", "gy"), None),
    )
    return jax.shard_map(body, mesh=mesh, in_specs=in_specs, out_specs=out_specs, check_vma=False)
```

```python
import functools
import math

import jax
import jax.numpy as jnp
from jax import lax
from jax.experimental import pallas as pl
from jax.experimental.pallas import tpu as pltpu
from jax.sharding import PartitionSpec as P

HD = 128
epsilon = 1e-05
rope_theta = 500000.0
MIB = 1024 * 1024


def rope_frequencies(index, head_size):
    frequency = jnp.exp(-math.log(rope_theta) * 2.0 * index / head_size)
    wavelength = 2.0 * math.pi / frequency
    smooth = (8192.0 / wavelength - 1.0) / 3.0
    blended = (1.0 - smooth) * frequency / 8.0 + smooth * frequency
    adjusted = jnp.where(wavelength > 8192.0, frequency / 8.0, blended)
    return jnp.where(wavelength < 2048.0, frequency, adjusted)


def slot_patterns(order):
    count = len(order)
    return [
        sum(((j >> (count - 1 - i)) & 1) << bit for i, bit in enumerate(order))
        for j in range(1 << count)]


def in_hbm(array):
    return pltpu.with_memory_space_constraint(array, pltpu.HBM)


def in_vmem(array):
    return pltpu.with_memory_space_constraint(array, pltpu.VMEM)


def project_kernel(steps, group, colors, order, chunk, place_ref, mine_ref, other_ref, gain_ref, early_ref, wk_ref, wv_ref,
                   wq_ref, *rest):
    part_refs, rest = rest[:-5], rest[-5:]
    mine_buf, gain_buf, wq_buf, rows_buf, sems = rest
    early = early_ref.shape[1]
    q_cols = wq_ref.shape[1]
    chunks = (q_cols - early) // chunk
    copies = [pltpu.make_async_copy(mine_ref, mine_buf, sems.at[chunks]),
              pltpu.make_async_copy(gain_ref, gain_buf, sems.at[chunks + 1])]
    for c in range(chunks):
        copies.append(pltpu.make_async_copy(
            wq_ref.at[:, early + c * chunk:early + (c + 1) * chunk], wq_buf.at[c], sems.at[c]))
    for copy in copies:
        copy.start()

    device = place_ref[0]
    half_rows = mine_ref.shape[0]
    total_rows = 2 * half_rows
    half_seqs = half_rows // steps
    pitch = group + 4
    stride = colors * steps * pitch

    def spread(color, row, block):
        for g in range(2):
            for t in range(steps):
                first = (g * steps + t) * half_seqs
                start = g * half_seqs * stride + (color * steps + t) * pitch + row
                rows_buf[pl.ds(start, half_seqs, stride=stride), :] = block[first:first + half_seqs, :]

    low_side = device % 2 == 0
    copies[0].wait()
    copies[1].wait()
    mine = mine_buf[...].astype(jnp.float32)
    other = other_ref[...].astype(jnp.float32)
    x = jnp.concatenate(
        [jnp.where(low_side, mine, other), jnp.where(low_side, other, mine)], axis=0)
    gain = gain_buf[...].astype(jnp.float32)
    gain = jnp.concatenate([gain[i:i + 1] for i in range(gain.shape[0])], axis=1)
    scaled = (x * gain).astype(jnp.bfloat16)
    squares = jnp.sum(x * x, axis=-1, keepdims=True)
    high = squares.astype(jnp.bfloat16).astype(jnp.float32)
    low = squares - high
    for color in range(colors):
        spread(color, group + 2, jnp.broadcast_to(high, (total_rows, HD)))
        spread(color, group + 3, jnp.broadcast_to(low, (total_rows, HD)))

    def multiply(weights, place_of_head):
        product = jnp.dot(scaled, weights, preferred_element_type=jnp.float32)
        for i in range(product.shape[1] // HD):
            spread(*place_of_head(i), product[:, i * HD:(i + 1) * HD])

    multiply(wk_ref[...], lambda i: (i, group))
    multiply(wv_ref[...], lambda i: (i, group + 1))
    multiply(early_ref[...], lambda i: (i // group, i % group))

    for c in range(chunks):
        copies[2 + c].wait()
        first = (early + c * chunk) // HD
        multiply(wq_buf[c], lambda i: ((first + i) // group, (first + i) % group))
    per_part = part_refs[0].shape[0]
    for slot, pattern in enumerate(slot_patterns(order)):
        ref = part_refs[slot // per_part]
        start = pl.multiple_of((device ^ pattern) * stride, 8)
        ref[slot % per_part] = rows_buf[pl.ds(start, stride), :].astype(ref.dtype)


def part_shapes(total, count, block):
    shape = (total // count,) + block
    return (jax.ShapeDtypeStruct(shape, jnp.float32),) + (jax.ShapeDtypeStruct(shape, jnp.bfloat16),) * (count - 1)


def project(place, mine, other, gain, early, wk, wv, wq, steps, group, colors, order, count):
    half_rows, depth = mine.shape
    q_cols, kv_cols = wq.shape[1], wk.shape[1]
    seqs = 2 * half_rows // steps
    chunk = 512
    chunks = (q_cols - early.shape[1]) // chunk
    vmem = pl.BlockSpec(memory_space=pltpu.VMEM)
    smem = pl.BlockSpec(memory_space=pltpu.SMEM)
    hbm = pl.BlockSpec(memory_space=pltpu.HBM)
    out_shape = part_shapes(
        seqs, count, (colors * steps * (group + 4), HD))
    return pl.pallas_call(
        functools.partial(project_kernel, steps, group, colors, order, chunk),
        out_shape=out_shape,
        in_specs=[smem, hbm, vmem, hbm, vmem, vmem, vmem, hbm],
        out_specs=(vmem,) * len(out_shape),
        scratch_shapes=[
            pltpu.VMEM(mine.shape, jnp.bfloat16),
            pltpu.VMEM(gain.shape, jnp.bfloat16),
            pltpu.VMEM((chunks, depth, chunk), jnp.bfloat16),
            pltpu.VMEM((seqs * colors * steps * (group + 4), HD), jnp.float32),
            pltpu.SemaphoreType.DMA((chunks + 2,)),
        ],
        compiler_params=pltpu.CompilerParams(vmem_limit_bytes=28 * MIB),
        cost_estimate=pl.CostEstimate(
            flops=4 * half_rows * depth * (q_cols + 2 * kv_cols),
            bytes_accessed=2 * depth * (q_cols + 2 * kv_cols), transcendentals=0),
        name="project",
    )(place, in_hbm(mine), other, in_hbm(gain), in_vmem(early), in_vmem(wk), in_vmem(wv), in_hbm(wq))


def fetch_first_kernel(wq_ref, wk_ref, wv_ref, early_ref, wk_out, wv_out, sems):
    copies = [
        pltpu.make_async_copy(wk_ref, wk_out, sems.at[0]),
        pltpu.make_async_copy(wv_ref, wv_out, sems.at[1]),
        pltpu.make_async_copy(wq_ref.at[:, :early_ref.shape[1]], early_ref, sems.at[2])]
    for copy in copies:
        copy.start()
    for copy in copies:
        copy.wait()


def fetch_first(wq, wk, wv, early):
    hbm = pl.BlockSpec(memory_space=pltpu.HBM)
    vmem = pl.BlockSpec(memory_space=pltpu.VMEM)
    depth = wq.shape[0]
    return pl.pallas_call(
        fetch_first_kernel,
        out_shape=(
            pltpu.VMEM((depth, early), wq.dtype), pltpu.VMEM(wk.shape, wk.dtype), pltpu.VMEM(wv.shape, wv.dtype)),
        in_specs=[hbm] * 3,
        out_specs=(vmem,) * 3,
        scratch_shapes=[pltpu.SemaphoreType.DMA((3,))],
        compiler_params=pltpu.CompilerParams(vmem_limit_bytes=16 * MIB),
        cost_estimate=pl.CostEstimate(
            flops=0, bytes_accessed=2 * depth * (early + 2 * wk.shape[1]), transcendentals=0),
        name="fetch_first",
    )(in_hbm(wq), in_hbm(wk), in_hbm(wv))


def notes_kernel(steps, position_ref, length_ref, after_ref, notes_ref):
    lane = lax.broadcasted_iota(jnp.int32, (1, HD), 1)
    frequency = rope_frequencies((lane % (HD // 2)).astype(jnp.float32), HD)
    sign = jnp.where(lane < HD // 2, -1.0, 1.0)
    for t in range(steps):
        angle = (position_ref[0] + t).astype(jnp.float32) * frequency
        notes_ref[2 * t:2 * t + 1, :] = jnp.cos(angle)
        notes_ref[2 * t + 1:2 * t + 2, :] = jnp.sin(angle) * sign
    length = length_ref[0].astype(jnp.float32)
    notes_ref[2 * steps:, :] = jnp.full((notes_ref.shape[0] - 2 * steps, HD), length)


def take_notes(position, length, after, steps):
    smem = pl.BlockSpec(memory_space=pltpu.SMEM)
    return pl.pallas_call(
        functools.partial(notes_kernel, steps),
        out_shape=jax.ShapeDtypeStruct((2 * steps + 4, HD), jnp.float32),
        in_specs=[smem, smem, pl.BlockSpec(memory_space=pl.ANY)],
        out_specs=pl.BlockSpec(memory_space=pltpu.VMEM),
        compiler_params=pltpu.CompilerParams(vmem_limit_bytes=4 * MIB),
        name="notes",
    )(position, length, after)


def combine_kernel(arrived, parts, *refs):
    total = refs[0][...]
    for ref in refs[1:arrived + 1]:
        total = total + ref[...].astype(jnp.float32)
    count = total.shape[0] // parts
    for i, ref in enumerate(refs[-parts:]):
        ref[...] = total[i * count:(i + 1) * count].astype(ref.dtype)


def combine(keep, came, held, parts):
    vmem = pl.BlockSpec(memory_space=pltpu.VMEM)
    out_shape = part_shapes(keep.shape[0], parts, keep.shape[1:])
    return pl.pallas_call(
        functools.partial(combine_kernel, len(came), parts),
        out_shape=out_shape,
        in_specs=[vmem] * (1 + len(came)) + [pl.BlockSpec(memory_space=pl.ANY)] * len(held),
        out_specs=(vmem,) * parts,
        compiler_params=pltpu.CompilerParams(vmem_limit_bytes=24 * MIB),
        name="combine",
    )(keep, *came, *[in_vmem(piece) for piece in held])


def fetch_kernel(first, parts, weight_ref, *rest):
    held_ref, sems = rest[-2:]
    rows = held_ref.shape[0] // parts
    copies = [
        pltpu.make_async_copy(
            weight_ref.at[first + c * rows:first + (c + 1) * rows],
            held_ref.at[c * rows:(c + 1) * rows], sems.at[c])
        for c in range(parts)]
    for copy in copies:
        copy.start()
    for copy in copies:
        copy.wait()


def fetch(weight, first, rows, after):
    parts = 4
    return pl.pallas_call(
        functools.partial(fetch_kernel, first, parts),
        out_shape=pltpu.VMEM((rows, weight.shape[1]), weight.dtype),
        in_specs=[pl.BlockSpec(memory_space=pltpu.HBM)] + [pl.BlockSpec(memory_space=pl.ANY)] * len(after),
        out_specs=pl.BlockSpec(memory_space=pltpu.VMEM),
        scratch_shapes=[pltpu.SemaphoreType.DMA((parts,))],
        compiler_params=pltpu.CompilerParams(vmem_limit_bytes=16 * MIB),
        cost_estimate=pl.CostEstimate(
            flops=0, bytes_accessed=2 * rows * weight.shape[1], transcendentals=0),
        name="fetch",
    )(in_hbm(weight), *after)


def attend_kernel(steps, width, place_ref, table_ref, keys_ref, values_ref, same_in_ref, cross_in_ref,
                  same_ref, cross_ref, new_keys_ref, new_values_ref):
    kv_heads = keys_ref.shape[1] // HD
    half_kv = kv_heads // 2
    pitch = same_in_ref.shape[1] // (half_kv * steps)
    group = pitch - 4
    slots = keys_ref.shape[0]
    factor = 1.0 / math.sqrt(HD)
    low_side = place_ref[0] % 2 == 0
    same, cross = same_in_ref[0], cross_in_ref[0].astype(jnp.float32)
    halves = [jnp.where(low_side, same, cross), jnp.where(low_side, cross, same)]
    live = lax.broadcasted_iota(jnp.int32, (steps * group, slots), 1) < (
        table_ref[2 * steps:2 * steps + 1, :1].astype(jnp.int32))
    row_step = lax.broadcasted_iota(jnp.int32, (steps * group, 1), 0) // group
    fresh_keys = [[None] * kv_heads for _ in range(steps)]
    fresh_values = [[None] * kv_heads for _ in range(steps)]
    queries = [None] * kv_heads
    for k in range(half_kv):
        for g in range(2):
            head = g * half_kv + k
            query = []
            for t in range(steps):
                rows = halves[g][(k * steps + t) * pitch:(k * steps + t + 1) * pitch]
                squares = rows[group + 2:group + 3] + rows[group + 3:group + 4]
                rows = rows * lax.rsqrt(squares / width + epsilon)
                cosine = table_ref[2 * t:2 * t + 1, :]
                sine = table_ref[2 * t + 1:2 * t + 2, :]
                turned = rows * cosine + pltpu.roll(rows, HD // 2, 1) * sine
                query.append(turned[:group])
                fresh_keys[t][head] = turned[group:group + 1].astype(jnp.bfloat16).astype(jnp.float32)
                fresh_values[t][head] = rows[group + 1:group + 2].astype(jnp.bfloat16).astype(jnp.float32)
            queries[head] = jnp.concatenate(query, axis=0).astype(jnp.bfloat16)
    new_keys_ref[...] = jnp.concatenate(
        [jnp.concatenate(row, axis=1) for row in fresh_keys], axis=0).astype(jnp.bfloat16)
    new_values_ref[...] = jnp.concatenate(
        [jnp.concatenate(row, axis=1) for row in fresh_values], axis=0).astype(jnp.bfloat16)
    contexts = []
    for head in range(kv_heads):
        columns = slice(head * HD, (head + 1) * HD)
        query = queries[head]
        scores = lax.dot_general(
            query, keys_ref[:, columns], (((1,), (1,)), ((), ())),
            preferred_element_type=jnp.float32) * factor
        scores = jnp.where(live, scores, -jnp.inf)
        top = jnp.max(scores, axis=-1, keepdims=True)
        wide = query.astype(jnp.float32)
        fresh = []
        for s in range(steps):
            score = jnp.sum(wide * fresh_keys[s][head], axis=-1, keepdims=True) * factor
            score = jnp.where(row_step >= s, score, -jnp.inf)
            fresh.append(score)
            top = jnp.maximum(top, score)
        scores = jnp.exp(scores - top)
        total = jnp.sum(scores, axis=-1, keepdims=True)
        fresh = [jnp.exp(score - top) for score in fresh]
        for score in fresh:
            total = total + score
        weight = (scores / total).astype(jnp.bfloat16)
        mixed = jnp.dot(weight, values_ref[:, columns], preferred_element_type=jnp.float32)
        for s in range(steps):
            weight = (fresh[s] / total).astype(jnp.bfloat16).astype(jnp.float32)
            mixed = mixed + weight * fresh_values[s][head]
        contexts.append(mixed)
    for k in range(half_kv):
        lower, upper = contexts[k], contexts[half_kv + k]
        span = slice(k * steps * group, (k + 1) * steps * group)
        same_ref[span, :] = jnp.where(low_side, lower, upper).astype(jnp.bfloat16)
        cross_ref[span, :] = jnp.where(low_side, upper, lower).astype(jnp.bfloat16)


def attend(place, same, cross, table, keys, values, steps, width, half_heads):
    vmem = pl.BlockSpec(memory_space=pltpu.VMEM)
    smem = pl.BlockSpec(memory_space=pltpu.SMEM)
    kv_cols = keys.shape[1]
    half = jax.ShapeDtypeStruct((steps * half_heads, HD), jnp.bfloat16)
    fresh = jax.ShapeDtypeStruct((steps, kv_cols), jnp.bfloat16)
    return pl.pallas_call(
        functools.partial(attend_kernel, steps, width),
        out_shape=(half, half, fresh, fresh),
        in_specs=[smem] + [vmem] * 5,
        out_specs=(vmem,) * 4,
        compiler_params=pltpu.CompilerParams(vmem_limit_bytes=16 * MIB),
        name="attend",
    )(place, table, keys, values, same, cross)


def pack_kernel(same_ref, other_ref, out_ref):
    out_ref[0] = same_ref[...]
    out_ref[1] = other_ref[...]


def join_kernel(arrived, *refs):
    out_ref = refs[-1]
    for i, ref in enumerate(refs[:arrived + 1]):
        count = ref.shape[0]
        out_ref[i * count:(i + 1) * count] = ref[...]


def local_call(kernel, shape, arrays, held=()):
    vmem = pl.BlockSpec(memory_space=pltpu.VMEM)
    return pl.pallas_call(
        kernel,
        out_shape=jax.ShapeDtypeStruct(shape, jnp.bfloat16),
        in_specs=[vmem] * len(arrays) + [pl.BlockSpec(memory_space=pl.ANY)] * len(held),
        out_specs=vmem,
        compiler_params=pltpu.CompilerParams(vmem_limit_bytes=16 * MIB),
        name="local",
    )(*arrays, *[in_vmem(piece) for piece in held])


def output_kernel(steps, colors, patterns, pieces, place_ref, *rest):
    weight_refs, context_refs = rest[:pieces], rest[pieces:-4]
    mine_ref, other_ref, wide_buf, rows_buf = rest[-4:]
    device = place_ref[0]
    devices = len(patterns)
    half_seqs = devices // 2
    count, block, _ = context_refs[0].shape
    group = block // (steps * colors)
    for j, pattern in enumerate(patterns):
        rows = context_refs[j // count][j % count]
        start = pl.multiple_of((device ^ pattern) * block, 8)
        wide_buf[pl.ds(start, block), :] = rows.astype(jnp.float32)
    for head in range(colors * group):
        color, h = head // group, head % group
        lines = []
        for g in range(2):
            for t in range(steps):
                start = g * half_seqs * block + (color * steps + t) * group + h
                lines.append(wide_buf[pl.ds(start, half_seqs, stride=block), :])
        rows_buf[:, head * HD:(head + 1) * HD] = jnp.concatenate(lines, axis=0).astype(jnp.bfloat16)
    low_side = device % 2 == 0
    half = rows_buf.shape[0] // 2
    columns = mine_ref.shape[1]
    chunk = min(columns, 512)
    for c in range(columns // chunk):
        span = slice(c * chunk, (c + 1) * chunk)
        product, first = None, 0
        for weight_ref in weight_refs:
            last = first + weight_ref.shape[0]
            part = jnp.dot(rows_buf[:, first:last], weight_ref[:, span], preferred_element_type=jnp.float32)
            product = part if product is None else product + part
            first = last
        lower, upper = product[:half], product[half:]
        mine_ref[:, span] = jnp.where(low_side, lower, upper)
        other_ref[:, span] = jnp.where(low_side, upper, lower).astype(jnp.bfloat16)


def output(place, contexts, patterns, held, steps, colors):
    columns = held[0].shape[1]
    depth = sum(piece.shape[0] for piece in held)
    devices = len(patterns)
    half = devices * steps // 2
    vmem = pl.BlockSpec(memory_space=pltpu.VMEM)
    smem = pl.BlockSpec(memory_space=pltpu.SMEM)
    return pl.pallas_call(
        functools.partial(output_kernel, steps, colors, patterns, len(held)),
        out_shape=(
            jax.ShapeDtypeStruct((half, columns), jnp.float32),
            jax.ShapeDtypeStruct((half, columns), jnp.bfloat16),
        ),
        in_specs=[smem] + [vmem] * (len(held) + len(contexts)),
        out_specs=(vmem, vmem),
        scratch_shapes=[
            pltpu.VMEM((devices * contexts[0].shape[1], HD), jnp.float32),
            pltpu.VMEM((devices * steps, depth), jnp.bfloat16),
        ],
        compiler_params=pltpu.CompilerParams(vmem_limit_bytes=26 * MIB),
        cost_estimate=pl.CostEstimate(
            flops=2 * devices * steps * depth * columns,
            bytes_accessed=2 * depth * columns, transcendentals=0),
        name="output",
    )(place, *[in_vmem(piece) for piece in held], *contexts)


def body(hidden_in, norm_gain, query_weight, key_weight, value_weight, out_weight,
         cache_keys, cache_values, lengths, positions):
    steps, half_seqs, depth = hidden_in.shape
    everyone = ("gx", "gy")
    devices = lax.axis_size(everyone)
    bits = devices.bit_length() - 1
    colors = key_weight.shape[1] // HD
    half_heads = query_weight.shape[1] // HD
    group = half_heads // colors
    place = lax.axis_index(everyone).astype(jnp.int32).reshape(1)

    def partner(array, pattern):
        return lax.ppermute(array, everyone, [(i, i ^ pattern) for i in range(devices)])

    near_first = [list(range(first, min(first + 2, bits))) for first in range(1, bits, 2)]
    stages = near_first + [[0]]
    order = [bit for stage in stages for bit in stage]
    total = out_weight.shape[0]
    cuts = [total * i // 8 for i in (0, 3, 8)]
    held = []

    def fetch_next(window, after):
        i = len(held)
        if window not in (0, 3):
            return []
        held.append(fetch(out_weight, cuts[i], cuts[i + 1] - cuts[i], after))
        return held[-1:]

    mine = hidden_in.reshape(steps * half_seqs, depth)
    other = partner(mine, 1)
    early, wk, wv = fetch_first(query_weight, key_weight, value_weight, 512)
    parts = project(
        place, mine, other, norm_gain.reshape(-1, HD), early, wk, wv, query_weight,
        steps, group, colors, order, 1 << len(stages[0]))
    notes = take_notes(positions, lengths, parts[1], steps)
    for i, stage in enumerate(stages[:-1]):
        came = [partner(part, pattern) for part, pattern in zip(parts[1:], slot_patterns(stage)[1:])]
        now = fetch_next(i, [parts[1], notes])
        parts = combine(parts[0], came, now, 1 << len(stages[i + 1]))
    same, cross, new_keys, new_values = attend(
        place, parts[0], partner(parts[1], 1), notes, cache_keys[0], cache_values[0],
        steps, depth * lax.axis_size("gx"), half_heads)

    context = local_call(pack_kernel, (2,) + same.shape, [same, partner(cross, 1)])
    patterns = [0, 1]
    for i, stage in enumerate(near_first[::-1]):
        moves = slot_patterns(stage)
        came = [partner(context, move) for move in moves[1:]]
        patterns = [p ^ move for move in moves for p in patterns]
        now = fetch_next(len(near_first) + i, [context])
        if i < len(near_first) - 1:
            shape = (len(moves) * context.shape[0],) + context.shape[1:]
            context = local_call(functools.partial(join_kernel, len(came)), shape, [context, *came], now)
    mine, other = output(place, [context, *came], patterns, held, steps, colors)
    other = partner(other, 1)
    result = (mine + other.astype(jnp.float32)).astype(jnp.bfloat16)
    return (
        result.reshape(steps, half_seqs, -1),
        new_keys[:, None, :],
        new_values[:, None, :],
    )


def solution(mesh):
    in_specs = (
        P(None, ("rep", "gy"), "gx"),
        P("gx"),
        P("gx", "gy"),
        P("gx", "gy"),
        P("gx", "gy"),
        P("gy", "gx"),
        P(("rep", "gx", "gy"), None, None),
        P(("rep", "gx", "gy"), None, None),
        P(("rep", "gx", "gy")),
        P(("rep", "gx", "gy")),
    )
    out_specs = (
        P(None, ("rep", "gy"), "gx"),
        P(None, ("rep", "gx", "gy"), None),
        P(None, ("rep", "gx", "gy"), None),
    )
    return jax.shard_map(body, mesh=mesh, in_specs=in_specs, out_specs=out_specs, check_vma=False)
```

```python
import functools
import math

import jax
import jax.numpy as jnp
from jax import lax
from jax.experimental import pallas as pl
from jax.experimental.pallas import tpu as pltpu
from jax.sharding import PartitionSpec as P

HD = 128
epsilon = 1e-05
rope_theta = 500000.0
MIB = 1024 * 1024


def rope_frequencies(index, head_size):
    frequency = jnp.exp(-math.log(rope_theta) * 2.0 * index / head_size)
    wavelength = 2.0 * math.pi / frequency
    smooth = (8192.0 / wavelength - 1.0) / 3.0
    blended = (1.0 - smooth) * frequency / 8.0 + smooth * frequency
    adjusted = jnp.where(wavelength > 8192.0, frequency / 8.0, blended)
    return jnp.where(wavelength < 2048.0, frequency, adjusted)


def slot_patterns(order):
    count = len(order)
    return [
        sum(((j >> (count - 1 - i)) & 1) << bit for i, bit in enumerate(order))
        for j in range(1 << count)]


def in_hbm(array):
    return pltpu.with_memory_space_constraint(array, pltpu.HBM)


def in_vmem(array):
    return pltpu.with_memory_space_constraint(array, pltpu.VMEM)


def project_kernel(steps, group, colors, order, chunk, place_ref, mine_ref, other_ref, gain_ref, early_ref, wk_ref, wv_ref,
                   wq_ref, *rest):
    part_refs, rest = rest[:-5], rest[-5:]
    mine_buf, gain_buf, wq_buf, rows_buf, sems = rest
    early = early_ref.shape[1]
    q_cols = wq_ref.shape[1]
    chunks = (q_cols - early) // chunk
    copies = [pltpu.make_async_copy(mine_ref, mine_buf, sems.at[chunks]),
              pltpu.make_async_copy(gain_ref, gain_buf, sems.at[chunks + 1])]
    for c in range(chunks):
        copies.append(pltpu.make_async_copy(
            wq_ref.at[:, early + c * chunk:early + (c + 1) * chunk], wq_buf.at[c], sems.at[c]))
    for copy in copies:
        copy.start()

    device = place_ref[0]
    half_rows = mine_ref.shape[0]
    total_rows = 2 * half_rows
    half_seqs = half_rows // steps
    pitch = group + 4
    stride = colors * steps * pitch

    def spread(color, row, block):
        for g in range(2):
            for t in range(steps):
                first = (g * steps + t) * half_seqs
                start = g * half_seqs * stride + (color * steps + t) * pitch + row
                rows_buf[pl.ds(start, half_seqs, stride=stride), :] = block[first:first + half_seqs, :]

    low_side = device % 2 == 0
    copies[0].wait()
    copies[1].wait()
    mine = mine_buf[...].astype(jnp.float32)
    other = other_ref[...].astype(jnp.float32)
    x = jnp.concatenate(
        [jnp.where(low_side, mine, other), jnp.where(low_side, other, mine)], axis=0)
    gain = gain_buf[...].astype(jnp.float32)
    gain = jnp.concatenate([gain[i:i + 1] for i in range(gain.shape[0])], axis=1)
    scaled = (x * gain).astype(jnp.bfloat16)
    squares = jnp.sum(x * x, axis=-1, keepdims=True)
    high = squares.astype(jnp.bfloat16).astype(jnp.float32)
    low = squares - high
    for color in range(colors):
        spread(color, group + 2, jnp.broadcast_to(high, (total_rows, HD)))
        spread(color, group + 3, jnp.broadcast_to(low, (total_rows, HD)))

    def multiply(weights, place_of_head):
        product = jnp.dot(scaled, weights, preferred_element_type=jnp.float32)
        for i in range(product.shape[1] // HD):
            spread(*place_of_head(i), product[:, i * HD:(i + 1) * HD])

    multiply(wk_ref[...], lambda i: (i, group))
    multiply(wv_ref[...], lambda i: (i, group + 1))
    multiply(early_ref[...], lambda i: (i // group, i % group))

    for c in range(chunks):
        copies[2 + c].wait()
        first = (early + c * chunk) // HD
        multiply(wq_buf[c], lambda i: ((first + i) // group, (first + i) % group))
    per_part = part_refs[0].shape[0]
    for slot, pattern in enumerate(slot_patterns(order)):
        ref = part_refs[slot // per_part]
        start = pl.multiple_of((device ^ pattern) * stride, 8)
        ref[slot % per_part] = rows_buf[pl.ds(start, stride), :].astype(ref.dtype)


def part_shapes(total, count, block):
    shape = (total // count,) + block
    return (jax.ShapeDtypeStruct(shape, jnp.float32),) + (jax.ShapeDtypeStruct(shape, jnp.bfloat16),) * (count - 1)


def project(place, mine, other, gain, early, wk, wv, wq, steps, group, colors, order, count):
    half_rows, depth = mine.shape
    q_cols, kv_cols = wq.shape[1], wk.shape[1]
    seqs = 2 * half_rows // steps
    chunk = 512
    chunks = (q_cols - early.shape[1]) // chunk
    vmem = pl.BlockSpec(memory_space=pltpu.VMEM)
    smem = pl.BlockSpec(memory_space=pltpu.SMEM)
    hbm = pl.BlockSpec(memory_space=pltpu.HBM)
    out_shape = part_shapes(
        seqs, count, (colors * steps * (group + 4), HD))
    return pl.pallas_call(
        functools.partial(project_kernel, steps, group, colors, order, chunk),
        out_shape=out_shape,
        in_specs=[smem, hbm, vmem, hbm, vmem, vmem, vmem, hbm],
        out_specs=(vmem,) * len(out_shape),
        scratch_shapes=[
            pltpu.VMEM(mine.shape, jnp.bfloat16),
            pltpu.VMEM(gain.shape, jnp.bfloat16),
            pltpu.VMEM((chunks, depth, chunk), jnp.bfloat16),
            pltpu.VMEM((seqs * colors * steps * (group + 4), HD), jnp.float32),
            pltpu.SemaphoreType.DMA((chunks + 2,)),
        ],
        compiler_params=pltpu.CompilerParams(vmem_limit_bytes=28 * MIB),
        cost_estimate=pl.CostEstimate(
            flops=4 * half_rows * depth * (q_cols + 2 * kv_cols),
            bytes_accessed=2 * depth * (q_cols + 2 * kv_cols), transcendentals=0),
        name="project",
    )(place, in_hbm(mine), other, in_hbm(gain), in_vmem(early), in_vmem(wk), in_vmem(wv), in_hbm(wq))


def fetch_first_kernel(wq_ref, wk_ref, wv_ref, early_ref, wk_out, wv_out, sems):
    copies = [
        pltpu.make_async_copy(wk_ref, wk_out, sems.at[0]),
        pltpu.make_async_copy(wv_ref, wv_out, sems.at[1]),
        pltpu.make_async_copy(wq_ref.at[:, :early_ref.shape[1]], early_ref, sems.at[2])]
    for copy in copies:
        copy.start()
    for copy in copies:
        copy.wait()


def fetch_first(wq, wk, wv, early):
    hbm = pl.BlockSpec(memory_space=pltpu.HBM)
    vmem = pl.BlockSpec(memory_space=pltpu.VMEM)
    depth = wq.shape[0]
    return pl.pallas_call(
        fetch_first_kernel,
        out_shape=(
            pltpu.VMEM((depth, early), wq.dtype), pltpu.VMEM(wk.shape, wk.dtype), pltpu.VMEM(wv.shape, wv.dtype)),
        in_specs=[hbm] * 3,
        out_specs=(vmem,) * 3,
        scratch_shapes=[pltpu.SemaphoreType.DMA((3,))],
        compiler_params=pltpu.CompilerParams(vmem_limit_bytes=16 * MIB),
        cost_estimate=pl.CostEstimate(
            flops=0, bytes_accessed=2 * depth * (early + 2 * wk.shape[1]), transcendentals=0),
        name="fetch_first",
    )(in_hbm(wq), in_hbm(wk), in_hbm(wv))


def notes_kernel(steps, position_ref, length_ref, after_ref, notes_ref):
    lane = lax.broadcasted_iota(jnp.int32, (1, HD), 1)
    frequency = rope_frequencies((lane % (HD // 2)).astype(jnp.float32), HD)
    sign = jnp.where(lane < HD // 2, -1.0, 1.0)
    for t in range(steps):
        angle = (position_ref[0] + t).astype(jnp.float32) * frequency
        notes_ref[2 * t:2 * t + 1, :] = jnp.cos(angle)
        notes_ref[2 * t + 1:2 * t + 2, :] = jnp.sin(angle) * sign
    length = length_ref[0].astype(jnp.float32)
    notes_ref[2 * steps:, :] = jnp.full((notes_ref.shape[0] - 2 * steps, HD), length)


def take_notes(position, length, after, steps):
    smem = pl.BlockSpec(memory_space=pltpu.SMEM)
    return pl.pallas_call(
        functools.partial(notes_kernel, steps),
        out_shape=jax.ShapeDtypeStruct((2 * steps + 4, HD), jnp.float32),
        in_specs=[smem, smem, pl.BlockSpec(memory_space=pl.ANY)],
        out_specs=pl.BlockSpec(memory_space=pltpu.VMEM),
        compiler_params=pltpu.CompilerParams(vmem_limit_bytes=4 * MIB),
        name="notes",
    )(position, length, after)


def combine_kernel(arrived, parts, *refs):
    total = refs[0][...]
    for ref in refs[1:arrived + 1]:
        total = total + ref[...].astype(jnp.float32)
    count = total.shape[0] // parts
    for i, ref in enumerate(refs[-parts:]):
        ref[...] = total[i * count:(i + 1) * count].astype(ref.dtype)


def combine(keep, came, held, parts):
    vmem = pl.BlockSpec(memory_space=pltpu.VMEM)
    out_shape = part_shapes(keep.shape[0], parts, keep.shape[1:])
    return pl.pallas_call(
        functools.partial(combine_kernel, len(came), parts),
        out_shape=out_shape,
        in_specs=[vmem] * (1 + len(came)) + [pl.BlockSpec(memory_space=pl.ANY)] * len(held),
        out_specs=(vmem,) * parts,
        compiler_params=pltpu.CompilerParams(vmem_limit_bytes=24 * MIB),
        name="combine",
    )(keep, *came, *[in_vmem(piece) for piece in held])


def fetch_kernel(first, parts, weight_ref, *rest):
    held_ref, sems = rest[-2:]
    rows = held_ref.shape[0] // parts
    copies = [
        pltpu.make_async_copy(
            weight_ref.at[first + c * rows:first + (c + 1) * rows],
            held_ref.at[c * rows:(c + 1) * rows], sems.at[c])
        for c in range(parts)]
    for copy in copies:
        copy.start()
    for copy in copies:
        copy.wait()


def fetch(weight, first, rows, after):
    parts = 4
    return pl.pallas_call(
        functools.partial(fetch_kernel, first, parts),
        out_shape=pltpu.VMEM((rows, weight.shape[1]), weight.dtype),
        in_specs=[pl.BlockSpec(memory_space=pltpu.HBM)] + [pl.BlockSpec(memory_space=pl.ANY)] * len(after),
        out_specs=pl.BlockSpec(memory_space=pltpu.VMEM),
        scratch_shapes=[pltpu.SemaphoreType.DMA((parts,))],
        compiler_params=pltpu.CompilerParams(vmem_limit_bytes=16 * MIB),
        cost_estimate=pl.CostEstimate(
            flops=0, bytes_accessed=2 * rows * weight.shape[1], transcendentals=0),
        name="fetch",
    )(in_hbm(weight), *after)


def attend_kernel(steps, width, unused, place_ref, table_ref, keys_ref, values_ref, *rest):
    rest = rest[unused:]
    part_refs, (same_ref, cross_ref, new_keys_ref, new_values_ref) = rest[:-4], rest[-4:]
    kv_heads = keys_ref.shape[1] // HD
    half_kv = kv_heads // 2
    pitch = part_refs[0].shape[1] // (half_kv * steps)
    group = pitch - 4
    slots = keys_ref.shape[0]
    factor = 1.0 / math.sqrt(HD)
    low_side = place_ref[0] % 2 == 0
    same, cross = [
        functools.reduce(jnp.add, [ref[0].astype(jnp.float32) for ref in part_refs[i::2]]) for i in range(2)]
    halves = [jnp.where(low_side, same, cross), jnp.where(low_side, cross, same)]
    live = lax.broadcasted_iota(jnp.int32, (steps * group, slots), 1) < (
        table_ref[2 * steps:2 * steps + 1, :1].astype(jnp.int32))
    row_step = lax.broadcasted_iota(jnp.int32, (steps * group, 1), 0) // group
    fresh_keys = [[None] * kv_heads for _ in range(steps)]
    fresh_values = [[None] * kv_heads for _ in range(steps)]
    queries = [None] * kv_heads
    for k in range(half_kv):
        for g in range(2):
            head = g * half_kv + k
            query = []
            for t in range(steps):
                rows = halves[g][(k * steps + t) * pitch:(k * steps + t + 1) * pitch]
                squares = rows[group + 2:group + 3] + rows[group + 3:group + 4]
                rows = rows * lax.rsqrt(squares / width + epsilon)
                cosine = table_ref[2 * t:2 * t + 1, :]
                sine = table_ref[2 * t + 1:2 * t + 2, :]
                turned = rows * cosine + pltpu.roll(rows, HD // 2, 1) * sine
                query.append(turned[:group])
                fresh_keys[t][head] = turned[group:group + 1].astype(jnp.bfloat16).astype(jnp.float32)
                fresh_values[t][head] = rows[group + 1:group + 2].astype(jnp.bfloat16).astype(jnp.float32)
            queries[head] = jnp.concatenate(query, axis=0).astype(jnp.bfloat16)
    new_keys_ref[...] = jnp.concatenate(
        [jnp.concatenate(row, axis=1) for row in fresh_keys], axis=0).astype(jnp.bfloat16)
    new_values_ref[...] = jnp.concatenate(
        [jnp.concatenate(row, axis=1) for row in fresh_values], axis=0).astype(jnp.bfloat16)
    contexts = []
    for head in range(kv_heads):
        columns = slice(head * HD, (head + 1) * HD)
        query = queries[head]
        scores = lax.dot_general(
            query, keys_ref[:, columns], (((1,), (1,)), ((), ())),
            preferred_element_type=jnp.float32) * factor
        scores = jnp.where(live, scores, -jnp.inf)
        top = jnp.max(scores, axis=-1, keepdims=True)
        wide = query.astype(jnp.float32)
        fresh = []
        for s in range(steps):
            score = jnp.sum(wide * fresh_keys[s][head], axis=-1, keepdims=True) * factor
            score = jnp.where(row_step >= s, score, -jnp.inf)
            fresh.append(score)
            top = jnp.maximum(top, score)
        scores = jnp.exp(scores - top)
        total = jnp.sum(scores, axis=-1, keepdims=True)
        fresh = [jnp.exp(score - top) for score in fresh]
        for score in fresh:
            total = total + score
        weight = (scores / total).astype(jnp.bfloat16)
        mixed = jnp.dot(weight, values_ref[:, columns], preferred_element_type=jnp.float32)
        for s in range(steps):
            weight = (fresh[s] / total).astype(jnp.bfloat16).astype(jnp.float32)
            mixed = mixed + weight * fresh_values[s][head]
        contexts.append(mixed)
    for k in range(half_kv):
        lower, upper = contexts[k], contexts[half_kv + k]
        span = slice(k * steps * group, (k + 1) * steps * group)
        same_ref[0, span, :] = jnp.where(low_side, lower, upper).astype(jnp.bfloat16)
        cross_ref[0, span, :] = jnp.where(low_side, upper, lower).astype(jnp.bfloat16)


def attend(place, parts, table, keys, values, held, steps, width, half_heads):
    vmem = pl.BlockSpec(memory_space=pltpu.VMEM)
    smem = pl.BlockSpec(memory_space=pltpu.SMEM)
    kv_cols = keys.shape[1]
    half = jax.ShapeDtypeStruct((1, steps * half_heads, HD), jnp.bfloat16)
    fresh = jax.ShapeDtypeStruct((steps, kv_cols), jnp.bfloat16)
    return pl.pallas_call(
        functools.partial(attend_kernel, steps, width, len(held)),
        out_shape=(half, half, fresh, fresh),
        in_specs=[smem] + [vmem] * 3 + [pl.BlockSpec(memory_space=pl.ANY)] * len(held) + [vmem] * len(parts),
        out_specs=(vmem,) * 4,
        compiler_params=pltpu.CompilerParams(vmem_limit_bytes=16 * MIB),
        name="attend",
    )(place, table, keys, values, *[in_vmem(piece) for piece in held], *parts)


def join_kernel(arrived, *refs):
    out_ref = refs[-1]
    for i, ref in enumerate(refs[:arrived + 1]):
        count = ref.shape[0]
        out_ref[i * count:(i + 1) * count] = ref[...]


def local_call(kernel, shape, arrays, held=()):
    vmem = pl.BlockSpec(memory_space=pltpu.VMEM)
    return pl.pallas_call(
        kernel,
        out_shape=jax.ShapeDtypeStruct(shape, jnp.bfloat16),
        in_specs=[vmem] * len(arrays) + [pl.BlockSpec(memory_space=pl.ANY)] * len(held),
        out_specs=vmem,
        compiler_params=pltpu.CompilerParams(vmem_limit_bytes=16 * MIB),
        name="local",
    )(*arrays, *[in_vmem(piece) for piece in held])


def output_kernel(steps, colors, patterns, pieces, place_ref, *rest):
    weight_refs, context_refs = rest[:pieces], rest[pieces:-4]
    mine_ref, other_ref, wide_buf, rows_buf = rest[-4:]
    device = place_ref[0]
    devices = len(patterns)
    half_seqs = devices // 2
    count, block, _ = context_refs[0].shape
    group = block // (steps * colors)
    for j, pattern in enumerate(patterns):
        rows = context_refs[j // count][j % count]
        start = pl.multiple_of((device ^ pattern) * block, 8)
        wide_buf[pl.ds(start, block), :] = rows.astype(jnp.float32)
    for head in range(colors * group):
        color, h = head // group, head % group
        lines = []
        for g in range(2):
            for t in range(steps):
                start = g * half_seqs * block + (color * steps + t) * group + h
                lines.append(wide_buf[pl.ds(start, half_seqs, stride=block), :])
        rows_buf[:, head * HD:(head + 1) * HD] = jnp.concatenate(lines, axis=0).astype(jnp.bfloat16)
    low_side = device % 2 == 0
    half = rows_buf.shape[0] // 2
    columns = mine_ref.shape[1]
    chunk = min(columns, 512)
    for c in range(columns // chunk):
        span = slice(c * chunk, (c + 1) * chunk)
        product, first = None, 0
        for weight_ref in weight_refs:
            last = first + weight_ref.shape[0]
            part = jnp.dot(rows_buf[:, first:last], weight_ref[:, span], preferred_element_type=jnp.float32)
            product = part if product is None else product + part
            first = last
        lower, upper = product[:half], product[half:]
        mine_ref[:, span] = jnp.where(low_side, lower, upper)
        other_ref[:, span] = jnp.where(low_side, upper, lower).astype(jnp.bfloat16)


def output(place, contexts, patterns, held, steps, colors):
    columns = held[0].shape[1]
    depth = sum(piece.shape[0] for piece in held)
    devices = len(patterns)
    half = devices * steps // 2
    vmem = pl.BlockSpec(memory_space=pltpu.VMEM)
    smem = pl.BlockSpec(memory_space=pltpu.SMEM)
    return pl.pallas_call(
        functools.partial(output_kernel, steps, colors, patterns, len(held)),
        out_shape=(
            jax.ShapeDtypeStruct((half, columns), jnp.float32),
            jax.ShapeDtypeStruct((half, columns), jnp.bfloat16),
        ),
        in_specs=[smem] + [vmem] * (len(held) + len(contexts)),
        out_specs=(vmem, vmem),
        scratch_shapes=[
            pltpu.VMEM((devices * contexts[0].shape[1], HD), jnp.float32),
            pltpu.VMEM((devices * steps, depth), jnp.bfloat16),
        ],
        compiler_params=pltpu.CompilerParams(vmem_limit_bytes=26 * MIB),
        cost_estimate=pl.CostEstimate(
            flops=2 * devices * steps * depth * columns,
            bytes_accessed=2 * depth * columns, transcendentals=0),
        name="output",
    )(place, *[in_vmem(piece) for piece in held], *contexts)


def body(hidden_in, norm_gain, query_weight, key_weight, value_weight, out_weight,
         cache_keys, cache_values, lengths, positions):
    steps, half_seqs, depth = hidden_in.shape
    everyone = ("gx", "gy")
    devices = lax.axis_size(everyone)
    bits = devices.bit_length() - 1
    colors = key_weight.shape[1] // HD
    half_heads = query_weight.shape[1] // HD
    group = half_heads // colors
    place = lax.axis_index(everyone).astype(jnp.int32).reshape(1)

    def partner(array, pattern):
        return lax.ppermute(array, everyone, [(i, i ^ pattern) for i in range(devices)])

    stages = [list(range(first, min(first + 2, bits))) for first in range(1, bits, 2)]
    stages[-1] = stages[-1] + [0]
    order = [bit for stage in stages for bit in stage]
    total = out_weight.shape[0]
    cuts = [total * i // 8 for i in (0, 3, 4, 5, 8)]
    held = []

    def fetch_next(window, after):
        i = len(held)
        if window not in (0, 1, 2, 3):
            return []
        held.append(fetch(out_weight, cuts[i], cuts[i + 1] - cuts[i], after))
        return held[-1:]

    mine = hidden_in.reshape(steps * half_seqs, depth)
    other = partner(mine, 1)
    early, wk, wv = fetch_first(query_weight, key_weight, value_weight, 512)
    parts = project(
        place, mine, other, norm_gain.reshape(-1, HD), early, wk, wv, query_weight,
        steps, group, colors, order, 1 << len(stages[0]))
    notes = take_notes(positions, lengths, parts[1], steps)
    for i, stage in enumerate(stages):
        came = [partner(part, pattern) for part, pattern in zip(parts[1:], slot_patterns(stage)[1:])]
        now = fetch_next(i, [parts[1], notes])
        if i < len(stages) - 1:
            parts = combine(parts[0], came, now, 1 << len(stages[i + 1]))
    same, cross, new_keys, new_values = attend(
        place, [parts[0], *came], notes, cache_keys[0], cache_values[0], now,
        steps, depth * lax.axis_size("gx"), half_heads)

    context, patterns = None, [0]
    for i, stage in enumerate(stages[::-1]):
        moves = slot_patterns(stage)
        if i == 0:
            context = same
            came = [partner(cross if move & 1 else same, move) for move in moves[1:]]
        else:
            came = [partner(context, move) for move in moves[1:]]
        patterns = [p ^ move for move in moves for p in patterns]
        now = fetch_next(len(stages) + i, [context])
        if i < len(stages) - 1:
            shape = (len(moves) * context.shape[0],) + context.shape[1:]
            context = local_call(functools.partial(join_kernel, len(came)), shape, [context, *came], now)
    mine, other = output(place, [context, *came], patterns, held, steps, colors)
    other = partner(other, 1)
    result = (mine + other.astype(jnp.float32)).astype(jnp.bfloat16)
    return (
        result.reshape(steps, half_seqs, -1),
        new_keys[:, None, :],
        new_values[:, None, :],
    )


def solution(mesh):
    in_specs = (
        P(None, ("rep", "gy"), "gx"),
        P("gx"),
        P("gx", "gy"),
        P("gx", "gy"),
        P("gx", "gy"),
        P("gy", "gx"),
        P(("rep", "gx", "gy"), None, None),
        P(("rep", "gx", "gy"), None, None),
        P(("rep", "gx", "gy")),
        P(("rep", "gx", "gy")),
    )
    out_specs = (
        P(None, ("rep", "gy"), "gx"),
        P(None, ("rep", "gx", "gy"), None),
        P(None, ("rep", "gx", "gy"), None),
    )
    return jax.shard_map(body, mesh=mesh, in_specs=in_specs, out_specs=out_specs, check_vma=False)
```

```python
import functools
import math

import jax
import jax.numpy as jnp
from jax import lax
from jax.experimental import pallas as pl
from jax.experimental.pallas import tpu as pltpu
from jax.sharding import PartitionSpec as P

HD = 128
epsilon = 1e-05
rope_theta = 500000.0
MIB = 1024 * 1024


def rope_frequencies(index, head_size):
    frequency = jnp.exp(-math.log(rope_theta) * 2.0 * index / head_size)
    wavelength = 2.0 * math.pi / frequency
    smooth = (8192.0 / wavelength - 1.0) / 3.0
    blended = (1.0 - smooth) * frequency / 8.0 + smooth * frequency
    adjusted = jnp.where(wavelength > 8192.0, frequency / 8.0, blended)
    return jnp.where(wavelength < 2048.0, frequency, adjusted)


def slot_patterns(order):
    count = len(order)
    return [
        sum(((j >> (count - 1 - i)) & 1) << bit for i, bit in enumerate(order))
        for j in range(1 << count)]


def in_hbm(array):
    return pltpu.with_memory_space_constraint(array, pltpu.HBM)


def in_vmem(array):
    return pltpu.with_memory_space_constraint(array, pltpu.VMEM)


def project_kernel(steps, group, colors, order, chunk, place_ref, mine_ref, other_ref, gain_ref, early_ref, wk_ref, wv_ref,
                   wq_ref, *rest):
    part_refs, rest = rest[:-5], rest[-5:]
    mine_buf, gain_buf, wq_buf, rows_buf, sems = rest
    early = early_ref.shape[1]
    q_cols = wq_ref.shape[1]
    chunks = (q_cols - early) // chunk
    copies = [pltpu.make_async_copy(mine_ref, mine_buf, sems.at[chunks]),
              pltpu.make_async_copy(gain_ref, gain_buf, sems.at[chunks + 1])]
    for c in range(chunks):
        copies.append(pltpu.make_async_copy(
            wq_ref.at[:, early + c * chunk:early + (c + 1) * chunk], wq_buf.at[c], sems.at[c]))
    for copy in copies:
        copy.start()

    device = place_ref[0]
    half_rows = mine_ref.shape[0]
    total_rows = 2 * half_rows
    half_seqs = half_rows // steps
    pitch = group + 4
    stride = colors * steps * pitch

    def spread(color, row, block):
        for g in range(2):
            for t in range(steps):
                first = (g * steps + t) * half_seqs
                start = g * half_seqs * stride + (color * steps + t) * pitch + row
                rows_buf[pl.ds(start, half_seqs, stride=stride), :] = block[first:first + half_seqs, :]

    low_side = device % 2 == 0
    copies[0].wait()
    copies[1].wait()
    mine = mine_buf[...].astype(jnp.float32)
    other = other_ref[...].astype(jnp.float32)
    x = jnp.concatenate(
        [jnp.where(low_side, mine, other), jnp.where(low_side, other, mine)], axis=0)
    gain = gain_buf[...].astype(jnp.float32)
    gain = jnp.concatenate([gain[i:i + 1] for i in range(gain.shape[0])], axis=1)
    scaled = (x * gain).astype(jnp.bfloat16)
    squares = jnp.sum(x * x, axis=-1, keepdims=True)
    high = squares.astype(jnp.bfloat16).astype(jnp.float32)
    low = squares - high
    for color in range(colors):
        spread(color, group + 2, jnp.broadcast_to(high, (total_rows, HD)))
        spread(color, group + 3, jnp.broadcast_to(low, (total_rows, HD)))

    def multiply(weights, place_of_head):
        product = jnp.dot(scaled, weights, preferred_element_type=jnp.float32)
        for i in range(product.shape[1] // HD):
            spread(*place_of_head(i), product[:, i * HD:(i + 1) * HD])

    multiply(wk_ref[...], lambda i: (i, group))
    multiply(wv_ref[...], lambda i: (i, group + 1))
    multiply(early_ref[...], lambda i: (i // group, i % group))

    for c in range(chunks):
        copies[2 + c].wait()
        first = (early + c * chunk) // HD
        multiply(wq_buf[c], lambda i: ((first + i) // group, (first + i) % group))
    per_part = part_refs[0].shape[0]
    for slot, pattern in enumerate(slot_patterns(order)):
        ref = part_refs[slot // per_part]
        start = pl.multiple_of((device ^ pattern) * stride, 8)
        ref[slot % per_part] = rows_buf[pl.ds(start, stride), :].astype(ref.dtype)


def part_shapes(total, count, block):
    shape = (total // count,) + block
    return (jax.ShapeDtypeStruct(shape, jnp.float32),) + (jax.ShapeDtypeStruct(shape, jnp.bfloat16),) * (count - 1)


def project(place, mine, other, gain, early, wk, wv, wq, steps, group, colors, order, count):
    half_rows, depth = mine.shape
    q_cols, kv_cols = wq.shape[1], wk.shape[1]
    seqs = 2 * half_rows // steps
    chunk = 512
    chunks = (q_cols - early.shape[1]) // chunk
    vmem = pl.BlockSpec(memory_space=pltpu.VMEM)
    smem = pl.BlockSpec(memory_space=pltpu.SMEM)
    hbm = pl.BlockSpec(memory_space=pltpu.HBM)
    out_shape = part_shapes(
        seqs, count, (colors * steps * (group + 4), HD))
    return pl.pallas_call(
        functools.partial(project_kernel, steps, group, colors, order, chunk),
        out_shape=out_shape,
        in_specs=[smem, hbm, vmem, hbm, vmem, vmem, vmem, hbm],
        out_specs=(vmem,) * len(out_shape),
        scratch_shapes=[
            pltpu.VMEM(mine.shape, jnp.bfloat16),
            pltpu.VMEM(gain.shape, jnp.bfloat16),
            pltpu.VMEM((chunks, depth, chunk), jnp.bfloat16),
            pltpu.VMEM((seqs * colors * steps * (group + 4), HD), jnp.float32),
            pltpu.SemaphoreType.DMA((chunks + 2,)),
        ],
        compiler_params=pltpu.CompilerParams(vmem_limit_bytes=28 * MIB),
        cost_estimate=pl.CostEstimate(
            flops=4 * half_rows * depth * (q_cols + 2 * kv_cols),
            bytes_accessed=2 * depth * (q_cols + 2 * kv_cols), transcendentals=0),
        name="project",
    )(place, in_hbm(mine), other, in_hbm(gain), in_vmem(early), in_vmem(wk), in_vmem(wv), in_hbm(wq))


def fetch_first_kernel(wq_ref, wk_ref, wv_ref, early_ref, wk_out, wv_out, sems):
    copies = [
        pltpu.make_async_copy(wk_ref, wk_out, sems.at[0]),
        pltpu.make_async_copy(wv_ref, wv_out, sems.at[1]),
        pltpu.make_async_copy(wq_ref.at[:, :early_ref.shape[1]], early_ref, sems.at[2])]
    for copy in copies:
        copy.start()
    for copy in copies:
        copy.wait()


def fetch_first(wq, wk, wv, early):
    hbm = pl.BlockSpec(memory_space=pltpu.HBM)
    vmem = pl.BlockSpec(memory_space=pltpu.VMEM)
    depth = wq.shape[0]
    return pl.pallas_call(
        fetch_first_kernel,
        out_shape=(
            pltpu.VMEM((depth, early), wq.dtype), pltpu.VMEM(wk.shape, wk.dtype), pltpu.VMEM(wv.shape, wv.dtype)),
        in_specs=[hbm] * 3,
        out_specs=(vmem,) * 3,
        scratch_shapes=[pltpu.SemaphoreType.DMA((3,))],
        compiler_params=pltpu.CompilerParams(vmem_limit_bytes=16 * MIB),
        cost_estimate=pl.CostEstimate(
            flops=0, bytes_accessed=2 * depth * (early + 2 * wk.shape[1]), transcendentals=0),
        name="fetch_first",
    )(in_hbm(wq), in_hbm(wk), in_hbm(wv))


def notes_kernel(steps, position_ref, length_ref, after_ref, notes_ref):
    lane = lax.broadcasted_iota(jnp.int32, (1, HD), 1)
    frequency = rope_frequencies((lane % (HD // 2)).astype(jnp.float32), HD)
    sign = jnp.where(lane < HD // 2, -1.0, 1.0)
    for t in range(steps):
        angle = (position_ref[0] + t).astype(jnp.float32) * frequency
        notes_ref[2 * t:2 * t + 1, :] = jnp.cos(angle)
        notes_ref[2 * t + 1:2 * t + 2, :] = jnp.sin(angle) * sign
    length = length_ref[0].astype(jnp.float32)
    notes_ref[2 * steps:, :] = jnp.full((notes_ref.shape[0] - 2 * steps, HD), length)


def take_notes(position, length, after, steps):
    smem = pl.BlockSpec(memory_space=pltpu.SMEM)
    return pl.pallas_call(
        functools.partial(notes_kernel, steps),
        out_shape=jax.ShapeDtypeStruct((2 * steps + 4, HD), jnp.float32),
        in_specs=[smem, smem, pl.BlockSpec(memory_space=pl.ANY)],
        out_specs=pl.BlockSpec(memory_space=pltpu.VMEM),
        compiler_params=pltpu.CompilerParams(vmem_limit_bytes=4 * MIB),
        name="notes",
    )(position, length, after)


def combine_kernel(arrived, parts, *refs):
    total = refs[0][...]
    for ref in refs[1:arrived + 1]:
        total = total + ref[...].astype(jnp.float32)
    count = total.shape[0] // parts
    for i, ref in enumerate(refs[-parts:]):
        ref[...] = total[i * count:(i + 1) * count].astype(ref.dtype)


def combine(keep, came, held, after, parts):
    vmem = pl.BlockSpec(memory_space=pltpu.VMEM)
    out_shape = part_shapes(keep.shape[0], parts, keep.shape[1:])
    return pl.pallas_call(
        functools.partial(combine_kernel, len(came), parts),
        out_shape=out_shape,
        in_specs=[vmem] * (1 + len(came)) + [pl.BlockSpec(memory_space=pl.ANY)] * (1 + len(held)),
        out_specs=(vmem,) * parts,
        compiler_params=pltpu.CompilerParams(vmem_limit_bytes=24 * MIB),
        name="combine",
    )(keep, *came, after, *[in_vmem(piece) for piece in held])


def fetch_kernel(first, parts, weight_ref, *rest):
    held_ref, sems = rest[-2:]
    rows = held_ref.shape[0] // parts
    copies = [
        pltpu.make_async_copy(
            weight_ref.at[first + c * rows:first + (c + 1) * rows],
            held_ref.at[c * rows:(c + 1) * rows], sems.at[c])
        for c in range(parts)]
    for copy in copies:
        copy.start()
    for copy in copies:
        copy.wait()


def fetch(weight, first, rows, after):
    parts = 4
    return pl.pallas_call(
        functools.partial(fetch_kernel, first, parts),
        out_shape=pltpu.VMEM((rows, weight.shape[1]), weight.dtype),
        in_specs=[pl.BlockSpec(memory_space=pltpu.HBM)] + [pl.BlockSpec(memory_space=pl.ANY)] * len(after),
        out_specs=pl.BlockSpec(memory_space=pltpu.VMEM),
        scratch_shapes=[pltpu.SemaphoreType.DMA((parts,))],
        compiler_params=pltpu.CompilerParams(vmem_limit_bytes=16 * MIB),
        cost_estimate=pl.CostEstimate(
            flops=0, bytes_accessed=2 * rows * weight.shape[1], transcendentals=0),
        name="fetch",
    )(in_hbm(weight), *after)


def attend_kernel(steps, width, unused, place_ref, table_ref, keys_ref, values_ref, *rest):
    rest = rest[unused:]
    part_refs, (same_ref, cross_ref, new_keys_ref, new_values_ref) = rest[:-4], rest[-4:]
    kv_heads = keys_ref.shape[1] // HD
    half_kv = kv_heads // 2
    pitch = part_refs[0].shape[1] // (half_kv * steps)
    group = pitch - 4
    slots = keys_ref.shape[0]
    factor = 1.0 / math.sqrt(HD)
    low_side = place_ref[0] % 2 == 0
    same, cross = [
        functools.reduce(jnp.add, [ref[0].astype(jnp.float32) for ref in part_refs[i::2]]) for i in range(2)]
    halves = [jnp.where(low_side, same, cross), jnp.where(low_side, cross, same)]
    per_head = steps * group
    lanes = kv_heads * per_head
    fresh_rows = 16
    fresh_keys = [[None] * kv_heads for _ in range(steps)]
    fresh_values = [[None] * kv_heads for _ in range(steps)]
    queries = [None] * kv_heads
    for k in range(half_kv):
        for g in range(2):
            head = g * half_kv + k
            query = []
            for t in range(steps):
                rows = halves[g][(k * steps + t) * pitch:(k * steps + t + 1) * pitch]
                squares = rows[group + 2:group + 3] + rows[group + 3:group + 4]
                rows = rows * lax.rsqrt(squares / width + epsilon)
                cosine = table_ref[2 * t:2 * t + 1, :]
                sine = table_ref[2 * t + 1:2 * t + 2, :]
                turned = rows * cosine + pltpu.roll(rows, HD // 2, 1) * sine
                query.append(turned[:group])
                fresh_keys[t][head] = turned[group:group + 1]
                fresh_values[t][head] = rows[group + 1:group + 2]
            blocks = [jnp.zeros((per_head, HD), jnp.float32)] * kv_heads
            blocks[head] = jnp.concatenate(query, axis=0)
            queries[head] = jnp.concatenate(blocks, axis=1)
    queries = jnp.concatenate(queries, axis=0).astype(jnp.bfloat16)
    padding = jnp.zeros((fresh_rows - steps, kv_heads * HD), jnp.float32)
    fresh_keys, fresh_values = [
        jnp.concatenate([jnp.concatenate(row, axis=1) for row in fresh] + [padding], axis=0).astype(jnp.bfloat16)
        for fresh in (fresh_keys, fresh_values)]
    new_keys_ref[...] = fresh_keys[:steps]
    new_values_ref[...] = fresh_values[:steps]

    length = table_ref[2 * steps:2 * steps + 1, :1].astype(jnp.int32)
    live = lax.broadcasted_iota(jnp.int32, (slots, lanes), 0) < length
    lane_step = (lax.broadcasted_iota(jnp.int32, (fresh_rows, lanes), 1) % per_head) // group
    seen = lax.broadcasted_iota(jnp.int32, (fresh_rows, lanes), 0) <= lane_step
    over_last, over_first = (((1,), (1,)), ((), ())), (((0,), (0,)), ((), ()))
    scores = lax.dot_general(keys_ref[...], queries, over_last, preferred_element_type=jnp.float32) * factor
    scores = jnp.where(live, scores, -jnp.inf)
    fresh = lax.dot_general(fresh_keys, queries, over_last, preferred_element_type=jnp.float32) * factor
    fresh = jnp.where(seen, fresh, -jnp.inf)
    top = jnp.maximum(jnp.max(scores, axis=0, keepdims=True), jnp.max(fresh, axis=0, keepdims=True))
    scores = jnp.exp(scores - top)
    fresh = jnp.exp(fresh - top)
    inverse = 1.0 / (jnp.sum(scores, axis=0, keepdims=True) + jnp.sum(fresh, axis=0, keepdims=True))
    weights = (scores * inverse).astype(jnp.bfloat16)
    fresh = (fresh * inverse).astype(jnp.bfloat16)
    mixed = lax.dot_general(weights, values_ref[...], over_first, preferred_element_type=jnp.float32)
    mixed = mixed + lax.dot_general(fresh, fresh_values, over_first, preferred_element_type=jnp.float32)
    contexts = [
        mixed[head * per_head:(head + 1) * per_head, head * HD:(head + 1) * HD] for head in range(kv_heads)]
    for k in range(half_kv):
        lower, upper = contexts[k], contexts[half_kv + k]
        span = slice(k * steps * group, (k + 1) * steps * group)
        same_ref[0, span, :] = jnp.where(low_side, lower, upper).astype(jnp.bfloat16)
        cross_ref[0, span, :] = jnp.where(low_side, upper, lower).astype(jnp.bfloat16)


def attend(place, parts, table, keys, values, held, steps, width, half_heads):
    vmem = pl.BlockSpec(memory_space=pltpu.VMEM)
    smem = pl.BlockSpec(memory_space=pltpu.SMEM)
    kv_cols = keys.shape[1]
    half = jax.ShapeDtypeStruct((1, steps * half_heads, HD), jnp.bfloat16)
    fresh = jax.ShapeDtypeStruct((steps, kv_cols), jnp.bfloat16)
    return pl.pallas_call(
        functools.partial(attend_kernel, steps, width, len(held)),
        out_shape=(half, half, fresh, fresh),
        in_specs=[smem] + [vmem] * 3 + [pl.BlockSpec(memory_space=pl.ANY)] * len(held) + [vmem] * len(parts),
        out_specs=(vmem,) * 4,
        compiler_params=pltpu.CompilerParams(vmem_limit_bytes=16 * MIB),
        name="attend",
    )(place, table, keys, values, *[in_vmem(piece) for piece in held], *parts)


def join_kernel(arrived, *refs):
    out_ref = refs[-1]
    for i, ref in enumerate(refs[:arrived + 1]):
        count = ref.shape[0]
        out_ref[i * count:(i + 1) * count] = ref[...]


def local_call(kernel, shape, arrays, held=()):
    vmem = pl.BlockSpec(memory_space=pltpu.VMEM)
    return pl.pallas_call(
        kernel,
        out_shape=jax.ShapeDtypeStruct(shape, jnp.bfloat16),
        in_specs=[vmem] * len(arrays) + [pl.BlockSpec(memory_space=pl.ANY)] * len(held),
        out_specs=vmem,
        compiler_params=pltpu.CompilerParams(vmem_limit_bytes=16 * MIB),
        name="local",
    )(*arrays, *[in_vmem(piece) for piece in held])


def output_kernel(steps, colors, patterns, pieces, place_ref, *rest):
    weight_refs, context_refs = rest[:pieces], rest[pieces:-4]
    mine_ref, other_ref, wide_buf, rows_buf = rest[-4:]
    device = place_ref[0]
    devices = len(patterns)
    half_seqs = devices // 2
    count, block, _ = context_refs[0].shape
    group = block // (steps * colors)
    for j, pattern in enumerate(patterns):
        rows = context_refs[j // count][j % count]
        start = pl.multiple_of((device ^ pattern) * block, 8)
        wide_buf[pl.ds(start, block), :] = rows.astype(jnp.float32)
    for head in range(colors * group):
        color, h = head // group, head % group
        lines = []
        for g in range(2):
            for t in range(steps):
                start = g * half_seqs * block + (color * steps + t) * group + h
                lines.append(wide_buf[pl.ds(start, half_seqs, stride=block), :])
        rows_buf[:, head * HD:(head + 1) * HD] = jnp.concatenate(lines, axis=0).astype(jnp.bfloat16)
    low_side = device % 2 == 0
    half = rows_buf.shape[0] // 2
    columns = mine_ref.shape[1]
    chunk = min(columns, 512)
    for c in range(columns // chunk):
        span = slice(c * chunk, (c + 1) * chunk)
        product, first = None, 0
        for weight_ref in weight_refs:
            last = first + weight_ref.shape[0]
            part = jnp.dot(rows_buf[:, first:last], weight_ref[:, span], preferred_element_type=jnp.float32)
            product = part if product is None else product + part
            first = last
        lower, upper = product[:half], product[half:]
        mine_ref[:, span] = jnp.where(low_side, lower, upper)
        other_ref[:, span] = jnp.where(low_side, upper, lower).astype(jnp.bfloat16)


def output(place, contexts, patterns, held, steps, colors):
    columns = held[0].shape[1]
    depth = sum(piece.shape[0] for piece in held)
    devices = len(patterns)
    half = devices * steps // 2
    vmem = pl.BlockSpec(memory_space=pltpu.VMEM)
    smem = pl.BlockSpec(memory_space=pltpu.SMEM)
    return pl.pallas_call(
        functools.partial(output_kernel, steps, colors, patterns, len(held)),
        out_shape=(
            jax.ShapeDtypeStruct((half, columns), jnp.float32),
            jax.ShapeDtypeStruct((half, columns), jnp.bfloat16),
        ),
        in_specs=[smem] + [vmem] * (len(held) + len(contexts)),
        out_specs=(vmem, vmem),
        scratch_shapes=[
            pltpu.VMEM((devices * contexts[0].shape[1], HD), jnp.float32),
            pltpu.VMEM((devices * steps, depth), jnp.bfloat16),
        ],
        compiler_params=pltpu.CompilerParams(vmem_limit_bytes=26 * MIB),
        cost_estimate=pl.CostEstimate(
            flops=2 * devices * steps * depth * columns,
            bytes_accessed=2 * depth * columns, transcendentals=0),
        name="output",
    )(place, *[in_vmem(piece) for piece in held], *contexts)


def body(hidden_in, norm_gain, query_weight, key_weight, value_weight, out_weight,
         cache_keys, cache_values, lengths, positions):
    steps, half_seqs, depth = hidden_in.shape
    everyone = ("gx", "gy")
    devices = lax.axis_size(everyone)
    bits = devices.bit_length() - 1
    colors = key_weight.shape[1] // HD
    half_heads = query_weight.shape[1] // HD
    group = half_heads // colors
    place = lax.axis_index(everyone).astype(jnp.int32).reshape(1)

    def partner(array, pattern):
        return lax.ppermute(array, everyone, [(i, i ^ pattern) for i in range(devices)])

    stages = [list(range(first, min(first + 2, bits))) for first in range(1, bits, 2)]
    stages[-1] = stages[-1] + [0]
    order = [bit for stage in stages for bit in stage]
    total = out_weight.shape[0]
    cuts = [total * i // 8 for i in (0, 3, 4, 8)]
    held = []

    def fetch_next(window, after):
        i = len(held)
        if window not in (1, 2, 3):
            return []
        held.append(fetch(out_weight, cuts[i], cuts[i + 1] - cuts[i], after))
        return held[-1:]

    mine = hidden_in.reshape(steps * half_seqs, depth)
    other = partner(mine, 1)
    early, wk, wv = fetch_first(query_weight, key_weight, value_weight, 512)
    parts = project(
        place, mine, other, norm_gain.reshape(-1, HD), early, wk, wv, query_weight,
        steps, group, colors, order, 1 << len(stages[0]))
    notes = take_notes(positions, lengths, parts[1], steps)
    for i, stage in enumerate(stages):
        came = [partner(part, pattern) for part, pattern in zip(parts[1:], slot_patterns(stage)[1:])]
        now = fetch_next(i, [parts[1], notes])
        if i < len(stages) - 1:
            parts = combine(parts[0], came, now, notes, 1 << len(stages[i + 1]))
    same, cross, new_keys, new_values = attend(
        place, [parts[0], *came], notes, cache_keys[0], cache_values[0], now,
        steps, depth * lax.axis_size("gx"), half_heads)

    context, patterns = None, [0]
    for i, stage in enumerate(stages[::-1]):
        moves = slot_patterns(stage)
        if i == 0:
            context = same
            came = [partner(cross if move & 1 else same, move) for move in moves[1:]]
        else:
            came = [partner(context, move) for move in moves[1:]]
        patterns = [p ^ move for move in moves for p in patterns]
        now = fetch_next(len(stages) + i, [context])
        if i < len(stages) - 1:
            shape = (len(moves) * context.shape[0],) + context.shape[1:]
            context = local_call(functools.partial(join_kernel, len(came)), shape, [context, *came], now)
    mine, other = output(place, [context, *came], patterns, held, steps, colors)
    other = partner(other, 1)
    result = (mine + other.astype(jnp.float32)).astype(jnp.bfloat16)
    return (
        result.reshape(steps, half_seqs, -1),
        new_keys[:, None, :],
        new_values[:, None, :],
    )


def solution(mesh):
    in_specs = (
        P(None, ("rep", "gy"), "gx"),
        P("gx"),
        P("gx", "gy"),
        P("gx", "gy"),
        P("gx", "gy"),
        P("gy", "gx"),
        P(("rep", "gx", "gy"), None, None),
        P(("rep", "gx", "gy"), None, None),
        P(("rep", "gx", "gy")),
        P(("rep", "gx", "gy")),
    )
    out_specs = (
        P(None, ("rep", "gy"), "gx"),
        P(None, ("rep", "gx", "gy"), None),
        P(None, ("rep", "gx", "gy"), None),
    )
    return jax.shard_map(body, mesh=mesh, in_specs=in_specs, out_specs=out_specs, check_vma=False)
```

```python
import functools
import math

import jax
import jax.numpy as jnp
from jax import lax
from jax.experimental import pallas as pl
from jax.experimental.pallas import tpu as pltpu
from jax.sharding import PartitionSpec as P

HD = 128
epsilon = 1e-05
rope_theta = 500000.0
MIB = 1024 * 1024


def rope_frequencies(index, head_size):
    frequency = jnp.exp(-math.log(rope_theta) * 2.0 * index / head_size)
    wavelength = 2.0 * math.pi / frequency
    smooth = (8192.0 / wavelength - 1.0) / 3.0
    blended = (1.0 - smooth) * frequency / 8.0 + smooth * frequency
    adjusted = jnp.where(wavelength > 8192.0, frequency / 8.0, blended)
    return jnp.where(wavelength < 2048.0, frequency, adjusted)


def slot_patterns(order):
    count = len(order)
    return [
        sum(((j >> (count - 1 - i)) & 1) << bit for i, bit in enumerate(order))
        for j in range(1 << count)]


def in_hbm(array):
    return pltpu.with_memory_space_constraint(array, pltpu.HBM)


def in_vmem(array):
    return pltpu.with_memory_space_constraint(array, pltpu.VMEM)


def project_kernel(steps, group, colors, order, chunk, place_ref, mine_ref, other_ref, gain_ref, early_ref, wk_ref, wv_ref,
                   wq_ref, keys_ref, values_ref, own_ref, send_ref, *rest):
    part_refs, rest = rest[:-5], rest[-5:]
    mine_buf, gain_buf, wq_buf, rows_buf, sems = rest
    early = early_ref.shape[1]
    q_cols = wq_ref.shape[1]
    chunks = (q_cols - early) // chunk
    copies = [pltpu.make_async_copy(mine_ref, mine_buf, sems.at[chunks]),
              pltpu.make_async_copy(gain_ref, gain_buf, sems.at[chunks + 1])]
    for c in range(chunks):
        copies.append(pltpu.make_async_copy(
            wq_ref.at[:, early + c * chunk:early + (c + 1) * chunk], wq_buf.at[c], sems.at[c]))
    device = place_ref[0]
    slots, kv_half = keys_ref.shape[0], keys_ref.shape[1] // 2
    for i, source in enumerate((keys_ref, values_ref)):
        for j, (target, part) in enumerate(((send_ref, 1 - device % 2), (own_ref, device % 2))):
            first = pl.multiple_of(part * kv_half, HD)
            copies.append(pltpu.make_async_copy(
                source.at[:, pl.ds(first, kv_half)], target.at[i * slots:(i + 1) * slots],
                sems.at[chunks + 2 + 2 * i + j]))
    for copy in copies:
        copy.start()

    half_rows = mine_ref.shape[0]
    total_rows = 2 * half_rows
    half_seqs = half_rows // steps
    pitch = group + 4
    stride = colors * steps * pitch

    def spread(color, row, block):
        for g in range(2):
            for t in range(steps):
                first = (g * steps + t) * half_seqs
                start = g * half_seqs * stride + (color * steps + t) * pitch + row
                rows_buf[pl.ds(start, half_seqs, stride=stride), :] = block[first:first + half_seqs, :]

    low_side = device % 2 == 0
    copies[0].wait()
    copies[1].wait()
    mine = mine_buf[...].astype(jnp.float32)
    other = other_ref[...].astype(jnp.float32)
    x = jnp.concatenate(
        [jnp.where(low_side, mine, other), jnp.where(low_side, other, mine)], axis=0)
    gain = gain_buf[...].astype(jnp.float32)
    gain = jnp.concatenate([gain[i:i + 1] for i in range(gain.shape[0])], axis=1)
    scaled = (x * gain).astype(jnp.bfloat16)
    squares = jnp.sum(x * x, axis=-1, keepdims=True)
    high = squares.astype(jnp.bfloat16).astype(jnp.float32)
    low = squares - high
    for color in range(colors):
        spread(color, group + 2, jnp.broadcast_to(high, (total_rows, HD)))
        spread(color, group + 3, jnp.broadcast_to(low, (total_rows, HD)))

    def multiply(weights, place_of_head):
        product = jnp.dot(scaled, weights, preferred_element_type=jnp.float32)
        for i in range(product.shape[1] // HD):
            spread(*place_of_head(i), product[:, i * HD:(i + 1) * HD])

    multiply(wk_ref[...], lambda i: (i, group))
    multiply(wv_ref[...], lambda i: (i, group + 1))
    multiply(early_ref[...], lambda i: (i // group, i % group))

    for c in range(chunks):
        copies[2 + c].wait()
        first = (early + c * chunk) // HD
        multiply(wq_buf[c], lambda i: ((first + i) // group, (first + i) % group))
    for copy in copies[2 + chunks:]:
        copy.wait()
    per_part = part_refs[0].shape[0]
    for slot, pattern in enumerate(slot_patterns(order)):
        ref = part_refs[slot // per_part]
        start = pl.multiple_of((device ^ pattern) * stride, 8)
        ref[slot % per_part] = rows_buf[pl.ds(start, stride), :].astype(ref.dtype)


def part_shapes(total, count, block):
    shape = (total // count,) + block
    return (jax.ShapeDtypeStruct(shape, jnp.float32),) + (jax.ShapeDtypeStruct(shape, jnp.bfloat16),) * (count - 1)


def project(place, mine, other, gain, early, wk, wv, wq, keys, values, steps, group, colors, order, count):
    half_rows, depth = mine.shape
    q_cols, kv_cols = wq.shape[1], wk.shape[1]
    seqs = 2 * half_rows // steps
    chunk = 512
    chunks = (q_cols - early.shape[1]) // chunk
    vmem = pl.BlockSpec(memory_space=pltpu.VMEM)
    smem = pl.BlockSpec(memory_space=pltpu.SMEM)
    hbm = pl.BlockSpec(memory_space=pltpu.HBM)
    cache = jax.ShapeDtypeStruct((2 * keys.shape[0], keys.shape[1] // 2), jnp.bfloat16)
    out_shape = (cache, cache) + part_shapes(
        seqs, count, (colors * steps * (group + 4), HD))
    return pl.pallas_call(
        functools.partial(project_kernel, steps, group, colors, order, chunk),
        out_shape=out_shape,
        in_specs=[smem, hbm, vmem, hbm, vmem, vmem, vmem, hbm, hbm, hbm],
        out_specs=(vmem,) * len(out_shape),
        scratch_shapes=[
            pltpu.VMEM(mine.shape, jnp.bfloat16),
            pltpu.VMEM(gain.shape, jnp.bfloat16),
            pltpu.VMEM((chunks, depth, chunk), jnp.bfloat16),
            pltpu.VMEM((seqs * colors * steps * (group + 4), HD), jnp.float32),
            pltpu.SemaphoreType.DMA((chunks + 6,)),
        ],
        compiler_params=pltpu.CompilerParams(vmem_limit_bytes=28 * MIB),
        cost_estimate=pl.CostEstimate(
            flops=4 * half_rows * depth * (q_cols + 2 * kv_cols),
            bytes_accessed=2 * depth * (q_cols + 2 * kv_cols), transcendentals=0),
        name="project",
    )(place, in_hbm(mine), other, in_hbm(gain), in_vmem(early), in_vmem(wk), in_vmem(wv), in_hbm(wq),
      in_hbm(keys), in_hbm(values))


def fetch_first_kernel(wq_ref, wk_ref, wv_ref, early_ref, wk_out, wv_out, sems):
    copies = [
        pltpu.make_async_copy(wk_ref, wk_out, sems.at[0]),
        pltpu.make_async_copy(wv_ref, wv_out, sems.at[1]),
        pltpu.make_async_copy(wq_ref.at[:, :early_ref.shape[1]], early_ref, sems.at[2])]
    for copy in copies:
        copy.start()
    for copy in copies:
        copy.wait()


def fetch_first(wq, wk, wv, early):
    hbm = pl.BlockSpec(memory_space=pltpu.HBM)
    vmem = pl.BlockSpec(memory_space=pltpu.VMEM)
    depth = wq.shape[0]
    return pl.pallas_call(
        fetch_first_kernel,
        out_shape=(
            pltpu.VMEM((depth, early), wq.dtype), pltpu.VMEM(wk.shape, wk.dtype), pltpu.VMEM(wv.shape, wv.dtype)),
        in_specs=[hbm] * 3,
        out_specs=(vmem,) * 3,
        scratch_shapes=[pltpu.SemaphoreType.DMA((3,))],
        compiler_params=pltpu.CompilerParams(vmem_limit_bytes=16 * MIB),
        cost_estimate=pl.CostEstimate(
            flops=0, bytes_accessed=2 * depth * (early + 2 * wk.shape[1]), transcendentals=0),
        name="fetch_first",
    )(in_hbm(wq), in_hbm(wk), in_hbm(wv))


def notes_kernel(steps, position_ref, length_ref, after_ref, notes_ref):
    lane = lax.broadcasted_iota(jnp.int32, (1, HD), 1)
    frequency = rope_frequencies((lane % (HD // 2)).astype(jnp.float32), HD)
    sign = jnp.where(lane < HD // 2, -1.0, 1.0)
    for t in range(steps):
        angle = (position_ref[0] + t).astype(jnp.float32) * frequency
        notes_ref[2 * t:2 * t + 1, :] = jnp.cos(angle)
        notes_ref[2 * t + 1:2 * t + 2, :] = jnp.sin(angle) * sign
    length = length_ref[0].astype(jnp.float32)
    notes_ref[2 * steps:, :] = jnp.full((notes_ref.shape[0] - 2 * steps, HD), length)


def take_notes(position, length, after, steps):
    smem = pl.BlockSpec(memory_space=pltpu.SMEM)
    return pl.pallas_call(
        functools.partial(notes_kernel, steps),
        out_shape=jax.ShapeDtypeStruct((2 * steps + 4, HD), jnp.float32),
        in_specs=[smem, smem, pl.BlockSpec(memory_space=pl.ANY)],
        out_specs=pl.BlockSpec(memory_space=pltpu.VMEM),
        compiler_params=pltpu.CompilerParams(vmem_limit_bytes=4 * MIB),
        name="notes",
    )(position, length, after)


def combine_kernel(arrived, parts, *refs):
    total = refs[0][...]
    for ref in refs[1:arrived + 1]:
        total = total + ref[...].astype(jnp.float32)
    count = total.shape[0] // parts
    for i, ref in enumerate(refs[-parts:]):
        ref[...] = total[i * count:(i + 1) * count].astype(ref.dtype)


def combine(keep, came, held, after, parts):
    vmem = pl.BlockSpec(memory_space=pltpu.VMEM)
    out_shape = part_shapes(keep.shape[0], parts, keep.shape[1:])
    return pl.pallas_call(
        functools.partial(combine_kernel, len(came), parts),
        out_shape=out_shape,
        in_specs=[vmem] * (1 + len(came)) + [pl.BlockSpec(memory_space=pl.ANY)] * (1 + len(held)),
        out_specs=(vmem,) * parts,
        compiler_params=pltpu.CompilerParams(vmem_limit_bytes=24 * MIB),
        name="combine",
    )(keep, *came, after, *[in_vmem(piece) for piece in held])


def fetch_kernel(first, parts, weight_ref, *rest):
    held_ref, sems = rest[-2:]
    rows = held_ref.shape[0] // parts
    copies = [
        pltpu.make_async_copy(
            weight_ref.at[first + c * rows:first + (c + 1) * rows],
            held_ref.at[c * rows:(c + 1) * rows], sems.at[c])
        for c in range(parts)]
    for copy in copies:
        copy.start()
    for copy in copies:
        copy.wait()


def fetch(weight, first, rows, after):
    parts = 4
    return pl.pallas_call(
        functools.partial(fetch_kernel, first, parts),
        out_shape=pltpu.VMEM((rows, weight.shape[1]), weight.dtype),
        in_specs=[pl.BlockSpec(memory_space=pltpu.HBM)] + [pl.BlockSpec(memory_space=pl.ANY)] * len(after),
        out_specs=pl.BlockSpec(memory_space=pltpu.VMEM),
        scratch_shapes=[pltpu.SemaphoreType.DMA((parts,))],
        compiler_params=pltpu.CompilerParams(vmem_limit_bytes=16 * MIB),
        cost_estimate=pl.CostEstimate(
            flops=0, bytes_accessed=2 * rows * weight.shape[1], transcendentals=0),
        name="fetch",
    )(in_hbm(weight), *after)


def attend_kernel(steps, width, unused, notes_ref, came_notes_ref, own_ref, came_ref, *rest):
    part_refs, (context_ref, fresh_ref, fresh_send_ref) = rest[unused:-3], rest[-3:]
    slots = own_ref.shape[0] // 2
    half_kv = own_ref.shape[1] // HD
    total = functools.reduce(jnp.add, [ref[...].astype(jnp.float32) for ref in part_refs])
    pitch = total.shape[1] // (half_kv * steps)
    group = pitch - 4
    factor = 1.0 / math.sqrt(HD)
    per_head = steps * group
    groups = 2 * half_kv
    lanes = groups * per_head
    fresh_rows = 16
    notes = [notes_ref[...], came_notes_ref[...]]
    fresh_keys = [[None] * groups for _ in range(steps)]
    fresh_values = [[None] * groups for _ in range(steps)]
    queries = []
    for seq in range(2):
        for k in range(half_kv):
            index = seq * half_kv + k
            query = []
            for t in range(steps):
                rows = total[seq, (k * steps + t) * pitch:(k * steps + t + 1) * pitch]
                squares = rows[group + 2:group + 3] + rows[group + 3:group + 4]
                rows = rows * lax.rsqrt(squares / width + epsilon)
                cosine = notes[seq][2 * t:2 * t + 1]
                sine = notes[seq][2 * t + 1:2 * t + 2]
                turned = rows * cosine + pltpu.roll(rows, HD // 2, 1) * sine
                query.append(turned[:group])
                fresh_keys[t][index] = turned[group:group + 1]
                fresh_values[t][index] = rows[group + 1:group + 2]
            blocks = [jnp.zeros((per_head, HD), jnp.float32)] * groups
            blocks[index] = jnp.concatenate(query, axis=0)
            queries.append(jnp.concatenate(blocks, axis=1))
    queries = jnp.concatenate(queries, axis=0).astype(jnp.bfloat16)
    keys_now, values_now = [
        jnp.concatenate([jnp.concatenate(row, axis=1) for row in fresh], axis=0)
        for fresh in (fresh_keys, fresh_values)]
    half = half_kv * HD
    for seq, ref in enumerate((fresh_ref, fresh_send_ref)):
        span = slice(seq * half, (seq + 1) * half)
        ref[...] = jnp.concatenate(
            [keys_now[:, span], values_now[:, span], jnp.zeros((fresh_rows - 2 * steps, half), jnp.float32)],
            axis=0).astype(jnp.bfloat16)
    padding = jnp.zeros((fresh_rows - steps, groups * HD), jnp.float32)
    keys_now, values_now = [
        jnp.concatenate([fresh, padding], axis=0).astype(jnp.bfloat16) for fresh in (keys_now, values_now)]

    keys = jnp.concatenate([own_ref[:slots, :], came_ref[:slots, :]], axis=1)
    values = jnp.concatenate([own_ref[slots:, :], came_ref[slots:2 * slots, :]], axis=1)
    lane = lax.broadcasted_iota(jnp.int32, (1, lanes), 1)
    lengths = [note[2 * steps:2 * steps + 1, :1].astype(jnp.int32) for note in notes]
    length = jnp.where(lane < half_kv * per_head, lengths[0], lengths[1])
    live = lax.broadcasted_iota(jnp.int32, (slots, lanes), 0) < length
    seen = lax.broadcasted_iota(jnp.int32, (fresh_rows, lanes), 0) <= (lane % per_head) // group
    over_last, over_first = (((1,), (1,)), ((), ())), (((0,), (0,)), ((), ()))
    scores = lax.dot_general(keys, queries, over_last, preferred_element_type=jnp.float32) * factor
    scores = jnp.where(live, scores, -jnp.inf)
    fresh = lax.dot_general(keys_now, queries, over_last, preferred_element_type=jnp.float32) * factor
    fresh = jnp.where(seen, fresh, -jnp.inf)
    top = jnp.maximum(jnp.max(scores, axis=0, keepdims=True), jnp.max(fresh, axis=0, keepdims=True))
    scores = jnp.exp(scores - top)
    fresh = jnp.exp(fresh - top)
    inverse = 1.0 / (jnp.sum(scores, axis=0, keepdims=True) + jnp.sum(fresh, axis=0, keepdims=True))
    weights = (scores * inverse).astype(jnp.bfloat16)
    fresh = (fresh * inverse).astype(jnp.bfloat16)
    mixed = lax.dot_general(weights, values, over_first, preferred_element_type=jnp.float32)
    mixed = mixed + lax.dot_general(fresh, values_now, over_first, preferred_element_type=jnp.float32)
    for index in range(groups):
        seq, k = index // half_kv, index % half_kv
        context_ref[seq, k * per_head:(k + 1) * per_head, :] = mixed[
            index * per_head:(index + 1) * per_head, index * HD:(index + 1) * HD].astype(jnp.bfloat16)


def attend(notes, came_notes, own, came, parts, held, steps, width, half_heads):
    vmem = pl.BlockSpec(memory_space=pltpu.VMEM)
    fresh = jax.ShapeDtypeStruct((16, own.shape[1]), jnp.bfloat16)
    return pl.pallas_call(
        functools.partial(attend_kernel, steps, width, len(held)),
        out_shape=(jax.ShapeDtypeStruct((2, steps * half_heads, HD), jnp.bfloat16), fresh, fresh),
        in_specs=[vmem] * 4 + [pl.BlockSpec(memory_space=pl.ANY)] * len(held) + [vmem] * len(parts),
        out_specs=(vmem,) * 3,
        compiler_params=pltpu.CompilerParams(vmem_limit_bytes=16 * MIB),
        name="attend",
    )(notes, came_notes, own, came, *[in_vmem(piece) for piece in held], *parts)


def join_kernel(arrived, *refs):
    out_ref = refs[-1]
    for i, ref in enumerate(refs[:arrived + 1]):
        count = ref.shape[0]
        out_ref[i * count:(i + 1) * count] = ref[...]


def local_call(kernel, shape, arrays, held=()):
    vmem = pl.BlockSpec(memory_space=pltpu.VMEM)
    return pl.pallas_call(
        kernel,
        out_shape=jax.ShapeDtypeStruct(shape, jnp.bfloat16),
        in_specs=[vmem] * len(arrays) + [pl.BlockSpec(memory_space=pl.ANY)] * len(held),
        out_specs=vmem,
        compiler_params=pltpu.CompilerParams(vmem_limit_bytes=16 * MIB),
        name="local",
    )(*arrays, *[in_vmem(piece) for piece in held])


def output_kernel(steps, colors, patterns, pieces, place_ref, fresh_ref, *rest):
    weight_refs, context_refs = rest[:pieces], rest[pieces:-4]
    mine_ref, other_ref, wide_buf, rows_buf = rest[-4:]
    device = place_ref[0]
    devices = len(patterns)
    half_seqs = devices // 2
    count, block, _ = context_refs[0].shape
    group = block // (steps * colors)
    for j, pattern in enumerate(patterns):
        rows = context_refs[j // count][j % count]
        start = pl.multiple_of((device ^ pattern) * block, 8)
        wide_buf[pl.ds(start, block), :] = rows.astype(jnp.float32)
    for head in range(colors * group):
        color, h = head // group, head % group
        lines = []
        for g in range(2):
            for t in range(steps):
                start = g * half_seqs * block + (color * steps + t) * group + h
                lines.append(wide_buf[pl.ds(start, half_seqs, stride=block), :])
        rows_buf[:, head * HD:(head + 1) * HD] = jnp.concatenate(lines, axis=0).astype(jnp.bfloat16)
    low_side = device % 2 == 0
    half = rows_buf.shape[0] // 2
    other_ref[half:, :fresh_ref.shape[1]] = fresh_ref[...]
    if other_ref.shape[1] > fresh_ref.shape[1]:
        other_ref[half:, fresh_ref.shape[1]:] = jnp.zeros(
            (fresh_ref.shape[0], other_ref.shape[1] - fresh_ref.shape[1]), jnp.bfloat16)
    columns = mine_ref.shape[1]
    chunk = min(columns, 512)
    for c in range(columns // chunk):
        span = slice(c * chunk, (c + 1) * chunk)
        product, first = None, 0
        for weight_ref in weight_refs:
            last = first + weight_ref.shape[0]
            part = jnp.dot(rows_buf[:, first:last], weight_ref[:, span], preferred_element_type=jnp.float32)
            product = part if product is None else product + part
            first = last
        lower, upper = product[:half], product[half:]
        mine_ref[:, span] = jnp.where(low_side, lower, upper)
        other_ref[:half, span] = jnp.where(low_side, upper, lower).astype(jnp.bfloat16)


def output(place, fresh, contexts, patterns, held, steps, colors):
    columns = held[0].shape[1]
    depth = sum(piece.shape[0] for piece in held)
    devices = len(patterns)
    half = devices * steps // 2
    vmem = pl.BlockSpec(memory_space=pltpu.VMEM)
    smem = pl.BlockSpec(memory_space=pltpu.SMEM)
    return pl.pallas_call(
        functools.partial(output_kernel, steps, colors, patterns, len(held)),
        out_shape=(
            jax.ShapeDtypeStruct((half, columns), jnp.float32),
            jax.ShapeDtypeStruct((half + fresh.shape[0], columns), jnp.bfloat16),
        ),
        in_specs=[smem, vmem] + [vmem] * (len(held) + len(contexts)),
        out_specs=(vmem, vmem),
        scratch_shapes=[
            pltpu.VMEM((devices * contexts[0].shape[1], HD), jnp.float32),
            pltpu.VMEM((devices * steps, depth), jnp.bfloat16),
        ],
        compiler_params=pltpu.CompilerParams(vmem_limit_bytes=26 * MIB),
        cost_estimate=pl.CostEstimate(
            flops=2 * devices * steps * depth * columns,
            bytes_accessed=2 * depth * columns, transcendentals=0),
        name="output",
    )(place, fresh, *[in_vmem(piece) for piece in held], *contexts)


def finish_kernel(steps, place_ref, mine_ref, came_ref, fresh_ref, result_ref, new_keys_ref, new_values_ref):
    half = mine_ref.shape[0]
    result_ref[...] = (mine_ref[...] + came_ref[:half, :].astype(jnp.float32)).astype(jnp.bfloat16)
    own = fresh_ref[...].astype(jnp.float32)
    came = came_ref[half:, :own.shape[1]].astype(jnp.float32)
    low_side = place_ref[0] % 2 == 0
    rows = jnp.concatenate(
        [jnp.where(low_side, own, came), jnp.where(low_side, came, own)], axis=1).astype(jnp.bfloat16)
    new_keys_ref[...] = rows[:steps]
    new_values_ref[...] = rows[steps:2 * steps]


def finish(place, mine, came, fresh, steps):
    vmem = pl.BlockSpec(memory_space=pltpu.VMEM)
    new = jax.ShapeDtypeStruct((steps, 2 * fresh.shape[1]), jnp.bfloat16)
    return pl.pallas_call(
        functools.partial(finish_kernel, steps),
        out_shape=(jax.ShapeDtypeStruct(mine.shape, jnp.bfloat16), new, new),
        in_specs=[pl.BlockSpec(memory_space=pltpu.SMEM)] + [vmem] * 3,
        out_specs=(vmem,) * 3,
        compiler_params=pltpu.CompilerParams(vmem_limit_bytes=8 * MIB),
        name="finish",
    )(place, mine, came, fresh)


def body(hidden_in, norm_gain, query_weight, key_weight, value_weight, out_weight,
         cache_keys, cache_values, lengths, positions):
    steps, half_seqs, depth = hidden_in.shape
    everyone = ("gx", "gy")
    devices = lax.axis_size(everyone)
    bits = devices.bit_length() - 1
    colors = key_weight.shape[1] // HD
    half_heads = query_weight.shape[1] // HD
    group = half_heads // colors
    place = lax.axis_index(everyone).astype(jnp.int32).reshape(1)

    def partner(array, pattern):
        return lax.ppermute(array, everyone, [(i, i ^ pattern) for i in range(devices)])

    stages = [list(range(first, min(first + 2, bits))) for first in range(1, bits, 2)]
    order = [bit for stage in stages for bit in stage] + [0]
    total = out_weight.shape[0]
    cuts = [total * i // 8 for i in (0, 3, 4, 8)]
    held = []

    def fetch_next(window, after):
        i = len(held)
        if window not in (1, 2, 3):
            return []
        held.append(fetch(out_weight, cuts[i], cuts[i + 1] - cuts[i], after))
        return held[-1:]

    mine = hidden_in.reshape(steps * half_seqs, depth)
    other = partner(mine, 1)
    early, wk, wv = fetch_first(query_weight, key_weight, value_weight, 512)
    own, cache, *parts = project(
        place, mine, other, norm_gain.reshape(-1, HD), early, wk, wv, query_weight,
        cache_keys[0], cache_values[0],
        steps, group, colors, order, 1 << len(stages[0]))
    cache = partner(cache, 1)
    notes = take_notes(positions, lengths, parts[1], steps)
    came_notes = partner(notes, 1)
    for i, stage in enumerate(stages):
        came = [partner(part, pattern) for part, pattern in zip(parts[1:], slot_patterns(stage)[1:])]
        now = fetch_next(i, [parts[1], notes])
        if i < len(stages) - 1:
            parts = combine(parts[0], came, now, notes, 1 << len(stages[i + 1]))
    context, fresh, fresh_send = attend(
        notes, came_notes, own, cache, [parts[0], *came], now, steps, depth * lax.axis_size("gx"), half_heads)

    patterns = [0, 1]
    for i, stage in enumerate(stages[::-1]):
        moves = slot_patterns(stage)
        came = [partner(context, move) for move in moves[1:]]
        patterns = [p ^ move for move in moves for p in patterns]
        now = fetch_next(len(stages) + i, [context])
        if i < len(stages) - 1:
            shape = (len(moves) * context.shape[0],) + context.shape[1:]
            context = local_call(functools.partial(join_kernel, len(came)), shape, [context, *came], now)
    mine, other = output(place, fresh_send, [context, *came], patterns, held, steps, colors)
    result, new_keys, new_values = finish(place, mine, partner(other, 1), fresh, steps)
    return (
        result.reshape(steps, half_seqs, -1),
        new_keys[:, None, :],
        new_values[:, None, :],
    )


def solution(mesh):
    in_specs = (
        P(None, ("rep", "gy"), "gx"),
        P("gx"),
        P("gx", "gy"),
        P("gx", "gy"),
        P("gx", "gy"),
        P("gy", "gx"),
        P(("rep", "gx", "gy"), None, None),
        P(("rep", "gx", "gy"), None, None),
        P(("rep", "gx", "gy")),
        P(("rep", "gx", "gy")),
    )
    out_specs = (
        P(None, ("rep", "gy"), "gx"),
        P(None, ("rep", "gx", "gy"), None),
        P(None, ("rep", "gx", "gy"), None),
    )
    return jax.shard_map(body, mesh=mesh, in_specs=in_specs, out_specs=out_specs, check_vma=False)
```

```python
import functools
import math

import jax
import jax.numpy as jnp
from jax import lax
from jax.experimental import pallas as pl
from jax.experimental.pallas import tpu as pltpu
from jax.sharding import PartitionSpec as P

HD = 128
epsilon = 1e-05
rope_theta = 500000.0
MIB = 1024 * 1024


def rope_frequencies(index, head_size):
    frequency = jnp.exp(-math.log(rope_theta) * 2.0 * index / head_size)
    wavelength = 2.0 * math.pi / frequency
    smooth = (8192.0 / wavelength - 1.0) / 3.0
    blended = (1.0 - smooth) * frequency / 8.0 + smooth * frequency
    adjusted = jnp.where(wavelength > 8192.0, frequency / 8.0, blended)
    return jnp.where(wavelength < 2048.0, frequency, adjusted)


def slot_patterns(order):
    count = len(order)
    return [
        sum(((j >> (count - 1 - i)) & 1) << bit for i, bit in enumerate(order))
        for j in range(1 << count)]


def in_hbm(array):
    return pltpu.with_memory_space_constraint(array, pltpu.HBM)


def in_vmem(array):
    return pltpu.with_memory_space_constraint(array, pltpu.VMEM)


def project_kernel(steps, group, colors, order, chunk, place_ref, mine_ref, other_ref, gain_ref, early_ref, wk_ref, wv_ref,
                   wq_ref, keys_ref, values_ref, own_ref, send_ref, *rest):
    part_refs, rest = rest[:-5], rest[-5:]
    mine_buf, gain_buf, wq_buf, rows_buf, sems = rest
    early = early_ref.shape[1]
    q_cols = wq_ref.shape[1]
    chunks = (q_cols - early) // chunk
    copies = [pltpu.make_async_copy(mine_ref, mine_buf, sems.at[chunks]),
              pltpu.make_async_copy(gain_ref, gain_buf, sems.at[chunks + 1])]
    for c in range(chunks):
        copies.append(pltpu.make_async_copy(
            wq_ref.at[:, early + c * chunk:early + (c + 1) * chunk], wq_buf.at[c], sems.at[c]))
    device = place_ref[0]
    slots, kv_half = keys_ref.shape[0], keys_ref.shape[1] // 2
    for i, source in enumerate((keys_ref, values_ref)):
        for j, (target, part) in enumerate(((send_ref, 1 - device % 2), (own_ref, device % 2))):
            first = pl.multiple_of(part * kv_half, HD)
            copies.append(pltpu.make_async_copy(
                source.at[:, pl.ds(first, kv_half)], target.at[i * slots:(i + 1) * slots],
                sems.at[chunks + 2 + 2 * i + j]))
    for copy in copies:
        copy.start()

    half_rows = mine_ref.shape[0]
    total_rows = 2 * half_rows
    half_seqs = half_rows // steps
    pitch = group + 4
    stride = colors * steps * pitch

    def spread(color, row, block):
        for g in range(2):
            for t in range(steps):
                first = (g * steps + t) * half_seqs
                start = g * half_seqs * stride + (color * steps + t) * pitch + row
                rows_buf[pl.ds(start, half_seqs, stride=stride), :] = block[first:first + half_seqs, :]

    low_side = device % 2 == 0
    copies[0].wait()
    copies[1].wait()
    mine = mine_buf[...].astype(jnp.float32)
    other = other_ref[...].astype(jnp.float32)
    x = jnp.concatenate(
        [jnp.where(low_side, mine, other), jnp.where(low_side, other, mine)], axis=0)
    gain = gain_buf[...].astype(jnp.float32)
    gain = jnp.concatenate([gain[i:i + 1] for i in range(gain.shape[0])], axis=1)
    scaled = (x * gain).astype(jnp.bfloat16)
    squares = jnp.sum(x * x, axis=-1, keepdims=True)
    high = squares.astype(jnp.bfloat16).astype(jnp.float32)
    low = squares - high
    for color in range(colors):
        spread(color, group + 2, jnp.broadcast_to(high, (total_rows, HD)))
        spread(color, group + 3, jnp.broadcast_to(low, (total_rows, HD)))

    def multiply(weights, place_of_head):
        product = jnp.dot(scaled, weights, preferred_element_type=jnp.float32)
        for i in range(product.shape[1] // HD):
            spread(*place_of_head(i), product[:, i * HD:(i + 1) * HD])

    multiply(wk_ref[...], lambda i: (i, group))
    multiply(wv_ref[...], lambda i: (i, group + 1))
    multiply(early_ref[...], lambda i: (i // group, i % group))

    for c in range(chunks):
        copies[2 + c].wait()
        first = (early + c * chunk) // HD
        multiply(wq_buf[c], lambda i: ((first + i) // group, (first + i) % group))
    for copy in copies[2 + chunks:]:
        copy.wait()
    per_part = part_refs[0].shape[0]
    for slot, pattern in enumerate(slot_patterns(order)):
        ref = part_refs[slot // per_part]
        start = pl.multiple_of((device ^ pattern) * stride, 8)
        ref[slot % per_part] = rows_buf[pl.ds(start, stride), :].astype(ref.dtype)


def part_shapes(total, count, block):
    shape = (total // count,) + block
    return (jax.ShapeDtypeStruct(shape, jnp.float32),) + (jax.ShapeDtypeStruct(shape, jnp.bfloat16),) * (count - 1)


def project(place, mine, other, gain, early, wk, wv, wq, keys, values, steps, group, colors, order, count):
    half_rows, depth = mine.shape
    q_cols, kv_cols = wq.shape[1], wk.shape[1]
    seqs = 2 * half_rows // steps
    chunk = 512
    chunks = (q_cols - early.shape[1]) // chunk
    vmem = pl.BlockSpec(memory_space=pltpu.VMEM)
    smem = pl.BlockSpec(memory_space=pltpu.SMEM)
    hbm = pl.BlockSpec(memory_space=pltpu.HBM)
    cache = jax.ShapeDtypeStruct((2 * keys.shape[0], keys.shape[1] // 2), jnp.bfloat16)
    out_shape = (cache, cache) + part_shapes(
        seqs, count, (colors * steps * (group + 4), HD))
    return pl.pallas_call(
        functools.partial(project_kernel, steps, group, colors, order, chunk),
        out_shape=out_shape,
        in_specs=[smem, hbm, vmem, hbm, vmem, vmem, vmem, hbm, hbm, hbm],
        out_specs=(vmem,) * len(out_shape),
        scratch_shapes=[
            pltpu.VMEM(mine.shape, jnp.bfloat16),
            pltpu.VMEM(gain.shape, jnp.bfloat16),
            pltpu.VMEM((chunks, depth, chunk), jnp.bfloat16),
            pltpu.VMEM((seqs * colors * steps * (group + 4), HD), jnp.float32),
            pltpu.SemaphoreType.DMA((chunks + 6,)),
        ],
        compiler_params=pltpu.CompilerParams(vmem_limit_bytes=28 * MIB),
        cost_estimate=pl.CostEstimate(
            flops=4 * half_rows * depth * (q_cols + 2 * kv_cols),
            bytes_accessed=2 * depth * (q_cols + 2 * kv_cols), transcendentals=0),
        name="project",
    )(place, in_hbm(mine), other, in_hbm(gain), in_vmem(early), in_vmem(wk), in_vmem(wv), in_hbm(wq),
      in_hbm(keys), in_hbm(values))


def fetch_first_kernel(wq_ref, wk_ref, wv_ref, early_ref, wk_out, wv_out, sems):
    copies = [
        pltpu.make_async_copy(wk_ref, wk_out, sems.at[0]),
        pltpu.make_async_copy(wv_ref, wv_out, sems.at[1]),
        pltpu.make_async_copy(wq_ref.at[:, :early_ref.shape[1]], early_ref, sems.at[2])]
    for copy in copies:
        copy.start()
    for copy in copies:
        copy.wait()


def fetch_first(wq, wk, wv, early):
    hbm = pl.BlockSpec(memory_space=pltpu.HBM)
    vmem = pl.BlockSpec(memory_space=pltpu.VMEM)
    depth = wq.shape[0]
    return pl.pallas_call(
        fetch_first_kernel,
        out_shape=(
            pltpu.VMEM((depth, early), wq.dtype), pltpu.VMEM(wk.shape, wk.dtype), pltpu.VMEM(wv.shape, wv.dtype)),
        in_specs=[hbm] * 3,
        out_specs=(vmem,) * 3,
        scratch_shapes=[pltpu.SemaphoreType.DMA((3,))],
        compiler_params=pltpu.CompilerParams(vmem_limit_bytes=16 * MIB),
        cost_estimate=pl.CostEstimate(
            flops=0, bytes_accessed=2 * depth * (early + 2 * wk.shape[1]), transcendentals=0),
        name="fetch_first",
    )(in_hbm(wq), in_hbm(wk), in_hbm(wv))


def notes_kernel(steps, position_ref, length_ref, after_ref, notes_ref):
    lane = lax.broadcasted_iota(jnp.int32, (1, HD), 1)
    frequency = rope_frequencies((lane % (HD // 2)).astype(jnp.float32), HD)
    sign = jnp.where(lane < HD // 2, -1.0, 1.0)
    for t in range(steps):
        angle = (position_ref[0] + t).astype(jnp.float32) * frequency
        notes_ref[2 * t:2 * t + 1, :] = jnp.cos(angle)
        notes_ref[2 * t + 1:2 * t + 2, :] = jnp.sin(angle) * sign
    length = length_ref[0].astype(jnp.float32)
    notes_ref[2 * steps:, :] = jnp.full((notes_ref.shape[0] - 2 * steps, HD), length)


def take_notes(position, length, after, steps):
    smem = pl.BlockSpec(memory_space=pltpu.SMEM)
    return pl.pallas_call(
        functools.partial(notes_kernel, steps),
        out_shape=jax.ShapeDtypeStruct((2 * steps + 4, HD), jnp.float32),
        in_specs=[smem, smem, pl.BlockSpec(memory_space=pl.ANY)],
        out_specs=pl.BlockSpec(memory_space=pltpu.VMEM),
        compiler_params=pltpu.CompilerParams(vmem_limit_bytes=4 * MIB),
        name="notes",
    )(position, length, after)


def combine_kernel(arrived, parts, *refs):
    total = refs[0][...]
    for ref in refs[1:arrived + 1]:
        total = total + ref[...].astype(jnp.float32)
    count = total.shape[0] // parts
    for i, ref in enumerate(refs[-parts:]):
        ref[...] = total[i * count:(i + 1) * count].astype(ref.dtype)


def combine(keep, came, held, after, parts):
    vmem = pl.BlockSpec(memory_space=pltpu.VMEM)
    out_shape = part_shapes(keep.shape[0], parts, keep.shape[1:])
    return pl.pallas_call(
        functools.partial(combine_kernel, len(came), parts),
        out_shape=out_shape,
        in_specs=[vmem] * (1 + len(came)) + [pl.BlockSpec(memory_space=pl.ANY)] * (1 + len(held)),
        out_specs=(vmem,) * parts,
        compiler_params=pltpu.CompilerParams(vmem_limit_bytes=24 * MIB),
        name="combine",
    )(keep, *came, after, *[in_vmem(piece) for piece in held])


def fetch_kernel(first, parts, weight_ref, *rest):
    held_ref, sems = rest[-2:]
    rows = held_ref.shape[0] // parts
    copies = [
        pltpu.make_async_copy(
            weight_ref.at[first + c * rows:first + (c + 1) * rows],
            held_ref.at[c * rows:(c + 1) * rows], sems.at[c])
        for c in range(parts)]
    for copy in copies:
        copy.start()
    for copy in copies:
        copy.wait()


def fetch(weight, first, rows, after):
    parts = 4
    return pl.pallas_call(
        functools.partial(fetch_kernel, first, parts),
        out_shape=pltpu.VMEM((rows, weight.shape[1]), weight.dtype),
        in_specs=[pl.BlockSpec(memory_space=pltpu.HBM)] + [pl.BlockSpec(memory_space=pl.ANY)] * len(after),
        out_specs=pl.BlockSpec(memory_space=pltpu.VMEM),
        scratch_shapes=[pltpu.SemaphoreType.DMA((parts,))],
        compiler_params=pltpu.CompilerParams(vmem_limit_bytes=16 * MIB),
        cost_estimate=pl.CostEstimate(
            flops=0, bytes_accessed=2 * rows * weight.shape[1], transcendentals=0),
        name="fetch",
    )(in_hbm(weight), *after)


def attend_kernel(steps, width, unused, notes_ref, came_notes_ref, own_ref, came_ref, *rest):
    part_refs, (context_ref, fresh_ref, fresh_send_ref) = rest[unused:-3], rest[-3:]
    slots = own_ref.shape[0] // 2
    half_kv = own_ref.shape[1] // HD
    total = functools.reduce(jnp.add, [ref[...].astype(jnp.float32) for ref in part_refs])
    pitch = total.shape[1] // (half_kv * steps)
    group = pitch - 4
    factor = 1.0 / math.sqrt(HD)
    per_head = steps * group
    groups = 2 * half_kv
    lanes = groups * per_head
    fresh_rows = 16
    notes = [notes_ref[...], came_notes_ref[...]]
    fresh_keys = [[None] * groups for _ in range(steps)]
    fresh_values = [[None] * groups for _ in range(steps)]
    queries = []
    for seq in range(2):
        for k in range(half_kv):
            index = seq * half_kv + k
            query = []
            for t in range(steps):
                rows = total[seq, (k * steps + t) * pitch:(k * steps + t + 1) * pitch]
                squares = rows[group + 2:group + 3] + rows[group + 3:group + 4]
                rows = rows * lax.rsqrt(squares / width + epsilon)
                cosine = notes[seq][2 * t:2 * t + 1]
                sine = notes[seq][2 * t + 1:2 * t + 2]
                turned = rows * cosine + pltpu.roll(rows, HD // 2, 1) * sine
                query.append(turned[:group])
                fresh_keys[t][index] = turned[group:group + 1]
                fresh_values[t][index] = rows[group + 1:group + 2]
            blocks = [jnp.zeros((per_head, HD), jnp.float32)] * groups
            blocks[index] = jnp.concatenate(query, axis=0)
            queries.append(jnp.concatenate(blocks, axis=1))
    queries = jnp.concatenate(queries, axis=0).astype(jnp.bfloat16)
    keys_now, values_now = [
        jnp.concatenate([jnp.concatenate(row, axis=1) for row in fresh], axis=0)
        for fresh in (fresh_keys, fresh_values)]
    half = half_kv * HD
    for seq, ref in enumerate((fresh_ref, fresh_send_ref)):
        span = slice(seq * half, (seq + 1) * half)
        ref[...] = jnp.concatenate(
            [keys_now[:, span], values_now[:, span], jnp.zeros((fresh_rows - 2 * steps, half), jnp.float32)],
            axis=0).astype(jnp.bfloat16)
    padding = jnp.zeros((fresh_rows - steps, groups * HD), jnp.float32)
    keys_now, values_now = [
        jnp.concatenate([fresh, padding], axis=0).astype(jnp.bfloat16) for fresh in (keys_now, values_now)]

    keys = jnp.concatenate([own_ref[:slots, :], came_ref[:slots, :]], axis=1)
    values = jnp.concatenate([own_ref[slots:, :], came_ref[slots:2 * slots, :]], axis=1)
    lane = lax.broadcasted_iota(jnp.int32, (1, lanes), 1)
    lengths = [note[2 * steps:2 * steps + 1, :1].astype(jnp.int32) for note in notes]
    length = jnp.where(lane < half_kv * per_head, lengths[0], lengths[1])
    live = lax.broadcasted_iota(jnp.int32, (slots, lanes), 0) < length
    seen = lax.broadcasted_iota(jnp.int32, (fresh_rows, lanes), 0) <= (lane % per_head) // group
    over_last, over_first = (((1,), (1,)), ((), ())), (((0,), (0,)), ((), ()))
    scores = lax.dot_general(keys, queries, over_last, preferred_element_type=jnp.float32) * factor
    scores = jnp.where(live, scores, -jnp.inf)
    fresh = lax.dot_general(keys_now, queries, over_last, preferred_element_type=jnp.float32) * factor
    fresh = jnp.where(seen, fresh, -jnp.inf)
    top = jnp.maximum(jnp.max(scores, axis=0, keepdims=True), jnp.max(fresh, axis=0, keepdims=True))
    scores = jnp.exp(scores - top)
    fresh = jnp.exp(fresh - top)
    inverse = 1.0 / (jnp.sum(scores, axis=0, keepdims=True) + jnp.sum(fresh, axis=0, keepdims=True))
    weights = (scores * inverse).astype(jnp.bfloat16)
    fresh = (fresh * inverse).astype(jnp.bfloat16)
    mixed = lax.dot_general(weights, values, over_first, preferred_element_type=jnp.float32)
    mixed = mixed + lax.dot_general(fresh, values_now, over_first, preferred_element_type=jnp.float32)
    for index in range(groups):
        seq, k = index // half_kv, index % half_kv
        context_ref[seq, k * per_head:(k + 1) * per_head, :] = mixed[
            index * per_head:(index + 1) * per_head, index * HD:(index + 1) * HD].astype(jnp.bfloat16)


def attend(notes, came_notes, own, came, parts, held, steps, width, half_heads):
    vmem = pl.BlockSpec(memory_space=pltpu.VMEM)
    fresh = jax.ShapeDtypeStruct((16, own.shape[1]), jnp.bfloat16)
    return pl.pallas_call(
        functools.partial(attend_kernel, steps, width, len(held)),
        out_shape=(jax.ShapeDtypeStruct((2, steps * half_heads, HD), jnp.bfloat16), fresh, fresh),
        in_specs=[vmem] * 4 + [pl.BlockSpec(memory_space=pl.ANY)] * len(held) + [vmem] * len(parts),
        out_specs=(vmem,) * 3,
        compiler_params=pltpu.CompilerParams(vmem_limit_bytes=16 * MIB),
        name="attend",
    )(notes, came_notes, own, came, *[in_vmem(piece) for piece in held], *parts)


def join_kernel(arrived, *refs):
    out_ref = refs[-1]
    for i, ref in enumerate(refs[:arrived + 1]):
        count = ref.shape[0]
        out_ref[i * count:(i + 1) * count] = ref[...]


def local_call(kernel, shape, arrays, held=()):
    vmem = pl.BlockSpec(memory_space=pltpu.VMEM)
    return pl.pallas_call(
        kernel,
        out_shape=jax.ShapeDtypeStruct(shape, jnp.bfloat16),
        in_specs=[vmem] * len(arrays) + [pl.BlockSpec(memory_space=pl.ANY)] * len(held),
        out_specs=vmem,
        compiler_params=pltpu.CompilerParams(vmem_limit_bytes=16 * MIB),
        name="local",
    )(*arrays, *[in_vmem(piece) for piece in held])


def output_kernel(steps, colors, patterns, pieces, place_ref, fresh_ref, *rest):
    weight_refs, context_refs = rest[:pieces], rest[pieces:-4]
    mine_ref, other_ref, wide_buf, rows_buf = rest[-4:]
    device = place_ref[0]
    devices = len(patterns)
    half_seqs = devices // 2
    count, block, _ = context_refs[0].shape
    group = block // (steps * colors)
    for j, pattern in enumerate(patterns):
        rows = context_refs[j // count][j % count]
        start = pl.multiple_of((device ^ pattern) * block, 8)
        wide_buf[pl.ds(start, block), :] = rows.astype(jnp.float32)
    for head in range(colors * group):
        color, h = head // group, head % group
        lines = []
        for g in range(2):
            for t in range(steps):
                start = g * half_seqs * block + (color * steps + t) * group + h
                lines.append(wide_buf[pl.ds(start, half_seqs, stride=block), :])
        rows_buf[:, head * HD:(head + 1) * HD] = jnp.concatenate(lines, axis=0).astype(jnp.bfloat16)
    low_side = device % 2 == 0
    half = rows_buf.shape[0] // 2
    other_ref[half:, :fresh_ref.shape[1]] = fresh_ref[...]
    if other_ref.shape[1] > fresh_ref.shape[1]:
        other_ref[half:, fresh_ref.shape[1]:] = jnp.zeros(
            (fresh_ref.shape[0], other_ref.shape[1] - fresh_ref.shape[1]), jnp.bfloat16)
    columns = mine_ref.shape[1]
    chunk = min(columns, 512)
    for c in range(columns // chunk):
        span = slice(c * chunk, (c + 1) * chunk)
        product, first = None, 0
        for weight_ref in weight_refs:
            last = first + weight_ref.shape[0]
            part = jnp.dot(rows_buf[:, first:last], weight_ref[:, span], preferred_element_type=jnp.float32)
            product = part if product is None else product + part
            first = last
        lower, upper = product[:half], product[half:]
        mine_ref[:, span] = jnp.where(low_side, lower, upper)
        other_ref[:half, span] = jnp.where(low_side, upper, lower).astype(jnp.bfloat16)


def output(place, fresh, contexts, patterns, held, steps, colors):
    columns = held[0].shape[1]
    depth = sum(piece.shape[0] for piece in held)
    devices = len(patterns)
    half = devices * steps // 2
    vmem = pl.BlockSpec(memory_space=pltpu.VMEM)
    smem = pl.BlockSpec(memory_space=pltpu.SMEM)
    return pl.pallas_call(
        functools.partial(output_kernel, steps, colors, patterns, len(held)),
        out_shape=(
            jax.ShapeDtypeStruct((half, columns), jnp.float32),
            jax.ShapeDtypeStruct((half + fresh.shape[0], columns), jnp.bfloat16),
        ),
        in_specs=[smem, vmem] + [vmem] * (len(held) + len(contexts)),
        out_specs=(vmem, vmem),
        scratch_shapes=[
            pltpu.VMEM((devices * contexts[0].shape[1], HD), jnp.float32),
            pltpu.VMEM((devices * steps, depth), jnp.bfloat16),
        ],
        compiler_params=pltpu.CompilerParams(vmem_limit_bytes=26 * MIB),
        cost_estimate=pl.CostEstimate(
            flops=2 * devices * steps * depth * columns,
            bytes_accessed=2 * depth * columns, transcendentals=0),
        name="output",
    )(place, fresh, *[in_vmem(piece) for piece in held], *contexts)


def finish_kernel(steps, place_ref, mine_ref, came_ref, fresh_ref, result_ref, new_keys_ref, new_values_ref):
    half = mine_ref.shape[0]
    result_ref[...] = (mine_ref[...] + came_ref[:half, :].astype(jnp.float32)).astype(jnp.bfloat16)
    own = fresh_ref[...].astype(jnp.float32)
    came = came_ref[half:, :own.shape[1]].astype(jnp.float32)
    low_side = place_ref[0] % 2 == 0
    rows = jnp.concatenate(
        [jnp.where(low_side, own, came), jnp.where(low_side, came, own)], axis=1).astype(jnp.bfloat16)
    new_keys_ref[...] = rows[:steps]
    new_values_ref[...] = rows[steps:2 * steps]


def finish(place, mine, came, fresh, steps):
    vmem = pl.BlockSpec(memory_space=pltpu.VMEM)
    new = jax.ShapeDtypeStruct((steps, 2 * fresh.shape[1]), jnp.bfloat16)
    return pl.pallas_call(
        functools.partial(finish_kernel, steps),
        out_shape=(jax.ShapeDtypeStruct(mine.shape, jnp.bfloat16), new, new),
        in_specs=[pl.BlockSpec(memory_space=pltpu.SMEM)] + [vmem] * 3,
        out_specs=(vmem,) * 3,
        compiler_params=pltpu.CompilerParams(vmem_limit_bytes=8 * MIB),
        name="finish",
    )(place, mine, came, fresh)


def body(hidden_in, norm_gain, query_weight, key_weight, value_weight, out_weight,
         cache_keys, cache_values, lengths, positions):
    steps, half_seqs, depth = hidden_in.shape
    everyone = ("gx", "gy")
    devices = lax.axis_size(everyone)
    bits = devices.bit_length() - 1
    colors = key_weight.shape[1] // HD
    half_heads = query_weight.shape[1] // HD
    group = half_heads // colors
    place = lax.axis_index(everyone).astype(jnp.int32).reshape(1)

    def partner(array, pattern):
        return lax.ppermute(array, everyone, [(i, i ^ pattern) for i in range(devices)])

    stages = [list(range(first, min(first + 2, bits))) for first in range(1, bits, 2)]
    order = [bit for stage in stages for bit in stage] + [0]
    total = out_weight.shape[0]
    cuts = [total * i // 8 for i in (0, 2, 3, 5, 8)]
    held = []

    def fetch_next(window, after):
        i = len(held)
        if window not in (0, 1, 2, 3):
            return []
        held.append(fetch(out_weight, cuts[i], cuts[i + 1] - cuts[i], after))
        return held[-1:]

    mine = hidden_in.reshape(steps * half_seqs, depth)
    other = partner(mine, 1)
    early, wk, wv = fetch_first(query_weight, key_weight, value_weight, 512)
    own, cache, *parts = project(
        place, mine, other, norm_gain.reshape(-1, HD), early, wk, wv, query_weight,
        cache_keys[0], cache_values[0],
        steps, group, colors, order, 1 << len(stages[0]))
    cache = partner(cache, 1)
    notes = take_notes(positions, lengths, parts[1], steps)
    came_notes = partner(notes, 1)
    for i, stage in enumerate(stages):
        came = [partner(part, pattern) for part, pattern in zip(parts[1:], slot_patterns(stage)[1:])]
        now = fetch_next(i, [parts[1], notes])
        if i < len(stages) - 1:
            parts = combine(parts[0], came, now, notes, 1 << len(stages[i + 1]))
    context, fresh, fresh_send = attend(
        notes, came_notes, own, cache, [parts[0], *came], now, steps, depth * lax.axis_size("gx"), half_heads)

    patterns = [0, 1]
    for i, stage in enumerate(stages[::-1]):
        moves = slot_patterns(stage)
        came = [partner(context, move) for move in moves[1:]]
        patterns = [p ^ move for move in moves for p in patterns]
        now = fetch_next(len(stages) + i, [context])
        if i < len(stages) - 1:
            shape = (len(moves) * context.shape[0],) + context.shape[1:]
            context = local_call(functools.partial(join_kernel, len(came)), shape, [context, *came], now)
    mine, other = output(place, fresh_send, [context, *came], patterns, held, steps, colors)
    result, new_keys, new_values = finish(place, mine, partner(other, 1), fresh, steps)
    return (
        result.reshape(steps, half_seqs, -1),
        new_keys[:, None, :],
        new_values[:, None, :],
    )


def solution(mesh):
    in_specs = (
        P(None, ("rep", "gy"), "gx"),
        P("gx"),
        P("gx", "gy"),
        P("gx", "gy"),
        P("gx", "gy"),
        P("gy", "gx"),
        P(("rep", "gx", "gy"), None, None),
        P(("rep", "gx", "gy"), None, None),
        P(("rep", "gx", "gy")),
        P(("rep", "gx", "gy")),
    )
    out_specs = (
        P(None, ("rep", "gy"), "gx"),
        P(None, ("rep", "gx", "gy"), None),
        P(None, ("rep", "gx", "gy"), None),
    )
    return jax.shard_map(body, mesh=mesh, in_specs=in_specs, out_specs=out_specs, check_vma=False)
```

```python
import functools
import math

import jax
import jax.numpy as jnp
from jax import lax
from jax.experimental import pallas as pl
from jax.experimental.pallas import tpu as pltpu
from jax.sharding import PartitionSpec as P

HD = 128
epsilon = 1e-05
rope_theta = 500000.0
MIB = 1024 * 1024


def rope_frequencies(index, head_size):
    frequency = jnp.exp(-math.log(rope_theta) * 2.0 * index / head_size)
    wavelength = 2.0 * math.pi / frequency
    smooth = (8192.0 / wavelength - 1.0) / 3.0
    blended = (1.0 - smooth) * frequency / 8.0 + smooth * frequency
    adjusted = jnp.where(wavelength > 8192.0, frequency / 8.0, blended)
    return jnp.where(wavelength < 2048.0, frequency, adjusted)


def slot_patterns(order):
    count = len(order)
    return [
        sum(((j >> (count - 1 - i)) & 1) << bit for i, bit in enumerate(order))
        for j in range(1 << count)]


def in_hbm(array):
    return pltpu.with_memory_space_constraint(array, pltpu.HBM)


def in_vmem(array):
    return pltpu.with_memory_space_constraint(array, pltpu.VMEM)


def project_kernel(steps, group, colors, order, chunk, place_ref, mine_ref, other_ref, gain_ref, early_ref, wk_ref, wv_ref,
                   wq_ref, keys_ref, values_ref, own_ref, send_ref, *rest):
    part_refs, rest = rest[:-5], rest[-5:]
    mine_buf, gain_buf, wq_buf, rows_buf, sems = rest
    early = early_ref.shape[1]
    q_cols = wq_ref.shape[1]
    chunks = (q_cols - early) // chunk
    copies = [pltpu.make_async_copy(mine_ref, mine_buf, sems.at[chunks]),
              pltpu.make_async_copy(gain_ref, gain_buf, sems.at[chunks + 1])]
    for c in range(chunks):
        copies.append(pltpu.make_async_copy(
            wq_ref.at[:, early + c * chunk:early + (c + 1) * chunk], wq_buf.at[c], sems.at[c]))
    device = place_ref[0]
    slots, kv_half = keys_ref.shape[0], keys_ref.shape[1] // 2
    for i, source in enumerate((keys_ref, values_ref)):
        for j, (target, part) in enumerate(((send_ref, 1 - device % 2), (own_ref, device % 2))):
            first = pl.multiple_of(part * kv_half, HD)
            copies.append(pltpu.make_async_copy(
                source.at[:, pl.ds(first, kv_half)], target.at[i * slots:(i + 1) * slots],
                sems.at[chunks + 2 + 2 * i + j]))
    for copy in copies:
        copy.start()

    half_rows = mine_ref.shape[0]
    total_rows = 2 * half_rows
    half_seqs = half_rows // steps
    pitch = group + 4
    stride = colors * steps * pitch

    def spread(color, row, block):
        for g in range(2):
            for t in range(steps):
                first = (g * steps + t) * half_seqs
                start = g * half_seqs * stride + (color * steps + t) * pitch + row
                rows_buf[pl.ds(start, half_seqs, stride=stride), :] = block[first:first + half_seqs, :]

    low_side = device % 2 == 0
    copies[0].wait()
    copies[1].wait()
    mine = mine_buf[...].astype(jnp.float32)
    other = other_ref[...].astype(jnp.float32)
    x = jnp.concatenate(
        [jnp.where(low_side, mine, other), jnp.where(low_side, other, mine)], axis=0)
    gain = gain_buf[...].astype(jnp.float32)
    gain = jnp.concatenate([gain[i:i + 1] for i in range(gain.shape[0])], axis=1)
    scaled = (x * gain).astype(jnp.bfloat16)
    squares = jnp.sum(x * x, axis=-1, keepdims=True)
    high = squares.astype(jnp.bfloat16).astype(jnp.float32)
    low = squares - high
    for color in range(colors):
        spread(color, group + 2, jnp.broadcast_to(high, (total_rows, HD)))
        spread(color, group + 3, jnp.broadcast_to(low, (total_rows, HD)))

    def multiply(weights, place_of_head):
        product = jnp.dot(scaled, weights, preferred_element_type=jnp.float32)
        for i in range(product.shape[1] // HD):
            spread(*place_of_head(i), product[:, i * HD:(i + 1) * HD])

    multiply(wk_ref[...], lambda i: (i, group))
    multiply(wv_ref[...], lambda i: (i, group + 1))
    multiply(early_ref[...], lambda i: (i // group, i % group))

    for c in range(chunks):
        copies[2 + c].wait()
        first = (early + c * chunk) // HD
        multiply(wq_buf[c], lambda i: ((first + i) // group, (first + i) % group))
    for copy in copies[2 + chunks:]:
        copy.wait()
    per_part = part_refs[0].shape[0]
    for slot, pattern in enumerate(slot_patterns(order)):
        ref = part_refs[slot // per_part]
        start = pl.multiple_of((device ^ pattern) * stride, 8)
        ref[slot % per_part] = rows_buf[pl.ds(start, stride), :].astype(ref.dtype)


def part_shapes(total, count, block):
    shape = (total // count,) + block
    return (jax.ShapeDtypeStruct(shape, jnp.float32),) + (jax.ShapeDtypeStruct(shape, jnp.bfloat16),) * (count - 1)


def project(place, mine, other, gain, early, wk, wv, wq, keys, values, steps, group, colors, order, count):
    half_rows, depth = mine.shape
    q_cols, kv_cols = wq.shape[1], wk.shape[1]
    seqs = 2 * half_rows // steps
    chunk = 512
    chunks = (q_cols - early.shape[1]) // chunk
    vmem = pl.BlockSpec(memory_space=pltpu.VMEM)
    smem = pl.BlockSpec(memory_space=pltpu.SMEM)
    hbm = pl.BlockSpec(memory_space=pltpu.HBM)
    cache = jax.ShapeDtypeStruct((2 * keys.shape[0], keys.shape[1] // 2), jnp.bfloat16)
    out_shape = (cache, cache) + part_shapes(
        seqs, count, (colors * steps * (group + 4), HD))
    return pl.pallas_call(
        functools.partial(project_kernel, steps, group, colors, order, chunk),
        out_shape=out_shape,
        in_specs=[smem, hbm, vmem, hbm, vmem, vmem, vmem, hbm, hbm, hbm],
        out_specs=(vmem,) * len(out_shape),
        scratch_shapes=[
            pltpu.VMEM(mine.shape, jnp.bfloat16),
            pltpu.VMEM(gain.shape, jnp.bfloat16),
            pltpu.VMEM((chunks, depth, chunk), jnp.bfloat16),
            pltpu.VMEM((seqs * colors * steps * (group + 4), HD), jnp.float32),
            pltpu.SemaphoreType.DMA((chunks + 6,)),
        ],
        compiler_params=pltpu.CompilerParams(vmem_limit_bytes=28 * MIB),
        cost_estimate=pl.CostEstimate(
            flops=4 * half_rows * depth * (q_cols + 2 * kv_cols),
            bytes_accessed=2 * depth * (q_cols + 2 * kv_cols), transcendentals=0),
        name="project",
    )(place, in_hbm(mine), other, in_hbm(gain), in_vmem(early), in_vmem(wk), in_vmem(wv), in_hbm(wq),
      in_hbm(keys), in_hbm(values))


def fetch_first_kernel(wq_ref, wk_ref, wv_ref, early_ref, wk_out, wv_out, sems):
    copies = [
        pltpu.make_async_copy(wk_ref, wk_out, sems.at[0]),
        pltpu.make_async_copy(wv_ref, wv_out, sems.at[1]),
        pltpu.make_async_copy(wq_ref.at[:, :early_ref.shape[1]], early_ref, sems.at[2])]
    for copy in copies:
        copy.start()
    for copy in copies:
        copy.wait()


def fetch_first(wq, wk, wv, early):
    hbm = pl.BlockSpec(memory_space=pltpu.HBM)
    vmem = pl.BlockSpec(memory_space=pltpu.VMEM)
    depth = wq.shape[0]
    return pl.pallas_call(
        fetch_first_kernel,
        out_shape=(
            pltpu.VMEM((depth, early), wq.dtype), pltpu.VMEM(wk.shape, wk.dtype), pltpu.VMEM(wv.shape, wv.dtype)),
        in_specs=[hbm] * 3,
        out_specs=(vmem,) * 3,
        scratch_shapes=[pltpu.SemaphoreType.DMA((3,))],
        compiler_params=pltpu.CompilerParams(vmem_limit_bytes=16 * MIB),
        cost_estimate=pl.CostEstimate(
            flops=0, bytes_accessed=2 * depth * (early + 2 * wk.shape[1]), transcendentals=0),
        name="fetch_first",
    )(in_hbm(wq), in_hbm(wk), in_hbm(wv))


def notes_kernel(steps, position_ref, length_ref, after_ref, notes_ref):
    lane = lax.broadcasted_iota(jnp.int32, (1, HD), 1)
    frequency = rope_frequencies((lane % (HD // 2)).astype(jnp.float32), HD)
    sign = jnp.where(lane < HD // 2, -1.0, 1.0)
    for t in range(steps):
        angle = (position_ref[0] + t).astype(jnp.float32) * frequency
        notes_ref[2 * t:2 * t + 1, :] = jnp.cos(angle)
        notes_ref[2 * t + 1:2 * t + 2, :] = jnp.sin(angle) * sign
    length = length_ref[0].astype(jnp.float32)
    notes_ref[2 * steps:, :] = jnp.full((notes_ref.shape[0] - 2 * steps, HD), length)


def take_notes(position, length, after, steps):
    smem = pl.BlockSpec(memory_space=pltpu.SMEM)
    return pl.pallas_call(
        functools.partial(notes_kernel, steps),
        out_shape=jax.ShapeDtypeStruct((2 * steps + 4, HD), jnp.float32),
        in_specs=[smem, smem, pl.BlockSpec(memory_space=pl.ANY)],
        out_specs=pl.BlockSpec(memory_space=pltpu.VMEM),
        compiler_params=pltpu.CompilerParams(vmem_limit_bytes=4 * MIB),
        name="notes",
    )(position, length, after)


def combine_kernel(arrived, parts, *refs):
    total = refs[0][...]
    for ref in refs[1:arrived + 1]:
        total = total + ref[...].astype(jnp.float32)
    count = total.shape[0] // parts
    for i, ref in enumerate(refs[-parts:]):
        ref[...] = total[i * count:(i + 1) * count].astype(ref.dtype)


def combine(keep, came, held, after, parts):
    vmem = pl.BlockSpec(memory_space=pltpu.VMEM)
    out_shape = part_shapes(keep.shape[0], parts, keep.shape[1:])
    return pl.pallas_call(
        functools.partial(combine_kernel, len(came), parts),
        out_shape=out_shape,
        in_specs=[vmem] * (1 + len(came)) + [pl.BlockSpec(memory_space=pl.ANY)] * (1 + len(held)),
        out_specs=(vmem,) * parts,
        compiler_params=pltpu.CompilerParams(vmem_limit_bytes=24 * MIB),
        name="combine",
    )(keep, *came, after, *[in_vmem(piece) for piece in held])


def fetch_kernel(first, parts, weight_ref, *rest):
    held_ref, sems = rest[-2:]
    rows = held_ref.shape[0] // parts
    copies = [
        pltpu.make_async_copy(
            weight_ref.at[first + c * rows:first + (c + 1) * rows],
            held_ref.at[c * rows:(c + 1) * rows], sems.at[c])
        for c in range(parts)]
    for copy in copies:
        copy.start()
    for copy in copies:
        copy.wait()


def fetch(weight, first, rows, after):
    parts = 4
    return pl.pallas_call(
        functools.partial(fetch_kernel, first, parts),
        out_shape=pltpu.VMEM((rows, weight.shape[1]), weight.dtype),
        in_specs=[pl.BlockSpec(memory_space=pltpu.HBM)] + [pl.BlockSpec(memory_space=pl.ANY)] * len(after),
        out_specs=pl.BlockSpec(memory_space=pltpu.VMEM),
        scratch_shapes=[pltpu.SemaphoreType.DMA((parts,))],
        compiler_params=pltpu.CompilerParams(vmem_limit_bytes=16 * MIB),
        cost_estimate=pl.CostEstimate(
            flops=0, bytes_accessed=2 * rows * weight.shape[1], transcendentals=0),
        name="fetch",
    )(in_hbm(weight), *after)


def attend_kernel(steps, width, unused, notes_ref, came_notes_ref, own_ref, came_ref, *rest):
    part_refs, (context_ref, fresh_ref, fresh_send_ref) = rest[unused:-3], rest[-3:]
    slots = own_ref.shape[0] // 2
    half_kv = own_ref.shape[1] // HD
    total = functools.reduce(jnp.add, [ref[...].astype(jnp.float32) for ref in part_refs])
    pitch = total.shape[1] // (half_kv * steps)
    group = pitch - 4
    factor = 1.0 / math.sqrt(HD)
    per_head = steps * group
    groups = 2 * half_kv
    lanes = groups * per_head
    fresh_rows = 16
    notes = [notes_ref[...], came_notes_ref[...]]
    fresh_keys = [[None] * groups for _ in range(steps)]
    fresh_values = [[None] * groups for _ in range(steps)]
    queries = []
    for seq in range(2):
        for k in range(half_kv):
            index = seq * half_kv + k
            query = []
            for t in range(steps):
                rows = total[seq, (k * steps + t) * pitch:(k * steps + t + 1) * pitch]
                squares = rows[group + 2:group + 3] + rows[group + 3:group + 4]
                rows = rows * lax.rsqrt(squares / width + epsilon)
                cosine = notes[seq][2 * t:2 * t + 1]
                sine = notes[seq][2 * t + 1:2 * t + 2]
                turned = rows * cosine + pltpu.roll(rows, HD // 2, 1) * sine
                query.append(turned[:group])
                fresh_keys[t][index] = turned[group:group + 1]
                fresh_values[t][index] = rows[group + 1:group + 2]
            blocks = [jnp.zeros((per_head, HD), jnp.float32)] * groups
            blocks[index] = jnp.concatenate(query, axis=0)
            queries.append(jnp.concatenate(blocks, axis=1))
    queries = jnp.concatenate(queries, axis=0).astype(jnp.bfloat16)
    keys_now, values_now = [
        jnp.concatenate([jnp.concatenate(row, axis=1) for row in fresh], axis=0)
        for fresh in (fresh_keys, fresh_values)]
    half = half_kv * HD
    for seq, ref in enumerate((fresh_ref, fresh_send_ref)):
        span = slice(seq * half, (seq + 1) * half)
        ref[...] = jnp.concatenate(
            [keys_now[:, span], values_now[:, span], jnp.zeros((fresh_rows - 2 * steps, half), jnp.float32)],
            axis=0).astype(jnp.bfloat16)
    padding = jnp.zeros((fresh_rows - steps, groups * HD), jnp.float32)
    keys_now, values_now = [
        jnp.concatenate([fresh, padding], axis=0).astype(jnp.bfloat16) for fresh in (keys_now, values_now)]

    keys = jnp.concatenate([own_ref[:slots, :], came_ref[:slots, :]], axis=1)
    values = jnp.concatenate([own_ref[slots:, :], came_ref[slots:2 * slots, :]], axis=1)
    lane = lax.broadcasted_iota(jnp.int32, (1, lanes), 1)
    lengths = [note[2 * steps:2 * steps + 1, :1].astype(jnp.int32) for note in notes]
    length = jnp.where(lane < half_kv * per_head, lengths[0], lengths[1])
    live = lax.broadcasted_iota(jnp.int32, (slots, lanes), 0) < length
    seen = lax.broadcasted_iota(jnp.int32, (fresh_rows, lanes), 0) <= (lane % per_head) // group
    over_last, over_first = (((1,), (1,)), ((), ())), (((0,), (0,)), ((), ()))
    scores = lax.dot_general(keys, queries, over_last, preferred_element_type=jnp.float32) * factor
    scores = jnp.where(live, scores, -jnp.inf)
    fresh = lax.dot_general(keys_now, queries, over_last, preferred_element_type=jnp.float32) * factor
    fresh = jnp.where(seen, fresh, -jnp.inf)
    top = jnp.maximum(jnp.max(scores, axis=0, keepdims=True), jnp.max(fresh, axis=0, keepdims=True))
    scores = jnp.exp(scores - top)
    fresh = jnp.exp(fresh - top)
    inverse = 1.0 / (jnp.sum(scores, axis=0, keepdims=True) + jnp.sum(fresh, axis=0, keepdims=True))
    weights = (scores * inverse).astype(jnp.bfloat16)
    fresh = (fresh * inverse).astype(jnp.bfloat16)
    mixed = lax.dot_general(weights, values, over_first, preferred_element_type=jnp.float32)
    mixed = mixed + lax.dot_general(fresh, values_now, over_first, preferred_element_type=jnp.float32)
    for index in range(groups):
        seq, k = index // half_kv, index % half_kv
        context_ref[seq, k * per_head:(k + 1) * per_head, :] = mixed[
            index * per_head:(index + 1) * per_head, index * HD:(index + 1) * HD].astype(jnp.bfloat16)


def attend(notes, came_notes, own, came, parts, held, steps, width, half_heads):
    vmem = pl.BlockSpec(memory_space=pltpu.VMEM)
    fresh = jax.ShapeDtypeStruct((16, own.shape[1]), jnp.bfloat16)
    return pl.pallas_call(
        functools.partial(attend_kernel, steps, width, len(held)),
        out_shape=(jax.ShapeDtypeStruct((2, steps * half_heads, HD), jnp.bfloat16), fresh, fresh),
        in_specs=[vmem] * 4 + [pl.BlockSpec(memory_space=pl.ANY)] * len(held) + [vmem] * len(parts),
        out_specs=(vmem,) * 3,
        compiler_params=pltpu.CompilerParams(vmem_limit_bytes=16 * MIB),
        name="attend",
    )(notes, came_notes, own, came, *[in_vmem(piece) for piece in held], *parts)


def join_kernel(arrived, *refs):
    out_ref = refs[-1]
    for i, ref in enumerate(refs[:arrived + 1]):
        count = ref.shape[0]
        out_ref[i * count:(i + 1) * count] = ref[...]


def local_call(kernel, shape, arrays, held=()):
    vmem = pl.BlockSpec(memory_space=pltpu.VMEM)
    return pl.pallas_call(
        kernel,
        out_shape=jax.ShapeDtypeStruct(shape, jnp.bfloat16),
        in_specs=[vmem] * len(arrays) + [pl.BlockSpec(memory_space=pl.ANY)] * len(held),
        out_specs=vmem,
        compiler_params=pltpu.CompilerParams(vmem_limit_bytes=16 * MIB),
        name="local",
    )(*arrays, *[in_vmem(piece) for piece in held])


def output_kernel(steps, colors, patterns, pieces, place_ref, fresh_ref, *rest):
    weight_refs, context_refs = rest[:pieces], rest[pieces:-4]
    mine_ref, other_ref, wide_buf, rows_buf = rest[-4:]
    device = place_ref[0]
    devices = len(patterns)
    half_seqs = devices // 2
    count, block, _ = context_refs[0].shape
    group = block // (steps * colors)
    for j, pattern in enumerate(patterns):
        rows = context_refs[j // count][j % count]
        start = pl.multiple_of((device ^ pattern) * block, 8)
        wide_buf[pl.ds(start, block), :] = rows.astype(jnp.float32)
    for head in range(colors * group):
        color, h = head // group, head % group
        lines = []
        for g in range(2):
            for t in range(steps):
                start = g * half_seqs * block + (color * steps + t) * group + h
                lines.append(wide_buf[pl.ds(start, half_seqs, stride=block), :])
        rows_buf[:, head * HD:(head + 1) * HD] = jnp.concatenate(lines, axis=0).astype(jnp.bfloat16)
    low_side = device % 2 == 0
    half = rows_buf.shape[0] // 2
    other_ref[half:, :fresh_ref.shape[1]] = fresh_ref[...]
    if other_ref.shape[1] > fresh_ref.shape[1]:
        other_ref[half:, fresh_ref.shape[1]:] = jnp.zeros(
            (fresh_ref.shape[0], other_ref.shape[1] - fresh_ref.shape[1]), jnp.bfloat16)
    columns = mine_ref.shape[1]
    chunk = min(columns, 512)
    for c in range(columns // chunk):
        span = slice(c * chunk, (c + 1) * chunk)
        product, first = None, 0
        for weight_ref in weight_refs:
            last = first + weight_ref.shape[0]
            part = jnp.dot(rows_buf[:, first:last], weight_ref[:, span], preferred_element_type=jnp.float32)
            product = part if product is None else product + part
            first = last
        lower, upper = product[:half], product[half:]
        mine_ref[:, span] = jnp.where(low_side, lower, upper)
        other_ref[:half, span] = jnp.where(low_side, upper, lower).astype(jnp.bfloat16)


def output(place, fresh, contexts, patterns, held, steps, colors):
    columns = held[0].shape[1]
    depth = sum(piece.shape[0] for piece in held)
    devices = len(patterns)
    half = devices * steps // 2
    vmem = pl.BlockSpec(memory_space=pltpu.VMEM)
    smem = pl.BlockSpec(memory_space=pltpu.SMEM)
    return pl.pallas_call(
        functools.partial(output_kernel, steps, colors, patterns, len(held)),
        out_shape=(
            jax.ShapeDtypeStruct((half, columns), jnp.float32),
            jax.ShapeDtypeStruct((half + fresh.shape[0], columns), jnp.bfloat16),
        ),
        in_specs=[smem, vmem] + [vmem] * (len(held) + len(contexts)),
        out_specs=(vmem, vmem),
        scratch_shapes=[
            pltpu.VMEM((devices * contexts[0].shape[1], HD), jnp.float32),
            pltpu.VMEM((devices * steps, depth), jnp.bfloat16),
        ],
        compiler_params=pltpu.CompilerParams(vmem_limit_bytes=26 * MIB),
        cost_estimate=pl.CostEstimate(
            flops=2 * devices * steps * depth * columns,
            bytes_accessed=2 * depth * columns, transcendentals=0),
        name="output",
    )(place, fresh, *[in_vmem(piece) for piece in held], *contexts)


def finish_kernel(steps, place_ref, mine_ref, came_ref, fresh_ref, result_ref, new_keys_ref, new_values_ref):
    half = mine_ref.shape[0]
    result_ref[...] = (mine_ref[...] + came_ref[:half, :].astype(jnp.float32)).astype(jnp.bfloat16)
    own = fresh_ref[...].astype(jnp.float32)
    came = came_ref[half:, :own.shape[1]].astype(jnp.float32)
    low_side = place_ref[0] % 2 == 0
    rows = jnp.concatenate(
        [jnp.where(low_side, own, came), jnp.where(low_side, came, own)], axis=1).astype(jnp.bfloat16)
    new_keys_ref[...] = rows[:steps]
    new_values_ref[...] = rows[steps:2 * steps]


def finish(place, mine, came, fresh, steps):
    vmem = pl.BlockSpec(memory_space=pltpu.VMEM)
    new = jax.ShapeDtypeStruct((steps, 2 * fresh.shape[1]), jnp.bfloat16)
    return pl.pallas_call(
        functools.partial(finish_kernel, steps),
        out_shape=(jax.ShapeDtypeStruct(mine.shape, jnp.bfloat16), new, new),
        in_specs=[pl.BlockSpec(memory_space=pltpu.SMEM)] + [vmem] * 3,
        out_specs=(vmem,) * 3,
        compiler_params=pltpu.CompilerParams(vmem_limit_bytes=8 * MIB),
        name="finish",
    )(place, mine, came, fresh)


def body(hidden_in, norm_gain, query_weight, key_weight, value_weight, out_weight,
         cache_keys, cache_values, lengths, positions):
    steps, half_seqs, depth = hidden_in.shape
    everyone = ("gx", "gy")
    devices = lax.axis_size(everyone)
    bits = devices.bit_length() - 1
    colors = key_weight.shape[1] // HD
    half_heads = query_weight.shape[1] // HD
    group = half_heads // colors
    place = lax.axis_index(everyone).astype(jnp.int32).reshape(1)

    def partner(array, pattern):
        return lax.ppermute(array, everyone, [(i, i ^ pattern) for i in range(devices)])

    stages = [list(range(first, min(first + 2, bits))) for first in range(1, bits, 2)]
    order = [bit for stage in stages for bit in stage] + [0]
    total = out_weight.shape[0]
    cuts = [total * i // 8 for i in (0, 2, 3, 5, 8)]
    held = []

    def fetch_next(window, after):
        i = len(held)
        if window not in (0, 1, 2, 3):
            return []
        held.append(fetch(out_weight, cuts[i], cuts[i + 1] - cuts[i], after))
        return held[-1:]

    mine = hidden_in.reshape(steps * half_seqs, depth)
    other = partner(mine, 1)
    early, wk, wv = fetch_first(query_weight, key_weight, value_weight, 512)
    own, cache, *parts = project(
        place, mine, other, norm_gain.reshape(-1, HD), early, wk, wv, query_weight,
        cache_keys[0], cache_values[0],
        steps, group, colors, order, 1 << len(stages[0]))
    cache = partner(cache, 1)
    notes = take_notes(positions, lengths, parts[1], steps)
    came_notes = partner(notes, 1)
    for i, stage in enumerate(stages):
        came = [partner(part, pattern) for part, pattern in zip(parts[1:], slot_patterns(stage)[1:])]
        now = fetch_next(i, [parts[1], notes])
        if i < len(stages) - 1:
            parts = combine(parts[0], came, now, notes, 1 << len(stages[i + 1]))
    context, fresh, fresh_send = attend(
        notes, came_notes, own, cache, [parts[0], *came], now, steps, depth * lax.axis_size("gx"), half_heads)

    patterns = [0, 1]
    for i, stage in enumerate(stages[::-1]):
        moves = slot_patterns(stage)
        moves = moves[:1] + moves[2:] + moves[1:2]
        came = [partner(context, move) for move in moves[1:]]
        patterns = [p ^ move for move in moves for p in patterns]
        now = fetch_next(len(stages) + i, [context])
        if i < len(stages) - 1:
            shape = (len(moves) * context.shape[0],) + context.shape[1:]
            context = local_call(functools.partial(join_kernel, len(came)), shape, [context, *came], now)
    mine, other = output(place, fresh_send, [context, *came], patterns, held, steps, colors)
    result, new_keys, new_values = finish(place, mine, partner(other, 1), fresh, steps)
    return (
        result.reshape(steps, half_seqs, -1),
        new_keys[:, None, :],
        new_values[:, None, :],
    )


def solution(mesh):
    in_specs = (
        P(None, ("rep", "gy"), "gx"),
        P("gx"),
        P("gx", "gy"),
        P("gx", "gy"),
        P("gx", "gy"),
        P("gy", "gx"),
        P(("rep", "gx", "gy"), None, None),
        P(("rep", "gx", "gy"), None, None),
        P(("rep", "gx", "gy")),
        P(("rep", "gx", "gy")),
    )
    out_specs = (
        P(None, ("rep", "gy"), "gx"),
        P(None, ("rep", "gx", "gy"), None),
        P(None, ("rep", "gx", "gy"), None),
    )
    return jax.shard_map(body, mesh=mesh, in_specs=in_specs, out_specs=out_specs, check_vma=False)
```

```python
import functools
import math

import jax
import jax.numpy as jnp
from jax import lax
from jax.experimental import pallas as pl
from jax.experimental.pallas import tpu as pltpu
from jax.sharding import PartitionSpec as P

HD = 128
epsilon = 1e-05
rope_theta = 500000.0
MIB = 1024 * 1024


def rope_frequencies(index, head_size):
    frequency = jnp.exp(-math.log(rope_theta) * 2.0 * index / head_size)
    wavelength = 2.0 * math.pi / frequency
    smooth = (8192.0 / wavelength - 1.0) / 3.0
    blended = (1.0 - smooth) * frequency / 8.0 + smooth * frequency
    adjusted = jnp.where(wavelength > 8192.0, frequency / 8.0, blended)
    return jnp.where(wavelength < 2048.0, frequency, adjusted)


def slot_patterns(order):
    count = len(order)
    return [
        sum(((j >> (count - 1 - i)) & 1) << bit for i, bit in enumerate(order))
        for j in range(1 << count)]


def in_hbm(array):
    return pltpu.with_memory_space_constraint(array, pltpu.HBM)


def in_vmem(array):
    return pltpu.with_memory_space_constraint(array, pltpu.VMEM)


def project_kernel(steps, group, colors, order, chunk, place_ref, mine_ref, other_ref, gain_ref, early_ref, wk_ref, wv_ref,
                   wq_ref, keys_ref, values_ref, own_ref, send_ref, *rest):
    part_refs, rest = rest[:-5], rest[-5:]
    mine_buf, gain_buf, wq_buf, rows_buf, sems = rest
    early = early_ref.shape[1]
    q_cols = wq_ref.shape[1]
    chunks = (q_cols - early) // chunk
    copies = [pltpu.make_async_copy(mine_ref, mine_buf, sems.at[chunks]),
              pltpu.make_async_copy(gain_ref, gain_buf, sems.at[chunks + 1])]
    for c in range(chunks):
        copies.append(pltpu.make_async_copy(
            wq_ref.at[:, early + c * chunk:early + (c + 1) * chunk], wq_buf.at[c], sems.at[c]))
    device = place_ref[0]
    slots, kv_half = keys_ref.shape[0], keys_ref.shape[1] // 2
    for i, source in enumerate((keys_ref, values_ref)):
        for j, (target, part) in enumerate(((send_ref, 1 - device % 2), (own_ref, device % 2))):
            first = pl.multiple_of(part * kv_half, HD)
            copies.append(pltpu.make_async_copy(
                source.at[:, pl.ds(first, kv_half)], target.at[i * slots:(i + 1) * slots],
                sems.at[chunks + 2 + 2 * i + j]))
    for copy in copies:
        copy.start()

    half_rows = mine_ref.shape[0]
    total_rows = 2 * half_rows
    half_seqs = half_rows // steps
    pitch = group + 4
    stride = colors * steps * pitch

    def spread(color, row, block):
        for g in range(2):
            for t in range(steps):
                first = (g * steps + t) * half_seqs
                start = g * half_seqs * stride + (color * steps + t) * pitch + row
                rows_buf[pl.ds(start, half_seqs, stride=stride), :] = block[first:first + half_seqs, :]

    low_side = device % 2 == 0
    copies[0].wait()
    copies[1].wait()
    mine = mine_buf[...].astype(jnp.float32)
    other = other_ref[...].astype(jnp.float32)
    x = jnp.concatenate(
        [jnp.where(low_side, mine, other), jnp.where(low_side, other, mine)], axis=0)
    gain = gain_buf[...].astype(jnp.float32)
    gain = jnp.concatenate([gain[i:i + 1] for i in range(gain.shape[0])], axis=1)
    scaled = (x * gain).astype(jnp.bfloat16)
    squares = jnp.sum(x * x, axis=-1, keepdims=True)
    high = squares.astype(jnp.bfloat16).astype(jnp.float32)
    low = squares - high
    for color in range(colors):
        spread(color, group + 2, jnp.broadcast_to(high, (total_rows, HD)))
        spread(color, group + 3, jnp.broadcast_to(low, (total_rows, HD)))

    def multiply(weights, place_of_head):
        product = jnp.dot(scaled, weights, preferred_element_type=jnp.float32)
        for i in range(product.shape[1] // HD):
            spread(*place_of_head(i), product[:, i * HD:(i + 1) * HD])

    multiply(wk_ref[...], lambda i: (i, group))
    multiply(wv_ref[...], lambda i: (i, group + 1))
    multiply(early_ref[...], lambda i: (i // group, i % group))

    for c in range(chunks):
        copies[2 + c].wait()
        first = (early + c * chunk) // HD
        multiply(wq_buf[c], lambda i: ((first + i) // group, (first + i) % group))
    for copy in copies[2 + chunks:]:
        copy.wait()
    per_part = part_refs[0].shape[0]
    for slot, pattern in enumerate(slot_patterns(order)):
        ref = part_refs[slot // per_part]
        start = pl.multiple_of((device ^ pattern) * stride, 8)
        ref[slot % per_part] = rows_buf[pl.ds(start, stride), :].astype(ref.dtype)


def part_shapes(total, count, block):
    shape = (total // count,) + block
    return (jax.ShapeDtypeStruct(shape, jnp.float32),) + (jax.ShapeDtypeStruct(shape, jnp.bfloat16),) * (count - 1)


def project(place, mine, other, gain, early, wk, wv, wq, keys, values, steps, group, colors, order, count):
    half_rows, depth = mine.shape
    q_cols, kv_cols = wq.shape[1], wk.shape[1]
    seqs = 2 * half_rows // steps
    chunk = 512
    chunks = (q_cols - early.shape[1]) // chunk
    vmem = pl.BlockSpec(memory_space=pltpu.VMEM)
    smem = pl.BlockSpec(memory_space=pltpu.SMEM)
    hbm = pl.BlockSpec(memory_space=pltpu.HBM)
    cache = jax.ShapeDtypeStruct((2 * keys.shape[0], keys.shape[1] // 2), jnp.bfloat16)
    out_shape = (cache, cache) + part_shapes(
        seqs, count, (colors * steps * (group + 4), HD))
    return pl.pallas_call(
        functools.partial(project_kernel, steps, group, colors, order, chunk),
        out_shape=out_shape,
        in_specs=[smem, hbm, vmem, hbm, vmem, vmem, vmem, hbm, hbm, hbm],
        out_specs=(vmem,) * len(out_shape),
        scratch_shapes=[
            pltpu.VMEM(mine.shape, jnp.bfloat16),
            pltpu.VMEM(gain.shape, jnp.bfloat16),
            pltpu.VMEM((chunks, depth, chunk), jnp.bfloat16),
            pltpu.VMEM((seqs * colors * steps * (group + 4), HD), jnp.float32),
            pltpu.SemaphoreType.DMA((chunks + 6,)),
        ],
        compiler_params=pltpu.CompilerParams(vmem_limit_bytes=28 * MIB),
        cost_estimate=pl.CostEstimate(
            flops=4 * half_rows * depth * (q_cols + 2 * kv_cols),
            bytes_accessed=2 * depth * (q_cols + 2 * kv_cols), transcendentals=0),
        name="project",
    )(place, in_hbm(mine), other, in_hbm(gain), in_vmem(early), in_vmem(wk), in_vmem(wv), in_hbm(wq),
      in_hbm(keys), in_hbm(values))


def fetch_first_kernel(wq_ref, wk_ref, wv_ref, early_ref, wk_out, wv_out, sems):
    copies = [
        pltpu.make_async_copy(wk_ref, wk_out, sems.at[0]),
        pltpu.make_async_copy(wv_ref, wv_out, sems.at[1]),
        pltpu.make_async_copy(wq_ref.at[:, :early_ref.shape[1]], early_ref, sems.at[2])]
    for copy in copies:
        copy.start()
    for copy in copies:
        copy.wait()


def fetch_first(wq, wk, wv, early):
    hbm = pl.BlockSpec(memory_space=pltpu.HBM)
    vmem = pl.BlockSpec(memory_space=pltpu.VMEM)
    depth = wq.shape[0]
    return pl.pallas_call(
        fetch_first_kernel,
        out_shape=(
            pltpu.VMEM((depth, early), wq.dtype), pltpu.VMEM(wk.shape, wk.dtype), pltpu.VMEM(wv.shape, wv.dtype)),
        in_specs=[hbm] * 3,
        out_specs=(vmem,) * 3,
        scratch_shapes=[pltpu.SemaphoreType.DMA((3,))],
        compiler_params=pltpu.CompilerParams(vmem_limit_bytes=16 * MIB),
        cost_estimate=pl.CostEstimate(
            flops=0, bytes_accessed=2 * depth * (early + 2 * wk.shape[1]), transcendentals=0),
        name="fetch_first",
    )(in_hbm(wq), in_hbm(wk), in_hbm(wv))


def notes_kernel(steps, position_ref, length_ref, after_ref, notes_ref):
    lane = lax.broadcasted_iota(jnp.int32, (1, HD), 1)
    frequency = rope_frequencies((lane % (HD // 2)).astype(jnp.float32), HD)
    sign = jnp.where(lane < HD // 2, -1.0, 1.0)
    for t in range(steps):
        angle = (position_ref[0] + t).astype(jnp.float32) * frequency
        notes_ref[2 * t:2 * t + 1, :] = jnp.cos(angle)
        notes_ref[2 * t + 1:2 * t + 2, :] = jnp.sin(angle) * sign
    length = length_ref[0].astype(jnp.float32)
    notes_ref[2 * steps:, :] = jnp.full((notes_ref.shape[0] - 2 * steps, HD), length)


def take_notes(position, length, after, steps):
    smem = pl.BlockSpec(memory_space=pltpu.SMEM)
    return pl.pallas_call(
        functools.partial(notes_kernel, steps),
        out_shape=jax.ShapeDtypeStruct((2 * steps + 4, HD), jnp.float32),
        in_specs=[smem, smem, pl.BlockSpec(memory_space=pl.ANY)],
        out_specs=pl.BlockSpec(memory_space=pltpu.VMEM),
        compiler_params=pltpu.CompilerParams(vmem_limit_bytes=4 * MIB),
        name="notes",
    )(position, length, after)


def combine_kernel(arrived, parts, *refs):
    total = refs[0][...]
    for ref in refs[1:arrived + 1]:
        total = total + ref[...].astype(jnp.float32)
    count = total.shape[0] // parts
    for i, ref in enumerate(refs[-parts:]):
        ref[...] = total[i * count:(i + 1) * count].astype(ref.dtype)


def combine(keep, came, held, after, parts):
    vmem = pl.BlockSpec(memory_space=pltpu.VMEM)
    out_shape = part_shapes(keep.shape[0], parts, keep.shape[1:])
    return pl.pallas_call(
        functools.partial(combine_kernel, len(came), parts),
        out_shape=out_shape,
        in_specs=[vmem] * (1 + len(came)) + [pl.BlockSpec(memory_space=pl.ANY)] * (1 + len(held)),
        out_specs=(vmem,) * parts,
        compiler_params=pltpu.CompilerParams(vmem_limit_bytes=24 * MIB),
        name="combine",
    )(keep, *came, after, *[in_vmem(piece) for piece in held])


def fetch_kernel(first, parts, weight_ref, *rest):
    held_ref, sems = rest[-2:]
    rows = held_ref.shape[0] // parts
    copies = [
        pltpu.make_async_copy(
            weight_ref.at[first + c * rows:first + (c + 1) * rows],
            held_ref.at[c * rows:(c + 1) * rows], sems.at[c])
        for c in range(parts)]
    for copy in copies:
        copy.start()
    for copy in copies:
        copy.wait()


def fetch(weight, first, rows, after):
    parts = 4
    return pl.pallas_call(
        functools.partial(fetch_kernel, first, parts),
        out_shape=pltpu.VMEM((rows, weight.shape[1]), weight.dtype),
        in_specs=[pl.BlockSpec(memory_space=pltpu.HBM)] + [pl.BlockSpec(memory_space=pl.ANY)] * len(after),
        out_specs=pl.BlockSpec(memory_space=pltpu.VMEM),
        scratch_shapes=[pltpu.SemaphoreType.DMA((parts,))],
        compiler_params=pltpu.CompilerParams(vmem_limit_bytes=16 * MIB),
        cost_estimate=pl.CostEstimate(
            flops=0, bytes_accessed=2 * rows * weight.shape[1], transcendentals=0),
        name="fetch",
    )(in_hbm(weight), *after)


def attend_kernel(steps, width, unused, notes_ref, came_notes_ref, own_ref, came_ref, *rest):
    part_refs, (context_ref, fresh_ref, fresh_send_ref, rows_buf) = rest[unused:-4], rest[-4:]
    slots = own_ref.shape[0] // 2
    half_kv = own_ref.shape[1] // HD
    total = functools.reduce(jnp.add, [ref[...].astype(jnp.float32) for ref in part_refs])
    pitch = total.shape[1] // (half_kv * steps)
    group = pitch - 4
    factor = 1.0 / math.sqrt(HD)
    per_head = steps * group
    groups = 2 * half_kv
    lanes = groups * per_head
    fresh_rows = 16
    notes = [notes_ref[...], came_notes_ref[...]]
    fresh_keys = [[None] * groups for _ in range(steps)]
    fresh_values = [[None] * groups for _ in range(steps)]
    queries = []
    for seq in range(2):
        for k in range(half_kv):
            index = seq * half_kv + k
            query = []
            for t in range(steps):
                rows = total[seq, (k * steps + t) * pitch:(k * steps + t + 1) * pitch]
                squares = rows[group + 2:group + 3] + rows[group + 3:group + 4]
                rows = rows * lax.rsqrt(squares / width + epsilon)
                cosine = notes[seq][2 * t:2 * t + 1]
                sine = notes[seq][2 * t + 1:2 * t + 2]
                turned = rows * cosine + pltpu.roll(rows, HD // 2, 1) * sine
                query.append(turned[:group])
                fresh_keys[t][index] = turned[group:group + 1]
                fresh_values[t][index] = rows[group + 1:group + 2]
            blocks = [jnp.zeros((per_head, HD), jnp.float32)] * groups
            blocks[index] = jnp.concatenate(query, axis=0)
            queries.append(jnp.concatenate(blocks, axis=1))
    queries = jnp.concatenate(queries, axis=0).astype(jnp.bfloat16)
    keys_now, values_now = [
        jnp.concatenate([jnp.concatenate(row, axis=1) for row in fresh], axis=0)
        for fresh in (fresh_keys, fresh_values)]
    half = half_kv * HD
    for seq, ref in enumerate((fresh_ref, fresh_send_ref)):
        span = slice(seq * half, (seq + 1) * half)
        ref[...] = jnp.concatenate(
            [keys_now[:, span], values_now[:, span], jnp.zeros((fresh_rows - 2 * steps, half), jnp.float32)],
            axis=0).astype(jnp.bfloat16)
    padding = jnp.zeros((fresh_rows - steps, groups * HD), jnp.float32)
    keys_now, values_now = [
        jnp.concatenate([fresh, padding], axis=0).astype(jnp.bfloat16) for fresh in (keys_now, values_now)]

    keys = jnp.concatenate([own_ref[:slots, :], came_ref[:slots, :]], axis=1)
    values = jnp.concatenate([own_ref[slots:, :], came_ref[slots:2 * slots, :]], axis=1)
    lane = lax.broadcasted_iota(jnp.int32, (1, lanes), 1)
    lengths = [note[2 * steps:2 * steps + 1, :1].astype(jnp.int32) for note in notes]
    length = jnp.where(lane < half_kv * per_head, lengths[0], lengths[1])
    live = lax.broadcasted_iota(jnp.int32, (slots, lanes), 0) < length
    seen = lax.broadcasted_iota(jnp.int32, (fresh_rows, lanes), 0) <= (lane % per_head) // group
    over_last, over_first = (((1,), (1,)), ((), ())), (((0,), (0,)), ((), ()))
    scores = lax.dot_general(keys, queries, over_last, preferred_element_type=jnp.float32) * factor
    scores = jnp.where(live, scores, -jnp.inf)
    fresh = lax.dot_general(keys_now, queries, over_last, preferred_element_type=jnp.float32) * factor
    fresh = jnp.where(seen, fresh, -jnp.inf)
    top = jnp.maximum(jnp.max(scores, axis=0, keepdims=True), jnp.max(fresh, axis=0, keepdims=True))
    scores = jnp.exp(scores - top)
    fresh = jnp.exp(fresh - top)
    inverse = 1.0 / (jnp.sum(scores, axis=0, keepdims=True) + jnp.sum(fresh, axis=0, keepdims=True))
    weights = (scores * inverse).astype(jnp.bfloat16)
    fresh = (fresh * inverse).astype(jnp.bfloat16)
    mixed = lax.dot_general(weights, values, over_first, preferred_element_type=jnp.float32)
    mixed = mixed + lax.dot_general(fresh, values_now, over_first, preferred_element_type=jnp.float32)
    half_heads = half_kv * group
    for index in range(groups):
        seq, k = index // half_kv, index % half_kv
        for t in range(steps):
            first = index * per_head + t * group
            start = (seq * steps + t) * half_heads + k * group
            rows_buf[start:start + group, :] = mixed[first:first + group, index * HD:(index + 1) * HD]
    context_ref[...] = jnp.concatenate([
        rows_buf[pl.ds(head, 2 * steps, stride=half_heads), :] for head in range(half_heads)],
        axis=1).astype(jnp.bfloat16)


def attend(notes, came_notes, own, came, parts, held, steps, width, half_heads):
    vmem = pl.BlockSpec(memory_space=pltpu.VMEM)
    fresh = jax.ShapeDtypeStruct((16, own.shape[1]), jnp.bfloat16)
    return pl.pallas_call(
        functools.partial(attend_kernel, steps, width, len(held)),
        out_shape=(jax.ShapeDtypeStruct((2 * steps, half_heads * HD), jnp.bfloat16), fresh, fresh),
        in_specs=[vmem] * 4 + [pl.BlockSpec(memory_space=pl.ANY)] * len(held) + [vmem] * len(parts),
        out_specs=(vmem,) * 3,
        scratch_shapes=[pltpu.VMEM((2 * steps * half_heads, HD), jnp.float32)],
        compiler_params=pltpu.CompilerParams(vmem_limit_bytes=16 * MIB),
        name="attend",
    )(notes, came_notes, own, came, *[in_vmem(piece) for piece in held], *parts)


def join_kernel(arrived, *refs):
    refs[-1][...] = jnp.concatenate(
        [ref[...].astype(jnp.float32) for ref in refs[:arrived + 1]], axis=0).astype(jnp.bfloat16)


def local_call(kernel, shape, arrays, held=()):
    vmem = pl.BlockSpec(memory_space=pltpu.VMEM)
    return pl.pallas_call(
        kernel,
        out_shape=jax.ShapeDtypeStruct(shape, jnp.bfloat16),
        in_specs=[vmem] * len(arrays) + [pl.BlockSpec(memory_space=pl.ANY)] * len(held),
        out_specs=vmem,
        compiler_params=pltpu.CompilerParams(vmem_limit_bytes=16 * MIB),
        name="local",
    )(*arrays, *[in_vmem(piece) for piece in held])


def output_kernel(steps, patterns, pieces, place_ref, fresh_ref, *rest):
    weight_refs, context_refs = rest[:pieces], rest[pieces:-3]
    mine_ref, other_ref, rows_buf = rest[-3:]
    device = place_ref[0]
    half_seqs = len(patterns) // 2
    rows = jnp.concatenate([ref[...].astype(jnp.float32) for ref in context_refs], axis=0).astype(jnp.bfloat16)
    total = rows.shape[0]
    column = lax.broadcasted_iota(jnp.int32, (1, total), 1)
    slot, step = column // steps, column % steps
    difference = jnp.zeros((1, total), jnp.int32)
    for j, pattern in enumerate(patterns):
        difference = jnp.where(slot == j, pattern, difference)
    seq = difference ^ device
    target = (seq // half_seqs * steps + step) * half_seqs + seq % half_seqs
    move = (lax.broadcasted_iota(jnp.int32, (total, total), 0) == target).astype(jnp.float32).astype(jnp.bfloat16)
    rows_buf[...] = jnp.dot(move, rows, preferred_element_type=jnp.float32).astype(jnp.bfloat16)
    low_side = device % 2 == 0
    half = rows_buf.shape[0] // 2
    other_ref[half:, :fresh_ref.shape[1]] = fresh_ref[...]
    if other_ref.shape[1] > fresh_ref.shape[1]:
        other_ref[half:, fresh_ref.shape[1]:] = jnp.zeros(
            (fresh_ref.shape[0], other_ref.shape[1] - fresh_ref.shape[1]), jnp.bfloat16)
    columns = mine_ref.shape[1]
    chunk = min(columns, 512)
    for c in range(columns // chunk):
        span = slice(c * chunk, (c + 1) * chunk)
        product, first = None, 0
        for weight_ref in weight_refs:
            last = first + weight_ref.shape[0]
            part = jnp.dot(rows_buf[:, first:last], weight_ref[:, span], preferred_element_type=jnp.float32)
            product = part if product is None else product + part
            first = last
        lower, upper = product[:half], product[half:]
        mine_ref[:, span] = jnp.where(low_side, lower, upper)
        other_ref[:half, span] = jnp.where(low_side, upper, lower).astype(jnp.bfloat16)


def output(place, fresh, contexts, patterns, held, steps):
    columns = held[0].shape[1]
    depth = sum(piece.shape[0] for piece in held)
    devices = len(patterns)
    half = devices * steps // 2
    vmem = pl.BlockSpec(memory_space=pltpu.VMEM)
    smem = pl.BlockSpec(memory_space=pltpu.SMEM)
    return pl.pallas_call(
        functools.partial(output_kernel, steps, patterns, len(held)),
        out_shape=(
            jax.ShapeDtypeStruct((half, columns), jnp.float32),
            jax.ShapeDtypeStruct((half + fresh.shape[0], columns), jnp.bfloat16),
        ),
        in_specs=[smem, vmem] + [vmem] * (len(held) + len(contexts)),
        out_specs=(vmem, vmem),
        scratch_shapes=[
            pltpu.VMEM((devices * steps, depth), jnp.bfloat16),
        ],
        compiler_params=pltpu.CompilerParams(vmem_limit_bytes=26 * MIB),
        cost_estimate=pl.CostEstimate(
            flops=2 * devices * steps * depth * columns,
            bytes_accessed=2 * depth * columns, transcendentals=0),
        name="output",
    )(place, fresh, *[in_vmem(piece) for piece in held], *contexts)


def finish_kernel(steps, place_ref, mine_ref, came_ref, fresh_ref, result_ref, new_keys_ref, new_values_ref):
    half = mine_ref.shape[0]
    result_ref[...] = (mine_ref[...] + came_ref[:half, :].astype(jnp.float32)).astype(jnp.bfloat16)
    own = fresh_ref[...].astype(jnp.float32)
    came = came_ref[half:, :own.shape[1]].astype(jnp.float32)
    low_side = place_ref[0] % 2 == 0
    rows = jnp.concatenate(
        [jnp.where(low_side, own, came), jnp.where(low_side, came, own)], axis=1).astype(jnp.bfloat16)
    new_keys_ref[...] = rows[:steps]
    new_values_ref[...] = rows[steps:2 * steps]


def finish(place, mine, came, fresh, steps):
    vmem = pl.BlockSpec(memory_space=pltpu.VMEM)
    new = jax.ShapeDtypeStruct((steps, 2 * fresh.shape[1]), jnp.bfloat16)
    return pl.pallas_call(
        functools.partial(finish_kernel, steps),
        out_shape=(jax.ShapeDtypeStruct(mine.shape, jnp.bfloat16), new, new),
        in_specs=[pl.BlockSpec(memory_space=pltpu.SMEM)] + [vmem] * 3,
        out_specs=(vmem,) * 3,
        compiler_params=pltpu.CompilerParams(vmem_limit_bytes=8 * MIB),
        name="finish",
    )(place, mine, came, fresh)


def body(hidden_in, norm_gain, query_weight, key_weight, value_weight, out_weight,
         cache_keys, cache_values, lengths, positions):
    steps, half_seqs, depth = hidden_in.shape
    everyone = ("gx", "gy")
    devices = lax.axis_size(everyone)
    bits = devices.bit_length() - 1
    colors = key_weight.shape[1] // HD
    half_heads = query_weight.shape[1] // HD
    group = half_heads // colors
    place = lax.axis_index(everyone).astype(jnp.int32).reshape(1)

    def partner(array, pattern):
        return lax.ppermute(array, everyone, [(i, i ^ pattern) for i in range(devices)])

    stages = [list(range(first, min(first + 2, bits))) for first in range(1, bits, 2)]
    order = [bit for stage in stages for bit in stage] + [0]
    total = out_weight.shape[0]
    cuts = [total * i // 8 for i in (0, 2, 3, 5, 8)]
    held = []

    def fetch_next(window, after):
        i = len(held)
        if window not in (0, 1, 2, 3):
            return []
        held.append(fetch(out_weight, cuts[i], cuts[i + 1] - cuts[i], after))
        return held[-1:]

    mine = hidden_in.reshape(steps * half_seqs, depth)
    other = partner(mine, 1)
    early, wk, wv = fetch_first(query_weight, key_weight, value_weight, 512)
    own, cache, *parts = project(
        place, mine, other, norm_gain.reshape(-1, HD), early, wk, wv, query_weight,
        cache_keys[0], cache_values[0],
        steps, group, colors, order, 1 << len(stages[0]))
    cache = partner(cache, 1)
    notes = take_notes(positions, lengths, parts[1], steps)
    came_notes = partner(notes, 1)
    for i, stage in enumerate(stages):
        came = [partner(part, pattern) for part, pattern in zip(parts[1:], slot_patterns(stage)[1:])]
        now = fetch_next(i, [parts[1], notes])
        if i < len(stages) - 1:
            parts = combine(parts[0], came, now, notes, 1 << len(stages[i + 1]))
    context, fresh, fresh_send = attend(
        notes, came_notes, own, cache, [parts[0], *came], now, steps, depth * lax.axis_size("gx"), half_heads)

    patterns = [0, 1]
    for i, stage in enumerate(stages[::-1]):
        moves = slot_patterns(stage)
        came = [partner(context, move) for move in moves[1:]]
        patterns = [p ^ move for move in moves for p in patterns]
        now = fetch_next(len(stages) + i, [context])
        if i < len(stages) - 1:
            shape = (len(moves) * context.shape[0],) + context.shape[1:]
            context = local_call(functools.partial(join_kernel, len(came)), shape, [context, *came], now)
    mine, other = output(place, fresh_send, [context, *came], patterns, held, steps)
    result, new_keys, new_values = finish(place, mine, partner(other, 1), fresh, steps)
    return (
        result.reshape(steps, half_seqs, -1),
        new_keys[:, None, :],
        new_values[:, None, :],
    )


def solution(mesh):
    in_specs = (
        P(None, ("rep", "gy"), "gx"),
        P("gx"),
        P("gx", "gy"),
        P("gx", "gy"),
        P("gx", "gy"),
        P("gy", "gx"),
        P(("rep", "gx", "gy"), None, None),
        P(("rep", "gx", "gy"), None, None),
        P(("rep", "gx", "gy")),
        P(("rep", "gx", "gy")),
    )
    out_specs = (
        P(None, ("rep", "gy"), "gx"),
        P(None, ("rep", "gx", "gy"), None),
        P(None, ("rep", "gx", "gy"), None),
    )
    return jax.shard_map(body, mesh=mesh, in_specs=in_specs, out_specs=out_specs, check_vma=False)
```
